32 devices in a mesh: clip: 4 (over y, x), frame: 8 (over z, core).
Axes of the slice: x: 2, y: 2, z: 4, core: 2. Of those that a mesh axis runs over, the one named last changes fastest.
Arguments:
- latents: bfloat16 [4, 8, 512, 1152], P('clip', 'frame'), may hold values from -6 to 6
- cotangent: bfloat16 [4, 8, 512, 1152], P('clip', 'frame'), may hold values from -6 to 6
- text_tokens: bfloat16 [4, 4, 120, 4096], P('clip'), may hold values from -6 to 6
- text_lengths: int32 [4, 4], P('clip'), may hold values from 77 to 120, as said below
- clip_frames: int32 [4, 4], P('clip'), may hold values from 0 to 6, as said below
- timesteps: int32 [4, 4], P('clip'), may hold values from 0 to 999
- motion_free: int32 [4, 4], P('clip'), may hold values from 0 to 1
- modulation_weight: bfloat16 [1152, 6912], P('frame'), may hold values from -0.1875 to 0.1875
- modulation_bias: bfloat16 [6912], P('frame'), may hold values from -3 to 3
- spatial_input: bfloat16 [1152, 3456], P('frame'), may hold values from -0.1875 to 0.1875
- spatial_output: bfloat16 [1152, 1152], P('frame'), may hold values from -1 to 1
- spatial_bias: bfloat16 [1152], P('frame'), may hold values from -3 to 3
- text_projection: bfloat16 [4096, 1152], P('frame'), may hold values from -0.09375 to 0.09375
- cross_query: bfloat16 [1152, 1152], P('frame'), may hold values from -0.1875 to 0.1875
- cross_memory: bfloat16 [1152, 2304], P('frame'), may hold values from -0.1875 to 0.1875
- cross_output: bfloat16 [1152, 1152], P('frame'), may hold values from -0.75 to 0.75
- cross_bias: bfloat16 [1152], P('frame'), may hold values from -3 to 3
- expand_weight: bfloat16 [1152, 4608], P('frame'), may hold values from -0.1875 to 0.1875
- expand_bias: bfloat16 [4608], P('frame'), may hold values from -3 to 3
- reduce_weight: bfloat16 [4608, 1152], P('frame'), may hold values from -0.09375 to 0.09375
- reduce_bias: bfloat16 [1152], P('frame'), may hold values from -3 to 3
- temporal_gain: bfloat16 [1152], P('frame'), may hold values from 0.5 to 1.5
- temporal_shift: bfloat16 [1152], P('frame'), may hold values from -3 to 3
- temporal_input: bfloat16 [1152, 3456], P('frame'), may hold values from -0.1875 to 0.1875
- temporal_output: bfloat16 [1152, 1152], P('frame'), may hold values from -0.375 to 0.375
- temporal_bias: bfloat16 [1152], P('frame'), may hold values from -3 to 3
- temporal_gate: bfloat16 [1152], P('frame'), may hold values from -6 to 6
Outputs:
- block_output: bfloat16 [4, 8, 512, 1152], P('clip', 'frame')
- input_gradient: bfloat16 [4, 8, 512, 1152], P('clip', 'frame')
- gradient_modulation_weight: float32 [1152, 6912], P('frame')
- gradient_modulation_bias: float32 [6912], P('frame')
- gradient_spatial_input: float32 [1152, 3456], P('frame')
- gradient_spatial_output: float32 [1152, 1152], P('frame')
- gradient_spatial_bias: float32 [1152], P('frame')
- gradient_text_projection: float32 [4096, 1152], P('frame')
- gradient_cross_query: float32 [1152, 1152], P('frame')
- gradient_cross_memory: float32 [1152, 2304], P('frame')
- gradient_cross_output: float32 [1152, 1152], P('frame')
- gradient_cross_bias: float32 [1152], P('frame')
- gradient_expand_weight: float32 [1152, 4608], P('frame')
- gradient_expand_bias: float32 [4608], P('frame')
- gradient_reduce_weight: float32 [4608, 1152], P('frame')
- gradient_reduce_bias: float32 [1152], P('frame')
- gradient_temporal_gain: float32 [1152], P('frame')
- gradient_temporal_shift: float32 [1152], P('frame')
- gradient_temporal_input: float32 [1152, 3456], P('frame')
- gradient_temporal_output: float32 [1152, 1152], P('frame')
- gradient_temporal_bias: float32 [1152], P('frame')
- gradient_temporal_gate: float32 [1152], P('frame')
The draws below stay inside these ranges and needn't reach their ends.
Inputs may be any that keep to these rules, and one draw needn't show every extreme that they name: `clip_frames`: each entry is a multiple of 2 frames; the entries of a group sum to 8, and every group holds a clip of 6 frames. `text_lengths`: A clip reads the first that many of its 120 text rows.
All inputs are finite; a program needn't handle non-finite values.
Results may differ from the reference program's by a relative error of at most 0.02875.
Values may be sent and summed in bfloat16 or wider, within the bound.
A program may use at most 384 MiB of HBM per device.

```python
import math
import jax
import jax.numpy as jnp
from jax import lax

D = 1152
HEADS = 16
FF = 4608
TXT_D = 4096
TXT = 120
TXT_MIN = 77
PATCHES = 512
FRAMES = 8
SLOTS = 4
GROUPS = 4
CLIP_MOST = 6


def draw_clip_frames(key, part):
    key = jax.random.fold_in(key, 11)
    unit_count = FRAMES // 2
    first_take = CLIP_MOST // 2
    random_picks = jax.random.randint(jax.random.fold_in(key, 1), (GROUPS, SLOTS), 2, 9)
    remaining = jnp.full((GROUPS,), unit_count - first_take, jnp.int32)
    columns = [jnp.full((GROUPS,), first_take, jnp.int32)]
    for slot_index in range(1, SLOTS):
        taken = jnp.minimum(jnp.minimum(random_picks[:, slot_index], remaining), first_take)
        remaining = remaining - taken
        columns.append(taken)
    frame_counts = jnp.stack(columns, axis=1) * 2
    roll_shifts = jax.random.randint(jax.random.fold_in(key, 2), (GROUPS,), 0, SLOTS)
    return jax.vmap(jnp.roll)(frame_counts, roll_shifts).astype(jnp.int32)


def draw_text_lengths(key, part):
    key = jax.random.fold_in(key, 12)
    lengths = jax.random.randint(jax.random.fold_in(key, 1), (GROUPS, SLOTS), TXT_MIN, TXT + 1)
    longest = jax.random.randint(jax.random.fold_in(key, 2), (GROUPS, 1), 0, SLOTS)
    offset = jax.random.randint(jax.random.fold_in(key, 3), (GROUPS, 1), 1, SLOTS)
    shortest = (longest + offset) % SLOTS
    slot_ids = jnp.arange(SLOTS, dtype=jnp.int32)[None, :]
    lengths = jnp.where(slot_ids == longest, TXT, lengths)
    return jnp.where(slot_ids == shortest, TXT_MIN, lengths).astype(jnp.int32)


def draw_motion_free(key, part):
    key = jax.random.fold_in(key, 13)
    flags = (jax.random.randint(jax.random.fold_in(key, 1), (GROUPS, SLOTS), 0, 3) == 0).astype(jnp.int32)
    forced_on = jax.random.randint(jax.random.fold_in(key, 2), (GROUPS, 1), 0, SLOTS)
    offset = jax.random.randint(jax.random.fold_in(key, 3), (GROUPS, 1), 1, SLOTS)
    forced_off = (forced_on + offset) % SLOTS
    slot_ids = jnp.arange(SLOTS, dtype=jnp.int32)[None, :]
    flags = jnp.where(slot_ids == forced_on, 1, flags)
    return jnp.where(slot_ids == forced_off, 0, flags).astype(jnp.int32)


def place_ends(drawn, rng, smallest, largest):
    longest = drawn.shape.index(max(drawn.shape))
    spots = []
    for shift in (0, 1):
        where = [jax.random.randint(jax.random.fold_in(rng, axis), (), 0, length) for axis, length in enumerate(drawn.shape)]
        where[longest] = (where[longest] + shift) % drawn.shape[longest]
        spots.append(tuple(where))
    return drawn.at[spots[0]].set(smallest).at[spots[1]].set(largest)


def steps_of(stream_key, shape, cuts, smallest, largest):
    def one(dim, parts):
        draws = jax.random.uniform(jax.random.fold_in(jax.random.fold_in(stream_key, 6), dim), (parts,), jnp.float32, smallest / len(cuts), largest / len(cuts))
        return jnp.repeat(jnp.exp(draws), shape[dim] // parts).reshape((-1,) + (1,) * (len(shape) - dim - 1))

    factor_of = one(*cuts[0])
    for cut in cuts[1:]:
        factor_of = factor_of * one(*cut)
    return factor_of


def scatter_about(stream_key, dims, scale, reach, shards=(), kind=jnp.bfloat16):
    factor_of = steps_of(stream_key, dims, shards, -0.22, 0.18) if shards else 1.0
    entries = jax.random.normal(stream_key, dims, jnp.float32) * scale * factor_of
    return jnp.minimum(jnp.maximum(entries, -reach), reach).astype(kind)


def setup_inputs(seed: int = 0) -> dict:
    key_of = jax.random.split(jax.random.key(seed), 28)
    latents = scatter_about(key_of[0], (GROUPS, FRAMES, PATCHES, D), 1.0, 6.0, ((0, 4), (1, 8)))
    cotangent = scatter_about(key_of[1], (GROUPS, FRAMES, PATCHES, D), 1.0, 6.0, ((0, 4), (1, 8)))
    text_tokens = scatter_about(key_of[2], (GROUPS, SLOTS, TXT, TXT_D), 1.0, 6.0, ((0, 4),))
    text_lengths = draw_text_lengths(jax.random.fold_in(key_of[27], 71), 0)
    clip_frames = draw_clip_frames(jax.random.fold_in(key_of[27], 71), 0)
    timesteps = place_ends(jax.random.randint(key_of[5], (GROUPS, SLOTS), 0, 1000), jax.random.fold_in(key_of[5], 1), 0, 999).astype(jnp.int32)
    motion_free = draw_motion_free(jax.random.fold_in(key_of[27], 71), 0)
    modulation_weight = scatter_about(key_of[7], (D, 6 * D), D ** -0.5, 0.1875, ((0, 8),))
    modulation_bias = scatter_about(key_of[8], (6 * D,), 0.5, 3.0, ((0, 8),))
    spatial_input = scatter_about(key_of[9], (D, 3 * D), D ** -0.5, 0.1875, ((0, 8),))
    spatial_output = scatter_about(key_of[10], (D, D), (D // 32) ** -0.5, 1.0, ((0, 8),))
    spatial_bias = scatter_about(key_of[11], (D,), 0.5, 3.0, ((0, 8),))
    text_projection = scatter_about(key_of[12], (TXT_D, D), TXT_D ** -0.5, 0.09375, ((0, 8),))
    cross_query = scatter_about(key_of[13], (D, D), D ** -0.5, 0.1875, ((0, 8),))
    cross_memory = scatter_about(key_of[14], (D, 2 * D), D ** -0.5, 0.1875, ((0, 8),))
    cross_output = scatter_about(key_of[15], (D, D), (D // 16) ** -0.5, 0.75, ((0, 8),))
    cross_bias = scatter_about(key_of[16], (D,), 0.5, 3.0, ((0, 8),))
    expand_weight = scatter_about(key_of[17], (D, FF), D ** -0.5, 0.1875, ((0, 8),))
    expand_bias = scatter_about(key_of[18], (FF,), 0.5, 3.0, ((0, 8),))
    reduce_weight = scatter_about(key_of[19], (FF, D), FF ** -0.5, 0.09375, ((0, 8),))
    reduce_bias = scatter_about(key_of[20], (D,), 0.5, 3.0, ((0, 8),))
    temporal_gain = jnp.clip(1.0 + 0.1 * jax.random.normal(key_of[21], (D,), jnp.float32), 0.5, 1.5).astype(jnp.bfloat16)
    temporal_shift = scatter_about(key_of[22], (D,), 0.5, 3.0, ((0, 8),))
    temporal_input = scatter_about(key_of[23], (D, 3 * D), D ** -0.5, 0.1875, ((0, 8),))
    temporal_output = scatter_about(key_of[24], (D, D), (D // 4) ** -0.5, 0.375, ((0, 8),))
    temporal_bias = scatter_about(key_of[25], (D,), 0.5, 3.0, ((0, 8),))
    temporal_gate = scatter_about(key_of[26], (D,), 1.0, 6.0, ((0, 8),))
    return {"latents": latents, "cotangent": cotangent, "text_tokens": text_tokens, "text_lengths": text_lengths, "clip_frames": clip_frames, "timesteps": timesteps, "motion_free": motion_free, "modulation_weight": modulation_weight, "modulation_bias": modulation_bias, "spatial_input": spatial_input, "spatial_output": spatial_output, "spatial_bias": spatial_bias, "text_projection": text_projection, "cross_query": cross_query, "cross_memory": cross_memory, "cross_output": cross_output, "cross_bias": cross_bias, "expand_weight": expand_weight, "expand_bias": expand_bias, "reduce_weight": reduce_weight, "reduce_bias": reduce_bias, "temporal_gain": temporal_gain, "temporal_shift": temporal_shift, "temporal_input": temporal_input, "temporal_output": temporal_output, "temporal_bias": temporal_bias, "temporal_gate": temporal_gate}


@jax.custom_vjp
def low(v):
    return lax.optimization_barrier(v.astype(jnp.bfloat16)).astype(jnp.float32)

@jax.custom_vjp
def low_back(v):
    return v

def low_keep(v):
    return (low(v), None)

def low_pass(kept, grad):
    return (grad,)

def back_keep(v):
    return (v, None)

def back_low(kept, grad):
    return (low(grad),)
low.defvjp(low_keep, low_pass)
low_back.defvjp(back_keep, back_low)
eps_norm = 1e-06
big_negative = -1e+30

def assign_clips(frame_counts, frame_count):
    slot_count = frame_counts.shape[0]
    slot_ids = jnp.arange(slot_count, dtype=jnp.int32)
    longest = jnp.max(frame_counts).astype(jnp.int32)
    long_slot = jnp.min(jnp.where(frame_counts == longest, slot_ids, slot_count)).astype(jnp.int32)
    frame_ids = jnp.arange(frame_count, dtype=jnp.int32)
    long_gaps = jnp.maximum(longest - 1, 1).astype(jnp.int32)
    frame_gaps = frame_count - 1
    step_index = ((frame_ids * long_gaps + frame_gaps - 1) // frame_gaps).astype(jnp.int32)
    on_long = step_index * frame_gaps // long_gaps == frame_ids
    long_marks = on_long.astype(jnp.int32)
    before_count = (jnp.cumsum(long_marks) - long_marks).astype(jnp.int32)
    order_rank = frame_ids - before_count
    rest_counts = jnp.where(slot_ids == long_slot, 0, frame_counts).astype(jnp.int32)
    rest_ends = jnp.cumsum(rest_counts).astype(jnp.int32)
    rest_ids = lax.optimization_barrier(jnp.sum((rest_ends[None, :] <= order_rank[:, None]).astype(jnp.int32), axis=1)).astype(jnp.int32)
    return jnp.where(on_long, long_slot, rest_ids).astype(jnp.int32)

def matmul(left, right):
    return jnp.dot(left, right, precision=lax.Precision.HIGHEST, preferred_element_type=jnp.float32)

def normalize(values):
    average = lax.optimization_barrier(jnp.mean(values, axis=-1, keepdims=True))
    centred = values - average
    spread = lax.optimization_barrier(jnp.mean(centred * centred, axis=-1, keepdims=True))
    return centred * lax.rsqrt(spread + eps_norm)

def modulate(values, offset, scaling):
    return normalize(values) * (1.0 + scaling) + offset

def smooth_gelu(values):
    return jax.nn.gelu(values, approximate=True)

def embed_time(time_steps, model_width):
    half_width = model_width // 2
    frequency = jnp.exp(-math.log(10000.0) * jnp.arange(half_width, dtype=jnp.float32) / half_width)
    angles = time_steps.astype(jnp.float32)[:, None] * frequency[None, :]
    return jax.nn.silu(jnp.concatenate([jnp.cos(angles), jnp.sin(angles)], axis=1))

def attention(queries, key_rows, values, valid_mask, att_scale):
    scores = low_back(jnp.einsum('qbhd,kbhd->bhqk', queries, key_rows, precision=lax.Precision.HIGHEST) * att_scale)
    if valid_mask is not None:
        scores = jnp.where(valid_mask, scores, big_negative)
    weights = low(jax.nn.softmax(scores, axis=-1))
    return jnp.einsum('bhqk,kbhd->qbhd', weights, values, precision=lax.Precision.HIGHEST)

def frame_block(params, tokens, modulation_row, context, text_length):
    spatial_input, spatial_output, spatial_bias, cross_query, cross_memory, cross_output, cross_bias, expand_weight, expand_bias, reduce_weight, reduce_bias = params
    patch_count, model_width = tokens.shape
    text_count = context.shape[0]
    head_size = model_width // HEADS
    att_scale = 1.0 / math.sqrt(head_size)
    shift_attend, scale_attend, gate_attend, shift_feed, scale_feed, gate_feed = jnp.split(modulation_row, 6)
    normed_attend = low(modulate(tokens, shift_attend, scale_attend))
    spatial_heads = low(low_back(matmul(normed_attend, spatial_input))).reshape(patch_count, 1, 3, HEADS, head_size)
    spatial_att = low(low_back(attention(spatial_heads[:, :, 0], spatial_heads[:, :, 1], spatial_heads[:, :, 2], None, att_scale)))
    branch_attend = low_back(matmul(spatial_att.reshape(patch_count, model_width), spatial_output) + spatial_bias)
    after_attend = tokens + gate_attend * branch_attend
    cross_heads = low(low_back(matmul(low(after_attend), cross_query))).reshape(patch_count, 1, HEADS, head_size)
    memory_heads = low(low_back(matmul(context, cross_memory))).reshape(text_count, 1, 2, HEADS, head_size)
    text_mask = (jnp.arange(text_count, dtype=jnp.int32) < text_length)[None, None, None, :]
    cross_att = low(low_back(attention(cross_heads, memory_heads[:, :, 0], memory_heads[:, :, 1], text_mask, att_scale)))
    branch_cross = low_back(matmul(cross_att.reshape(patch_count, model_width), cross_output) + cross_bias)
    after_cross = after_attend + branch_cross
    normed_feed = low(modulate(after_cross, shift_feed, scale_feed))
    hidden = low(smooth_gelu(low_back(matmul(normed_feed, expand_weight) + expand_bias)))
    branch_feed = low_back(matmul(hidden, reduce_weight) + reduce_bias)
    return after_cross + gate_feed * branch_feed

def group_block(params, tokens, text_block, text_lengths, clip_frames, time_steps, motion_flags):
    modulation_weight, modulation_bias, spatial_input, spatial_output, spatial_bias, text_projection, cross_query, cross_memory, cross_output, cross_bias, expand_weight, expand_bias, reduce_weight, reduce_bias, temporal_gain, temporal_shift, temporal_input, temporal_output, temporal_bias, temporal_gate = params
    frame_count, patch_count, model_width = tokens.shape
    head_size = model_width // HEADS
    att_scale = 1.0 / math.sqrt(head_size)
    clip_ids = assign_clips(clip_frames, frame_count)
    conditioning = low(embed_time(time_steps, model_width))
    modulation = matmul(conditioning, modulation_weight) + modulation_bias
    context = low(low_back(jnp.einsum('stk,kd->std', text_block, text_projection, precision=lax.Precision.HIGHEST)))
    frame_params = (spatial_input, spatial_output, spatial_bias, cross_query, cross_memory, cross_output, cross_bias, expand_weight, expand_bias, reduce_weight, reduce_bias)
    checked = jax.checkpoint(frame_block)
    after_feed = lax.map(lambda item: checked(frame_params, item[0], item[1], item[2], item[3]), (tokens, modulation[clip_ids], context[clip_ids], text_lengths[clip_ids]))
    sent = low_back(low(after_feed))
    normed_time = low(normalize(sent) * temporal_gain + temporal_shift)
    time_heads = low(low_back(matmul(normed_time.reshape(-1, model_width), temporal_input)))
    time_heads = time_heads.reshape(frame_count, patch_count, 3, HEADS, head_size)
    time_mask = (clip_ids[:, None] == clip_ids[None, :])[None, None]
    time_att = low(low_back(attention(time_heads[:, :, 0], time_heads[:, :, 1], time_heads[:, :, 2], time_mask, att_scale)))
    result = low(low_back(matmul(time_att.reshape(-1, model_width), temporal_output) + temporal_bias))
    result = result.reshape(frame_count, patch_count, model_width)
    keep_frames = 1.0 - motion_flags[clip_ids].astype(jnp.float32)
    return after_feed + temporal_gate[None, None, :] * keep_frames[:, None, None] * result

def reference(latents, cotangent, text_tokens, text_lengths, clip_frames, timesteps, motion_free, modulation_weight, modulation_bias, spatial_input, spatial_output, spatial_bias, text_projection, cross_query, cross_memory, cross_output, cross_bias, expand_weight, expand_bias, reduce_weight, reduce_bias, temporal_gain, temporal_shift, temporal_input, temporal_output, temporal_bias, temporal_gate):
    params = tuple((weight.astype(jnp.float32) for weight in (modulation_weight, modulation_bias, spatial_input, spatial_output, spatial_bias, text_projection, cross_query, cross_memory, cross_output, cross_bias, expand_weight, expand_bias, reduce_weight, reduce_bias, temporal_gain, temporal_shift, temporal_input, temporal_output, temporal_bias, temporal_gate)))

    def per_group(carry, group):
        tokens, upstream, text_block, lengths, frames, time_steps, motion_flags = group

        def forward(tokens_in, weights_in):
            return group_block(weights_in, tokens_in, text_block, lengths, frames, time_steps, motion_flags)
        output, back_fn = jax.vjp(forward, tokens, params)
        back_tokens, back_params = back_fn(upstream)
        carry = tuple((summed + addend for summed, addend in zip(carry, back_params)))
        return (carry, (output.astype(jnp.bfloat16), back_tokens.astype(jnp.bfloat16)))
    initial = tuple((jnp.zeros_like(weight) for weight in params))
    totals, (outputs, gradients) = lax.scan(per_group, initial, (latents.astype(jnp.float32), cotangent.astype(jnp.float32), text_tokens.astype(jnp.float32), text_lengths, clip_frames, timesteps, motion_free))
    back_modw, back_modb, back_sin, back_sout, back_sbias, back_text, back_cq, back_cmem, back_cout, back_cbias, back_expw, back_expb, back_redw, back_redb, back_tgain, back_tshift, back_tin, back_tout, back_tbias, back_tgate = totals
    return (outputs, gradients, back_modw, back_modb, back_sin, back_sout, back_sbias, back_text, back_cq, back_cmem, back_cout, back_cbias, back_expw, back_expb, back_redw, back_redb, back_tgain, back_tshift, back_tin, back_tout, back_tbias, back_tgate)
```

```python
import functools
import math

import jax
import jax.numpy as jnp
from jax import lax
from jax.experimental import pallas as pl
from jax.experimental.pallas import tpu as pltpu
from jax.sharding import PartitionSpec as P

HEADS = 16


eps_norm = 1e-06
big_negative = -1e30


def assign_clips(frame_counts, frame_count):
    slot_count = frame_counts.shape[0]
    slot_ids = jnp.arange(slot_count, dtype=jnp.int32)
    longest = jnp.max(frame_counts)
    long_slot = jnp.min(jnp.where(frame_counts == longest, slot_ids, slot_count))
    frame_ids = jnp.arange(frame_count, dtype=jnp.int32)
    long_gaps = jnp.maximum(longest - 1, 1)
    frame_gaps = frame_count - 1
    step_index = (frame_ids * long_gaps + frame_gaps - 1) // frame_gaps
    on_long = step_index * frame_gaps // long_gaps == frame_ids
    long_marks = on_long.astype(jnp.int32)
    before_count = jnp.cumsum(long_marks) - long_marks
    order_rank = frame_ids - before_count
    rest_counts = jnp.where(slot_ids == long_slot, 0, frame_counts)
    rest_ends = jnp.cumsum(rest_counts)
    rest_ids = jnp.sum((rest_ends[None, :] <= order_rank[:, None]).astype(jnp.int32), axis=1)
    return jnp.where(on_long, long_slot, rest_ids)


def normalize(values):
    average = jnp.mean(values, axis=-1, keepdims=True)
    centred = values - average
    spread = jnp.mean(centred * centred, axis=-1, keepdims=True)
    return centred * lax.rsqrt(spread + eps_norm)


def modulate(values, offset, scaling):
    return normalize(values) * (1.0 + scaling) + offset


def affine_norm(values, norm_gain, offset):
    return normalize(values) * norm_gain + offset


def smooth_gelu(values):
    return jax.nn.gelu(values, approximate=True)


def embed_time(time_steps, model_width):
    half_width = model_width // 2
    frequency = jnp.exp(-math.log(10000.0) * jnp.arange(half_width, dtype=jnp.float32) / half_width)
    angles = time_steps.astype(jnp.float32)[:, None] * frequency[None, :]
    return jax.nn.silu(jnp.concatenate([jnp.cos(angles), jnp.sin(angles)], axis=1))


def attend(queries, key_rows, values, valid_mask, att_scale):
    scores = (
        jnp.einsum("qbhd,kbhd->bhqk", queries, key_rows, preferred_element_type=jnp.float32)
        * att_scale
    )
    if valid_mask is not None:
        scores = jnp.where(valid_mask, scores, big_negative)
    largest = jnp.max(scores, axis=-1, keepdims=True)
    summed = jnp.sum(jnp.exp(scores - largest), axis=-1, keepdims=True)
    logsum = largest + jnp.log(summed)
    weights = jnp.exp(scores - logsum).astype(jnp.bfloat16)
    output = jnp.einsum("bhqk,kbhd->qbhd", weights, values, preferred_element_type=jnp.float32)
    return (output, logsum)


def attend_back(queries, key_rows, values, valid_mask, att_scale, logsum, upstream):
    scores = (
        jnp.einsum("qbhd,kbhd->bhqk", queries, key_rows, preferred_element_type=jnp.float32)
        * att_scale
    )
    if valid_mask is not None:
        scores = jnp.where(valid_mask, scores, big_negative)
    weights = jnp.exp(scores - logsum)
    back_weights = jnp.einsum(
        "qbhd,kbhd->bhqk", upstream, values, preferred_element_type=jnp.float32
    )
    back_values = jnp.einsum(
        "bhqk,qbhd->kbhd",
        weights.astype(jnp.bfloat16),
        upstream,
        preferred_element_type=jnp.float32,
    )
    inner_sum = jnp.sum(back_weights * weights, axis=-1, keepdims=True)
    back_scores = (weights * (back_weights - inner_sum)).astype(jnp.bfloat16)
    back_queries = (
        jnp.einsum("bhqk,kbhd->qbhd", back_scores, key_rows, preferred_element_type=jnp.float32)
        * att_scale
    )
    back_keys = (
        jnp.einsum("bhqk,qbhd->kbhd", back_scores, queries, preferred_element_type=jnp.float32)
        * att_scale
    )
    return (back_queries, back_keys, back_values)


MESH_ID = pl.DeviceIdType.MESH
LANES = 128
PIECE_SLOTS = 4


def neighbours():
    column = lax.axis_index("clip")
    frame = lax.axis_index("frame")
    depth = frame // 2
    core = frame % 2
    across_x = column + 1 - 2 * (column % 2)
    across_y = column + 2 - 4 * (column // 2)
    sibling = frame + 1 - 2 * core
    return column, frame, depth, core, across_x, across_y, sibling


def greet(peers):
    barrier = pltpu.get_barrier_semaphore()
    for peer in peers:
        pl.semaphore_signal(barrier, inc=1, device_id=peer, device_id_type=MESH_ID)
    pl.semaphore_wait(barrier, len(peers))


class Copies:
    def __init__(self, send_sems, recv_sems):
        self.send_sems, self.recv_sems, self.count, self.started = send_sems, recv_sems, 0, []

    def start(self, source, target, device):
        copy = pltpu.make_async_remote_copy(
            src_ref=source,
            dst_ref=target,
            send_sem=self.send_sems.at[self.count],
            recv_sem=self.recv_sems.at[self.count],
            device_id=device,
            device_id_type=MESH_ID,
        )
        self.count += 1
        copy.start()
        self.started.append(copy)
        return copy

    def finish(self):
        for copy in self.started:
            copy.wait_send()


def rows_at(ref, start, size, step):
    return ref.at[pl.ds(pl.multiple_of(start, step), size), :]


def whole_unit(ref, tall, unit, frame):
    if tall:
        height = ref.shape[0] // 32
        return rows_at(ref, frame * (4 * height) + unit * height, height, height)
    height, width = ref.shape[0] // 8, ref.shape[1] // 4
    return ref.at[
        pl.ds(pl.multiple_of(frame * height, height), height),
        pl.ds(pl.multiple_of(unit * width, LANES), width),
    ]


def whole_share(ref, tall, frame):
    height = ref.shape[0] // 8
    return rows_at(ref, frame * height, height, height)


def share_unit(ref, tall, unit):
    if tall:
        height = ref.shape[0] // 4
        return rows_at(ref, unit * height, height, height)
    width = ref.shape[1] // 4
    return ref.at[:, pl.ds(pl.multiple_of(unit * width, LANES), width)]


def gather_kernel(talls, *refs):
    count = len(talls)
    shares, (vec_in, mod_in, cot_in) = refs[:count], refs[count : count + 3]
    wholes, (vec_out, mod_out, cot_out) = (
        refs[count + 3 : 2 * count + 3],
        refs[2 * count + 3 : 2 * count + 6],
    )
    send_sems, recv_sems, local_sems = refs[2 * count + 6 :]
    column, frame, depth, core, across_x, across_y, sibling = neighbours()
    frame_peers = [(column, (frame + shift) % 8) for shift in range(1, 8)]
    greet(frame_peers + [(across_x, frame), (across_y, frame)])
    copies = Copies(send_sems, recv_sems)
    locals_started = []

    def local(source, target):
        copy = pltpu.make_async_copy(source, target, local_sems.at[len(locals_started)])
        copy.start()
        locals_started.append(copy)

    arrivals = []
    local(vec_in, vec_out.at[frame])
    local(mod_in.at[frame], mod_out.at[frame])
    for peer in frame_peers:
        arrivals.append(copies.start(vec_in, vec_out.at[frame], peer))
        arrivals.append(copies.start(mod_in.at[peer[1]], mod_out.at[frame], peer))
    from_depth = []
    for share, whole, tall in zip(shares, wholes, talls):
        own = whole_share(whole, tall, frame)
        local(share, own)
        from_depth.append(
            [
                copies.start(
                    share_unit(share, tall, column),
                    whole_unit(whole, tall, column, frame),
                    (column, ((depth + shift) % 4) * 2 + core),
                )
                for shift in range(1, 4)
            ]
        )
        arrivals.append(copies.start(share, own, (column, sibling)))
    local(cot_in.at[frame], cot_out.at[frame])
    for peer in frame_peers:
        arrivals.append(copies.start(cot_in.at[peer[1]], cot_out.at[frame], peer))

    from_x, from_y, from_far = {}, {}, {}

    def pass_on(index, shift, unit, device):
        source = ((depth + 4 - shift) % 4) * 2 + core
        piece = whole_unit(wholes[index], talls[index], unit, source)
        return copies.start(piece, piece, device)

    def first(index):
        for shift in range(1, 4):
            from_depth[index][shift - 1].wait_recv()
            from_x[index, shift] = pass_on(index, shift, column, (across_x, frame))
            from_y[index, shift] = pass_on(index, shift, column, (across_y, frame))
            arrivals.append(pass_on(index, shift, column, (column, sibling)))

    def second(index):
        for shift in range(1, 4):
            x_first = (index + shift) % 2 == 0
            from_x[index, shift].wait_recv()
            if x_first:
                from_far[index, shift] = pass_on(index, shift, across_x, (across_y, frame))
            arrivals.append(pass_on(index, shift, across_x, (column, sibling)))
            from_y[index, shift].wait_recv()
            if not x_first:
                from_far[index, shift] = pass_on(index, shift, across_y, (across_x, frame))
            arrivals.append(pass_on(index, shift, across_y, (column, sibling)))

    def third(index):
        for shift in range(1, 4):
            from_far[index, shift].wait_recv()
            arrivals.append(pass_on(index, shift, 3 - column, (column, sibling)))

    for step in range(count + 2):
        if step < count:
            first(step)
        if 0 <= step - 1 < count:
            second(step - 1)
        if 0 <= step - 2:
            third(step - 2)
    for copy in arrivals:
        copy.wait_recv()
    copies.finish()
    for copy in locals_started:
        copy.wait()


def gather_all(shares, talls, vec, mod_rows, cot_rows):
    if lax.axis_size("clip") != 4 or lax.axis_size("frame") != 8:
        wholes = [lax.all_gather(share, "frame", axis=0, tiled=True) for share in shares]
        vecs = lax.all_gather(vec, "frame", axis=0)
        mods = lax.all_to_all(mod_rows, "frame", split_axis=0, concat_axis=0, tiled=True)
        cots = lax.all_to_all(cot_rows, "frame", split_axis=0, concat_axis=0, tiled=True)
        return wholes, vecs, mods, cots
    count = len(shares)
    anywhere = pl.BlockSpec(memory_space=pl.ANY)
    out_shape = [
        jax.ShapeDtypeStruct((8 * share.shape[0], share.shape[1]), share.dtype) for share in shares
    ]
    out_shape.append(jax.ShapeDtypeStruct((8,) + vec.shape, vec.dtype))
    out_shape.append(jax.ShapeDtypeStruct(mod_rows.shape, mod_rows.dtype))
    out_shape.append(jax.ShapeDtypeStruct(cot_rows.shape, cot_rows.dtype))
    remote = 21 + count * 25
    outs = pl.pallas_call(
        functools.partial(gather_kernel, tuple(talls)),
        out_shape=out_shape,
        in_specs=[anywhere] * (count + 3),
        out_specs=[anywhere] * (count + 3),
        scratch_shapes=[
            pltpu.SemaphoreType.DMA((remote,)),
            pltpu.SemaphoreType.DMA((remote,)),
            pltpu.SemaphoreType.DMA((count + 3,)),
        ],
        compiler_params=pltpu.CompilerParams(collective_id=0, has_side_effects=True),
        name="gather_all",
    )(*shares, vec, mod_rows, cot_rows)
    return outs[:count], outs[count], outs[count + 1], outs[count + 2]


def add_stream(count, left_at, right_at, out_at, left_buf, right_buf, out_buf, sems):
    def loads(index):
        slot = index % PIECE_SLOTS
        return (
            pltpu.make_async_copy(left_at(index), left_buf.at[slot], sems.at[0, slot]),
            pltpu.make_async_copy(right_at(index), right_buf.at[slot], sems.at[1, slot]),
        )

    def store(index):
        slot = index % PIECE_SLOTS
        return pltpu.make_async_copy(out_buf.at[slot], out_at(index), sems.at[2, slot])

    ahead = min(PIECE_SLOTS - 1, count)
    for index in range(ahead):
        for copy in loads(index):
            copy.start()

    def step(index, carry):
        @pl.when(index + PIECE_SLOTS - 1 < count)
        def _():
            for copy in loads(index + PIECE_SLOTS - 1):
                copy.start()

        for copy in loads(index):
            copy.wait()

        @pl.when(index >= PIECE_SLOTS)
        def _():
            store(index - PIECE_SLOTS).wait()

        slot = index % PIECE_SLOTS
        out_buf[slot] = left_buf[slot] + right_buf[slot]
        store(index).start()
        return carry

    lax.fori_loop(0, count, step, 0)
    for index in range(max(0, count - PIECE_SLOTS), count):
        store(index).wait()


def reduce_kernel(plan, *refs):
    bundles = len(plan)
    refs = list(refs)
    take = lambda number: [refs.pop(0) for _ in range(number)]
    parts = [take(0 if tall else len(widths)) if not tall else take(1) for tall, widths in plan]
    text_in, vec_in, mod_in = take(3)
    outs = take(bundles)
    text_out, vec_out, mod_out = take(3)
    paired, halved, quartered, lined = take(bundles), take(bundles), take(bundles), take(bundles)
    text_got, vec_got = take(2)
    (
        send_sems,
        recv_sems,
        local_sems,
        stream_sems,
        left_buf,
        right_buf,
        out_buf,
        four_buf,
        vec_buf,
        vec_sum,
    ) = refs
    column, frame, depth, core, across_x, across_y, sibling = neighbours()
    far = 3 - column
    frame_peers = [(column, (frame + shift) % 8) for shift in range(1, 8)]
    plane_peers = [(across_x, frame), (across_y, frame), (far, frame)]
    greet(frame_peers + plane_peers)
    copies = Copies(send_sems, recv_sems)

    mod_own = pltpu.make_async_copy(mod_in, mod_out.at[column, frame], local_sems.at[0])
    mod_own.start()
    vec_own = pltpu.make_async_copy(vec_in.at[frame], vec_got.at[frame], local_sems.at[1])
    vec_own.start()
    vec_copies = [copies.start(vec_in.at[peer[1]], vec_got.at[frame], peer) for peer in frame_peers]
    mod_copies = [copies.start(mod_in, mod_out.at[column, frame], peer) for peer in frame_peers]
    text_rows = text_in.shape[0] // 4
    text_copies = [
        copies.start(
            rows_at(text_in, peer[0] * text_rows, text_rows, text_rows), text_got.at[slot], peer
        )
        for slot, peer in enumerate(plane_peers)
    ]

    def part_piece(index, unit, owner):
        tall, widths = plan[index]
        if tall:
            return whole_unit(parts[index][0], True, unit, owner)
        height, width = parts[index][0].shape[0] // 8, paired[index].shape[-1]
        for ref, units in zip(parts[index], widths):
            if unit < units:
                return ref.at[
                    pl.ds(pl.multiple_of(owner * height, height), height),
                    pl.ds(unit * width, width),
                ]
            unit -= units

    from_core = {}
    for index in range(bundles):
        for slot in range(4):
            owner = slot * 2 + 1 - core
            for unit in range(4):
                from_core[index, slot, unit] = copies.start(
                    part_piece(index, unit, owner), paired[index].at[unit, slot], (column, sibling)
                )

    def stream(count, left_at, right_at, out_at):
        add_stream(count, left_at, right_at, out_at, left_buf, right_buf, out_buf, stream_sems)

    from_half, from_quarter, from_line, ends = {}, {}, {}, []

    def pair(index):
        for slot in range(4):
            for unit in range(4):
                from_core[index, slot, unit].wait_recv()
        for unit in range(4):
            stream(
                4,
                lambda slot: part_piece(index, unit, slot * 2 + core),
                lambda slot: paired[index].at[unit, slot],
                lambda slot: paired[index].at[unit, slot],
            )
        for slot in range(4):
            near = across_x if slot < 2 else across_y
            for which, unit in enumerate((near, far)):
                from_half[index, slot, which] = copies.start(
                    paired[index].at[unit, slot], halved[index].at[slot, which], (near, frame)
                )

    def half(index):
        for slot in range(4):
            for which in range(2):
                from_half[index, slot, which].wait_recv()

        def source(step):
            slot, which = step // 2, step % 2
            late = slot // 2
            unit = column + which * (
                (1 - late) * (across_y - column) + late * (across_x - column)
            )
            return paired[index].at[unit, slot]

        place = lambda step: halved[index].at[step // 2, step % 2]
        stream(8, source, place, place)
        for slot in range(4):
            near = across_y if slot < 2 else across_x
            from_quarter[index, slot] = copies.start(
                halved[index].at[slot, 1], quartered[index].at[slot], (near, frame)
            )

    def quarter(index):
        for slot in range(4):
            from_quarter[index, slot].wait_recv()
        place = lambda slot: quartered[index].at[slot]
        stream(4, lambda slot: halved[index].at[slot, 0], place, place)
        for shift in range(1, 4):
            other = (depth + shift) % 4
            from_line[index, shift] = copies.start(
                quartered[index].at[other], lined[index].at[shift - 1], (column, other * 2 + core)
            )

    def total_of_four(own, others, target, height):
        loads = [
            pltpu.make_async_copy(
                source, four_buf.at[slot, pl.ds(0, height)], stream_sems.at[0, slot]
            )
            for slot, source in enumerate([own] + others)
        ]
        for copy in loads:
            copy.start()
        for copy in loads:
            copy.wait()
        total = four_buf[0, 0:height].astype(jnp.float32)
        for slot in range(1, 4):
            total = total + four_buf[slot, 0:height].astype(jnp.float32)
        out_buf[0, 0:height] = total.astype(jnp.bfloat16)
        copy = pltpu.make_async_copy(out_buf.at[0, pl.ds(0, height)], target, stream_sems.at[2, 0])
        copy.start()
        copy.wait()
        for peer in plane_peers:
            ends.append(copies.start(target, target, peer))

    def line(index):
        for shift in range(1, 4):
            from_line[index, shift].wait_recv()
        total_of_four(
            quartered[index].at[depth],
            [lined[index].at[slot] for slot in range(3)],
            share_unit(outs[index], plan[index][0], column),
            lined[index].shape[1],
        )

    def small():
        for copy in vec_copies + mod_copies + text_copies:
            copy.wait_recv()
        mod_own.wait()
        vec_own.wait()
        for peer in plane_peers:
            ends.append(copies.start(mod_out.at[column], mod_out.at[column], peer))
        load = pltpu.make_async_copy(vec_got, vec_buf, local_sems.at[0])
        load.start()
        load.wait()
        vec_sum[...] = jnp.sum(vec_buf[...], axis=0)
        keep = pltpu.make_async_copy(vec_sum, vec_out.at[column], local_sems.at[1])
        keep.start()
        keep.wait()
        for peer in plane_peers:
            ends.append(copies.start(vec_out.at[column], vec_out.at[column], peer))
        total_of_four(
            rows_at(text_in, column * text_rows, text_rows, text_rows),
            [text_got.at[slot] for slot in range(3)],
            rows_at(text_out, column * text_rows, text_rows, text_rows),
            text_rows,
        )

    for step in range(bundles + 3):
        if step < bundles:
            pair(step)
        if 0 <= step - 1 < bundles:
            half(step - 1)
        if 0 <= step - 2 < bundles:
            quarter(step - 2)
        if 0 <= step - 3:
            line(step - 3)
        if step == 1:
            small()
    for copy in ends:
        copy.wait_recv()
    copies.finish()


def reduce_all(parts, talls, text_part, vec_parts, mod_row):
    if lax.axis_size("clip") != 4 or lax.axis_size("frame") != 8:

        def total(part):
            share = lax.psum_scatter(part, "frame", scatter_dimension=0, tiled=True)
            return lax.psum(share, "clip")

        outs = [
            jnp.concatenate([total(part) for part in group], axis=1) for group in parts
        ]
        text = lax.psum(text_part, "clip")
        vec = lax.psum_scatter(vec_parts, "frame", scatter_dimension=0, tiled=True)
        vec = lax.all_gather(vec[0], "clip", axis=0)
        mods = lax.all_gather(lax.all_gather(mod_row, "frame", axis=0), "clip", axis=0)
        return outs, text, vec, mods
    anywhere = pl.BlockSpec(memory_space=pl.ANY)
    plan, out_shape, landing = [], [], [[], [], [], []]
    height = width = 0
    for group, tall in zip(parts, talls):
        rows = group[0].shape[0]
        wide = sum(part.shape[1] for part in group)
        height, width = (rows // 32, wide) if tall else (rows // 8, wide // 4)
        plan.append((tall, tuple(part.shape[1] // width for part in group)))
        out_shape.append(jax.ShapeDtypeStruct((rows // 8, wide), jnp.bfloat16))
        for place, lead in zip(landing, ((4, 4), (4, 2), (4,), (3,))):
            place.append(jax.ShapeDtypeStruct(lead + (height, width), jnp.bfloat16))
    out_shape.append(jax.ShapeDtypeStruct(text_part.shape, jnp.bfloat16))
    out_shape.append(jax.ShapeDtypeStruct((4,) + vec_parts.shape[1:], jnp.float32))
    out_shape.append(jax.ShapeDtypeStruct((4, 8) + mod_row.shape, jnp.float32))
    for place in landing:
        out_shape.extend(place)
    out_shape.append(
        jax.ShapeDtypeStruct((3, text_part.shape[0] // 4, text_part.shape[1]), jnp.bfloat16)
    )
    out_shape.append(jax.ShapeDtypeStruct(vec_parts.shape, jnp.float32))
    operands = [part for group in parts for part in group] + [text_part, vec_parts, mod_row]
    bundles = len(plan)
    remote = bundles * (16 + 8 + 4 + 3 + 3) + 7 + 7 + 3 + 3 + 3 + 3
    piece = (PIECE_SLOTS, height, width)
    outs = pl.pallas_call(
        functools.partial(reduce_kernel, tuple(plan)),
        out_shape=out_shape,
        in_specs=[anywhere] * len(operands),
        out_specs=[anywhere] * len(out_shape),
        scratch_shapes=[
            pltpu.SemaphoreType.DMA((remote,)),
            pltpu.SemaphoreType.DMA((remote,)),
            pltpu.SemaphoreType.DMA((2,)),
            pltpu.SemaphoreType.DMA((3, PIECE_SLOTS)),
            pltpu.VMEM(piece, jnp.bfloat16),
            pltpu.VMEM(piece, jnp.bfloat16),
            pltpu.VMEM(piece, jnp.bfloat16),
            pltpu.VMEM((4, height, width), jnp.bfloat16),
            pltpu.VMEM(vec_parts.shape, jnp.float32),
            pltpu.VMEM(vec_parts.shape[1:], jnp.float32),
        ],
        compiler_params=pltpu.CompilerParams(
            collective_id=1, has_side_effects=True, vmem_limit_bytes=32 * 1024 * 1024
        ),
        name="reduce_all",
    )(*operands)
    return outs[:bundles], outs[bundles], outs[bundles + 1], outs[bundles + 2]


def pack_rows(parts, rows):
    flat = jnp.concatenate(parts, axis=-1)
    flat = jnp.pad(flat, [(0, 0)] * (flat.ndim - 1) + [(0, rows * LANES - flat.shape[-1])])
    return flat.reshape(flat.shape[:-1] + (rows, LANES))


def on_device(
    latents,
    cotangent,
    text_tokens,
    text_lengths,
    clip_frames,
    timesteps,
    motion_free,
    modulation_weight,
    modulation_bias,
    spatial_input,
    spatial_output,
    spatial_bias,
    text_projection,
    cross_query,
    cross_memory,
    cross_output,
    cross_bias,
    expand_weight,
    expand_bias,
    reduce_weight,
    reduce_bias,
    temporal_gain,
    temporal_shift,
    temporal_input,
    temporal_output,
    temporal_bias,
    temporal_gate,
):
    frame_count = lax.axis_size("frame")
    frame_index = lax.axis_index("frame")
    patch_count = latents.shape[2]
    model_width = latents.shape[3]
    head_size = model_width // HEADS
    att_scale = 1.0 / math.sqrt(head_size)
    slot_count = clip_frames.shape[1]
    text_count = text_tokens.shape[2]
    frame_ids = jnp.arange(frame_count, dtype=jnp.int32)
    clip_ids = assign_clips(clip_frames[0], frame_count)
    slot_ids = jnp.arange(slot_count, dtype=jnp.int32)
    own_clip = jnp.sum(jnp.where(frame_ids == frame_index, clip_ids, 0))
    own_onehot = (slot_ids == own_clip).astype(jnp.float32)
    own_keep = 1.0 - jnp.sum(jnp.where(slot_ids == own_clip, motion_free[0], 0)).astype(jnp.float32)
    own_length = jnp.sum(jnp.where(slot_ids == own_clip, text_lengths[0], 0))
    conditioning = embed_time(timesteps[0], model_width).astype(jnp.bfloat16)
    row_count = modulation_weight.shape[0]
    cond_rows = lax.dynamic_slice_in_dim(conditioning, frame_index * row_count, row_count, 1)
    bias_width = modulation_bias.shape[0]
    bias_placed = lax.dynamic_update_slice_in_dim(
        jnp.zeros((6 * model_width,), jnp.float32),
        modulation_bias.astype(jnp.float32),
        frame_index * bias_width,
        0,
    )
    modulation_part = (
        jnp.dot(cond_rows, modulation_weight, preferred_element_type=jnp.float32)
        + bias_placed[None, :]
    )
    share_rows = text_projection.shape[0]
    text_share = lax.dynamic_slice_in_dim(
        text_tokens[0], frame_index * text_projection.shape[0], text_projection.shape[0], 2
    )
    own_text = lax.dynamic_index_in_dim(text_tokens[0], own_clip, 0, keepdims=False)
    vectors = (
        spatial_bias,
        cross_bias,
        expand_bias,
        reduce_bias,
        temporal_gain,
        temporal_shift,
        temporal_bias,
        temporal_gate,
    )
    vector_sizes = [vector.shape[0] for vector in vectors]
    vector_rows = -(-sum(vector_sizes) // (8 * LANES)) * 8
    packed_vectors = pack_rows([vector.astype(jnp.float32) for vector in vectors], vector_rows)
    mod_rows_high = -(-(6 * model_width) // (8 * LANES)) * 8
    frame_onehot = (clip_ids[:, None] == slot_ids[None, :]).astype(jnp.float32)
    frame_modulation = jnp.sum(frame_onehot[:, :, None] * modulation_part[None], axis=1)
    talls = (True, False, False, False, True, False)
    wholes, vecs, mods, cot_columns = gather_all(
        (
            text_projection,
            jnp.concatenate([spatial_input, spatial_output], axis=1),
            jnp.concatenate([cross_query, cross_memory, cross_output], axis=1),
            expand_weight,
            reduce_weight,
            jnp.concatenate([temporal_input, temporal_output], axis=1),
        ),
        talls,
        packed_vectors,
        pack_rows([frame_modulation], mod_rows_high),
        cotangent[0, 0].reshape(frame_count, patch_count // frame_count, model_width),
    )
    projection, whole_spatial, whole_text, whole_expand, whole_reduce, whole_time = wholes
    context = jnp.dot(own_text, projection, preferred_element_type=jnp.float32)
    own_modulation = jnp.sum(mods, axis=0).reshape(-1)[: 6 * model_width]
    shift_attend, scale_attend, gate_attend, shift_feed, scale_feed, gate_feed = jnp.split(
        own_modulation, 6
    )
    vecs = vecs.reshape(frame_count, -1)[:, : sum(vector_sizes)]
    vector_ends = [sum(vector_sizes[: index + 1]) for index in range(len(vector_sizes) - 1)]
    (
        whole_bias,
        whole_cross_bias,
        whole_expand_bias,
        whole_reduce_bias,
        whole_gain,
        whole_shift,
        whole_temporal_bias,
        whole_gate,
    ) = [part.reshape(-1) for part in jnp.split(vecs, vector_ends, axis=1)]
    whole_input, whole_output = whole_spatial[:, : 3 * model_width], whole_spatial[:, 3 * model_width :]
    whole_query = whole_text[:, :model_width]
    whole_memory = whole_text[:, model_width : 3 * model_width]
    whole_cross = whole_text[:, 3 * model_width :]
    whole_temporal, whole_temporal_out = whole_time[:, : 3 * model_width], whole_time[:, 3 * model_width :]
    tokens = latents[0, 0].astype(jnp.float32)
    normed_attend = modulate(tokens, shift_attend, scale_attend).astype(jnp.bfloat16)
    spatial_heads = jnp.dot(normed_attend, whole_input, preferred_element_type=jnp.float32).astype(
        jnp.bfloat16
    )
    spatial_heads = spatial_heads.reshape(patch_count, 1, 3, HEADS, head_size)
    spatial_att, spatial_logsum = attend(
        spatial_heads[:, :, 0], spatial_heads[:, :, 1], spatial_heads[:, :, 2], None, att_scale
    )
    spatial_low = spatial_att.reshape(patch_count, model_width).astype(jnp.bfloat16)
    branch_attend = jnp.dot(
        spatial_low, whole_output, preferred_element_type=jnp.float32
    ) + whole_bias.astype(jnp.float32)
    after_attend = tokens + gate_attend * branch_attend
    after_low = after_attend.astype(jnp.bfloat16)
    cross_heads = jnp.dot(after_low, whole_query, preferred_element_type=jnp.float32).astype(
        jnp.bfloat16
    )
    cross_heads = cross_heads.reshape(patch_count, 1, HEADS, head_size)
    context_low = context.astype(jnp.bfloat16)
    memory_heads = jnp.dot(context_low, whole_memory, preferred_element_type=jnp.float32).astype(
        jnp.bfloat16
    )
    memory_heads = memory_heads.reshape(text_count, 1, 2, HEADS, head_size)
    text_mask = (jnp.arange(text_count, dtype=jnp.int32) < own_length)[None, None, None, :]
    cross_att, cross_logsum = attend(
        cross_heads, memory_heads[:, :, 0], memory_heads[:, :, 1], text_mask, att_scale
    )
    cross_low = cross_att.reshape(patch_count, model_width).astype(jnp.bfloat16)
    branch_cross = jnp.dot(
        cross_low, whole_cross, preferred_element_type=jnp.float32
    ) + whole_cross_bias.astype(jnp.float32)
    after_cross = after_attend + branch_cross
    normed_feed = modulate(after_cross, shift_feed, scale_feed).astype(jnp.bfloat16)
    hidden_pre = jnp.dot(
        normed_feed, whole_expand, preferred_element_type=jnp.float32
    ) + whole_expand_bias.astype(jnp.float32)
    hidden_low = smooth_gelu(hidden_pre).astype(jnp.bfloat16)
    branch_feed = jnp.dot(
        hidden_low, whole_reduce, preferred_element_type=jnp.float32
    ) + whole_reduce_bias.astype(jnp.float32)
    after_feed = after_cross + gate_feed * branch_feed
    sent_low = after_feed.astype(jnp.bfloat16)
    time_mask = (clip_ids[:, None] == clip_ids[None, :])[None, None]
    gain_float = whole_gain.astype(jnp.float32)
    shift_float = whole_shift.astype(jnp.float32)
    columns = lax.all_to_all(sent_low[None], "frame", split_axis=1, concat_axis=0, tiled=True)
    frames_here = columns.shape[0]
    positions = columns.shape[1]
    normed_time = affine_norm(columns.astype(jnp.float32), gain_float, shift_float).astype(
        jnp.bfloat16
    )
    time_heads = jnp.einsum(
        "fpd,de->fpe", normed_time, whole_temporal, preferred_element_type=jnp.float32
    )
    time_heads = time_heads.astype(jnp.bfloat16).reshape(
        frames_here, positions, 3, HEADS, head_size
    )
    time_att, time_logsum = attend(
        time_heads[:, :, 0], time_heads[:, :, 1], time_heads[:, :, 2], time_mask, att_scale
    )
    time_low = time_att.reshape(frames_here, positions, model_width).astype(jnp.bfloat16)
    result = jnp.einsum(
        "fpd,de->fpe", time_low, whole_temporal_out, preferred_element_type=jnp.float32
    )
    result = result + whole_temporal_bias.astype(jnp.float32)
    result_low = result.astype(jnp.bfloat16)
    kept_state = (normed_time, time_heads, time_low, time_logsum)
    gate_keep = whole_gate.astype(jnp.float32) * own_keep
    upstream = cotangent[0, 0].astype(jnp.float32)
    keep_frames = 1.0 - jnp.sum(frame_onehot * motion_free[0].astype(jnp.float32)[None, :], axis=1)
    back_columns = (
        cot_columns.astype(jnp.float32) * (keep_frames[:, None, None] * whole_gate[None, None, :])
    ).astype(jnp.bfloat16)
    normed_time, time_heads, time_low, time_logsum = kept_state
    frames_here, positions = (columns.shape[0], columns.shape[1])
    back_temporal_bias = jnp.sum(back_columns.astype(jnp.float32), axis=(0, 1))
    back_temporal_out = jnp.einsum(
        "fpd,fpe->de", time_low, back_columns, preferred_element_type=jnp.float32
    )
    back_time_att = jnp.einsum(
        "fpe,de->fpd", back_columns, whole_temporal_out, preferred_element_type=jnp.float32
    )
    back_time_att = back_time_att.astype(jnp.bfloat16).reshape(
        frames_here, positions, HEADS, head_size
    )
    back_time_queries, back_time_keys, back_time_values = attend_back(
        time_heads[:, :, 0],
        time_heads[:, :, 1],
        time_heads[:, :, 2],
        time_mask,
        att_scale,
        time_logsum,
        back_time_att,
    )
    back_time_heads = jnp.stack([back_time_queries, back_time_keys, back_time_values], axis=2)
    back_time_heads = back_time_heads.reshape(frames_here, positions, 3 * model_width).astype(
        jnp.bfloat16
    )
    back_temporal = jnp.einsum(
        "fpd,fpe->de", normed_time, back_time_heads, preferred_element_type=jnp.float32
    )
    back_normed = jnp.einsum(
        "fpe,de->fpd", back_time_heads, whole_temporal, preferred_element_type=jnp.float32
    )
    unused_norm, norm_back = jax.vjp(
        affine_norm, columns.astype(jnp.float32), gain_float, shift_float
    )
    back_inputs, back_gain, back_shift = norm_back(back_normed)
    returned, back_return = jnp.split(
        lax.all_to_all(
            jnp.concatenate([result_low, back_inputs.astype(jnp.bfloat16)], axis=2),
            "frame",
            split_axis=0,
            concat_axis=1,
            tiled=True,
        ),
        2,
        axis=2,
    )
    temporal_value = returned[0].astype(jnp.float32)
    block_output = (after_feed + gate_keep * temporal_value).astype(jnp.bfloat16)[None, None]
    back_gate = jnp.sum(upstream * temporal_value, axis=0) * own_keep
    back_feed_total = upstream + back_return[0].astype(jnp.float32)
    back_gate_feed = jnp.sum(back_feed_total * branch_feed, axis=0)
    back_branch_feed = (back_feed_total * gate_feed).astype(jnp.bfloat16)
    back_reduce_bias = jnp.sum(back_branch_feed.astype(jnp.float32), axis=0)
    back_reduce = jnp.einsum(
        "pf,pd->fd", hidden_low, back_branch_feed, preferred_element_type=jnp.float32
    )
    back_hidden = jnp.einsum(
        "pd,fd->pf", back_branch_feed, whole_reduce, preferred_element_type=jnp.float32
    )
    unused_gelu, gelu_back = jax.vjp(smooth_gelu, hidden_pre)
    back_pre = gelu_back(back_hidden)[0].astype(jnp.bfloat16)
    back_expand_bias = jnp.sum(back_pre.astype(jnp.float32), axis=0)
    back_expand = jnp.einsum("pd,pf->df", normed_feed, back_pre, preferred_element_type=jnp.float32)
    back_normed_feed = jnp.einsum(
        "pf,df->pd", back_pre, whole_expand, preferred_element_type=jnp.float32
    )
    unused_feed, feed_back = jax.vjp(modulate, after_cross, shift_feed, scale_feed)
    back_cross_in, back_shift_feed, back_scale_feed = feed_back(back_normed_feed)
    back_after_cross = back_feed_total + back_cross_in
    back_branch_cross = back_after_cross.astype(jnp.bfloat16)
    back_cross_bias = jnp.sum(back_branch_cross.astype(jnp.float32), axis=0)
    back_cross_output = jnp.einsum(
        "pd,pe->de", cross_low, back_branch_cross, preferred_element_type=jnp.float32
    )
    back_cross_att = jnp.einsum(
        "pe,de->pd", back_branch_cross, whole_cross, preferred_element_type=jnp.float32
    )
    back_cross_att = back_cross_att.astype(jnp.bfloat16).reshape(patch_count, 1, HEADS, head_size)
    back_cross_queries, back_memory_keys, back_memory_values = attend_back(
        cross_heads,
        memory_heads[:, :, 0],
        memory_heads[:, :, 1],
        text_mask,
        att_scale,
        cross_logsum,
        back_cross_att,
    )
    back_cross_heads = back_cross_queries.reshape(patch_count, model_width).astype(jnp.bfloat16)
    back_memory_heads = jnp.stack([back_memory_keys, back_memory_values], axis=2)
    back_memory_heads = back_memory_heads.reshape(text_count, 2 * model_width).astype(jnp.bfloat16)
    back_cross_query = jnp.einsum(
        "pd,pe->de", after_low, back_cross_heads, preferred_element_type=jnp.float32
    )
    back_cross_memory = jnp.einsum(
        "td,te->de", context_low, back_memory_heads, preferred_element_type=jnp.float32
    )
    back_context = jnp.einsum(
        "te,de->td", back_memory_heads, whole_memory, preferred_element_type=jnp.float32
    )
    back_after_attend = back_after_cross + jnp.einsum(
        "pe,de->pd", back_cross_heads, whole_query, preferred_element_type=jnp.float32
    )
    back_gate_attend = jnp.sum(back_after_attend * branch_attend, axis=0)
    back_branch_attend = (back_after_attend * gate_attend).astype(jnp.bfloat16)
    back_spatial_bias = jnp.sum(back_branch_attend.astype(jnp.float32), axis=0)
    back_spatial_output = jnp.einsum(
        "pd,pe->de", spatial_low, back_branch_attend, preferred_element_type=jnp.float32
    )
    back_spatial_att = jnp.einsum(
        "pe,de->pd", back_branch_attend, whole_output, preferred_element_type=jnp.float32
    )
    back_spatial_att = back_spatial_att.astype(jnp.bfloat16).reshape(
        patch_count, 1, HEADS, head_size
    )
    back_spatial_queries, back_spatial_keys, back_spatial_values = attend_back(
        spatial_heads[:, :, 0],
        spatial_heads[:, :, 1],
        spatial_heads[:, :, 2],
        None,
        att_scale,
        spatial_logsum,
        back_spatial_att,
    )
    back_spatial_heads = jnp.stack(
        [back_spatial_queries, back_spatial_keys, back_spatial_values], axis=2
    )
    back_spatial_heads = back_spatial_heads.reshape(patch_count, 3 * model_width).astype(
        jnp.bfloat16
    )
    back_spatial_input = jnp.einsum(
        "pd,pe->de", normed_attend, back_spatial_heads, preferred_element_type=jnp.float32
    )
    back_normed_attend = jnp.einsum(
        "pe,de->pd", back_spatial_heads, whole_input, preferred_element_type=jnp.float32
    )
    unused_attend, attend_norm_back = jax.vjp(modulate, tokens, shift_attend, scale_attend)
    back_tokens, back_shift_attend, back_scale_attend = attend_norm_back(back_normed_attend)
    input_gradient = (back_after_attend + back_tokens).astype(jnp.bfloat16)[None, None]
    back_modulation_row = jnp.concatenate(
        [
            back_shift_attend,
            back_scale_attend,
            back_gate_attend,
            back_shift_feed,
            back_scale_feed,
            back_gate_feed,
        ]
    )
    own_conditioning = jnp.sum(own_onehot[:, None] * conditioning.astype(jnp.float32), axis=0)
    all_context = lax.all_gather(back_context.astype(jnp.bfloat16), "frame", axis=0)
    context_total = jnp.einsum("fs,ftd->std", frame_onehot, all_context.astype(jnp.float32))
    back_text_projection = jnp.einsum(
        "stk,std->kd",
        text_share,
        context_total.astype(jnp.bfloat16),
        preferred_element_type=jnp.float32,
    )
    back_vectors = (
        back_spatial_bias,
        back_cross_bias,
        back_expand_bias,
        back_reduce_bias,
        back_gain,
        back_shift,
        back_temporal_bias,
        back_gate,
    )
    vector_parts = pack_rows(
        [vector.reshape(frame_count, -1) for vector in back_vectors], vector_rows
    )
    row_high = -(-(7 * model_width) // (8 * LANES)) * 8
    row_parts = pack_rows([back_modulation_row, own_conditioning], row_high)
    low = lambda part: part.astype(jnp.bfloat16)
    totals, text_total, vec_totals, rows_all = reduce_all(
        (
            (low(back_temporal), low(back_temporal_out)),
            (low(back_reduce),),
            (low(back_expand),),
            (low(back_cross_query), low(back_cross_memory), low(back_cross_output)),
            (low(back_spatial_input), low(back_spatial_output)),
        ),
        (False, True, False, False, False),
        low(back_text_projection),
        vector_parts,
        row_parts,
    )
    high = lambda part: part.astype(jnp.float32)
    total_time, total_reduce, total_expand, total_text, total_spatial = totals
    vec_total = jnp.sum(vec_totals, axis=0).reshape(-1)
    vec_total = jnp.split(vec_total[: sum(vector_sizes)], vector_ends)
    rows_all = rows_all.reshape(-1, row_high * LANES)
    rows_gradient = rows_all[:, : 6 * model_width]
    rows_condition = lax.dynamic_slice_in_dim(
        rows_all, 6 * model_width + frame_index * row_count, row_count, 1
    )
    back_modulation_weight = jnp.einsum(
        "nd,ne->de", rows_condition, rows_gradient, precision=lax.Precision.HIGHEST
    )
    back_modulation_bias = jnp.sum(
        lax.dynamic_slice_in_dim(rows_gradient, frame_index * bias_width, bias_width, 1), axis=0
    )
    matrix_totals = (
        high(total_spatial[:, : 3 * model_width]),
        high(total_spatial[:, 3 * model_width :]),
        high(total_text[:, :model_width]),
        high(total_text[:, model_width : 3 * model_width]),
        high(total_text[:, 3 * model_width :]),
        high(total_expand),
        high(total_reduce),
        high(total_time[:, : 3 * model_width]),
        high(total_time[:, 3 * model_width :]),
    )
    others = (back_modulation_weight, back_modulation_bias, high(text_total)) + tuple(vec_total)
    return (
        block_output,
        input_gradient,
        others[0],
        others[1],
        matrix_totals[0],
        matrix_totals[1],
        others[3],
        others[2],
        matrix_totals[2],
        matrix_totals[3],
        matrix_totals[4],
        others[4],
        matrix_totals[5],
        others[5],
        matrix_totals[6],
        others[6],
        others[7],
        others[8],
        matrix_totals[7],
        matrix_totals[8],
        others[9],
        others[10],
    )


def solution(mesh):
    placed = (
        P("clip", "frame", None, None),
        P("clip", "frame", None, None),
        P("clip", None, None, None),
        P("clip", None),
        P("clip", None),
        P("clip", None),
        P("clip", None),
        P("frame", None),
        P("frame"),
        P("frame", None),
        P("frame", None),
        P("frame"),
        P("frame", None),
        P("frame", None),
        P("frame", None),
        P("frame", None),
        P("frame"),
        P("frame", None),
        P("frame"),
        P("frame", None),
        P("frame"),
        P("frame"),
        P("frame"),
        P("frame", None),
        P("frame", None),
        P("frame"),
        P("frame"),
    )
    return jax.shard_map(
        on_device,
        mesh=mesh,
        in_specs=placed,
        out_specs=(
            P("clip", "frame", None, None),
            P("clip", "frame", None, None),
            P("frame", None),
            P("frame"),
            P("frame", None),
            P("frame", None),
            P("frame"),
            P("frame", None),
            P("frame", None),
            P("frame", None),
            P("frame", None),
            P("frame"),
            P("frame", None),
            P("frame"),
            P("frame", None),
            P("frame"),
            P("frame"),
            P("frame"),
            P("frame", None),
            P("frame", None),
            P("frame"),
            P("frame"),
        ),
        check_vma=False,
    )
```

```python
import functools
import math
import types

import jax
import jax.numpy as jnp
from jax import lax
from jax.experimental import pallas as pl
from jax.experimental.pallas import tpu as pltpu
from jax.sharding import PartitionSpec as P

HEADS = 16


eps_norm = 1e-06
big_negative = -1e30


def assign_clips(frame_counts, frame_count):
    slot_count = frame_counts.shape[0]
    slot_ids = jnp.arange(slot_count, dtype=jnp.int32)
    longest = jnp.max(frame_counts)
    long_slot = jnp.min(jnp.where(frame_counts == longest, slot_ids, slot_count))
    frame_ids = jnp.arange(frame_count, dtype=jnp.int32)
    long_gaps = jnp.maximum(longest - 1, 1)
    frame_gaps = frame_count - 1
    step_index = (frame_ids * long_gaps + frame_gaps - 1) // frame_gaps
    on_long = step_index * frame_gaps // long_gaps == frame_ids
    long_marks = on_long.astype(jnp.int32)
    before_count = jnp.cumsum(long_marks) - long_marks
    order_rank = frame_ids - before_count
    rest_counts = jnp.where(slot_ids == long_slot, 0, frame_counts)
    rest_ends = jnp.cumsum(rest_counts)
    rest_ids = jnp.sum((rest_ends[None, :] <= order_rank[:, None]).astype(jnp.int32), axis=1)
    return jnp.where(on_long, long_slot, rest_ids)


def normalize(values):
    average = jnp.mean(values, axis=-1, keepdims=True)
    centred = values - average
    spread = jnp.mean(centred * centred, axis=-1, keepdims=True)
    return centred * lax.rsqrt(spread + eps_norm)


def normal_parts(values):
    average = jnp.mean(values, axis=-1, keepdims=True)
    centred = values - average
    rate = lax.rsqrt(jnp.mean(centred * centred, axis=-1, keepdims=True) + eps_norm)
    return centred * rate, rate


def modulate(values, offset, scaling):
    return normalize(values) * (1.0 + scaling) + offset


def affine_norm(values, norm_gain, offset):
    return normalize(values) * norm_gain + offset


def smooth_gelu(values):
    return jax.nn.gelu(values, approximate=True)


def slope_gelu(values):
    inner = math.sqrt(2.0 / math.pi)
    bent = jnp.tanh(inner * (values + 0.044715 * values * values * values))
    steep = inner * (1.0 + 3.0 * 0.044715 * values * values)
    return 0.5 * (1.0 + bent) + 0.5 * values * (1.0 - bent * bent) * steep


def embed_time(time_steps, model_width):
    half_width = model_width // 2
    frequency = jnp.exp(-math.log(10000.0) * jnp.arange(half_width, dtype=jnp.float32) / half_width)
    angles = time_steps.astype(jnp.float32)[:, None] * frequency[None, :]
    return jax.nn.silu(jnp.concatenate([jnp.cos(angles), jnp.sin(angles)], axis=1))


def attend(queries, key_rows, values, valid_mask, att_scale):
    scores = (
        jnp.einsum("qbhd,kbhd->bhqk", queries, key_rows, preferred_element_type=jnp.float32)
        * att_scale
    )
    if valid_mask is not None:
        scores = jnp.where(valid_mask, scores, big_negative)
    largest = jnp.max(scores, axis=-1, keepdims=True)
    summed = jnp.sum(jnp.exp(scores - largest), axis=-1, keepdims=True)
    logsum = largest + jnp.log(summed)
    weights = jnp.exp(scores - logsum).astype(jnp.bfloat16)
    output = jnp.einsum("bhqk,kbhd->qbhd", weights, values, preferred_element_type=jnp.float32)
    return (output, logsum)


def attend_back(queries, key_rows, values, valid_mask, att_scale, logsum, upstream):
    scores = (
        jnp.einsum("qbhd,kbhd->bhqk", queries, key_rows, preferred_element_type=jnp.float32)
        * att_scale
    )
    if valid_mask is not None:
        scores = jnp.where(valid_mask, scores, big_negative)
    weights = jnp.exp(scores - logsum)
    back_weights = jnp.einsum(
        "qbhd,kbhd->bhqk", upstream, values, preferred_element_type=jnp.float32
    )
    back_values = jnp.einsum(
        "bhqk,qbhd->kbhd",
        weights.astype(jnp.bfloat16),
        upstream,
        preferred_element_type=jnp.float32,
    )
    inner_sum = jnp.sum(back_weights * weights, axis=-1, keepdims=True)
    back_scores = (weights * (back_weights - inner_sum)).astype(jnp.bfloat16)
    back_queries = (
        jnp.einsum("bhqk,kbhd->qbhd", back_scores, key_rows, preferred_element_type=jnp.float32)
        * att_scale
    )
    back_keys = (
        jnp.einsum("bhqk,qbhd->kbhd", back_scores, queries, preferred_element_type=jnp.float32)
        * att_scale
    )
    return (back_queries, back_keys, back_values)


MESH_ID = pl.DeviceIdType.MESH
LANES = 128
PIECE_SLOTS = 4


def neighbours():
    column = lax.axis_index("clip")
    frame = lax.axis_index("frame")
    depth = frame // 2
    core = frame % 2
    across_x = column + 1 - 2 * (column % 2)
    across_y = column + 2 - 4 * (column // 2)
    sibling = frame + 1 - 2 * core
    return column, frame, depth, core, across_x, across_y, sibling


def greet(peers):
    barrier = pltpu.get_barrier_semaphore()
    for peer in peers:
        pl.semaphore_signal(barrier, inc=1, device_id=peer, device_id_type=MESH_ID)
    pl.semaphore_wait(barrier, len(peers))


class Copies:
    def __init__(self, send_sems, recv_sems):
        self.send_sems, self.recv_sems, self.count, self.started = send_sems, recv_sems, 0, []
        self.maybe = []

    def start(self, source, target, device):
        copy = pltpu.make_async_remote_copy(
            src_ref=source,
            dst_ref=target,
            send_sem=self.send_sems.at[self.count],
            recv_sem=self.recv_sems.at[self.count],
            device_id=device,
            device_id_type=MESH_ID,
        )
        self.count += 1
        assert self.count <= self.send_sems.shape[0]
        copy.start()
        self.started.append(copy)
        return copy

    def start_if(self, condition, source, target, device, recv_sem):
        copy = pltpu.make_async_remote_copy(
            src_ref=source,
            dst_ref=target,
            send_sem=self.send_sems.at[self.count],
            recv_sem=recv_sem,
            device_id=device,
            device_id_type=MESH_ID,
        )
        self.count += 1
        assert self.count <= self.send_sems.shape[0]
        pl.when(condition)(copy.start)
        self.maybe.append((condition, copy))

    def finish(self):
        for copy in self.started:
            copy.wait_send()
        for condition, copy in self.maybe:
            pl.when(condition)(copy.wait_send)


def rows_at(ref, start, size, step):
    return ref.at[pl.ds(pl.multiple_of(start, step), size), :]


def whole_unit(ref, tall, unit, frame):
    if tall:
        height = ref.shape[0] // 32
        return rows_at(ref, frame * (4 * height) + unit * height, height, height)
    height, width = ref.shape[0] // 8, ref.shape[1] // 4
    return ref.at[
        pl.ds(pl.multiple_of(frame * height, height), height),
        pl.ds(pl.multiple_of(unit * width, LANES), width),
    ]


def whole_share(ref, tall, frame):
    height = ref.shape[0] // 8
    return rows_at(ref, frame * height, height, height)


def share_unit(ref, tall, unit):
    if tall:
        height = ref.shape[0] // 4
        return rows_at(ref, unit * height, height, height)
    width = ref.shape[1] // 4
    return ref.at[:, pl.ds(pl.multiple_of(unit * width, LANES), width)]


def gather_all(shares, vec, mod_rows):
    wholes = [lax.all_gather(share, "frame", axis=0, tiled=True) for share in shares]
    vecs = lax.all_gather(vec, "frame", axis=0)
    mods = lax.all_to_all(mod_rows, "frame", split_axis=0, concat_axis=0, tiled=True)
    return wholes, vecs, mods


def add_stream(count, left_at, right_at, out_at, left_buf, right_buf, out_buf, sems):
    def loads(index):
        slot = index % PIECE_SLOTS
        return (
            pltpu.make_async_copy(left_at(index), left_buf.at[slot], sems.at[0, slot]),
            pltpu.make_async_copy(right_at(index), right_buf.at[slot], sems.at[1, slot]),
        )

    def store(index):
        slot = index % PIECE_SLOTS
        return pltpu.make_async_copy(out_buf.at[slot], out_at(index), sems.at[2, slot])

    ahead = min(PIECE_SLOTS - 1, count)
    for index in range(ahead):
        for copy in loads(index):
            copy.start()

    def step(index, carry):
        @pl.when(index + PIECE_SLOTS - 1 < count)
        def _():
            for copy in loads(index + PIECE_SLOTS - 1):
                copy.start()

        for copy in loads(index):
            copy.wait()

        @pl.when(index >= PIECE_SLOTS)
        def _():
            store(index - PIECE_SLOTS).wait()

        slot = index % PIECE_SLOTS
        out_buf[slot] = left_buf[slot] + right_buf[slot]
        store(index).start()
        return carry

    lax.fori_loop(0, count, step, 0)
    for index in range(max(0, count - PIECE_SLOTS), count):
        store(index).wait()


ROW_TILE = 64
HEAD_LANES = 128
MOD_ROWS = 6


def dot_rows(left, right):
    return lax.dot_general(
        left, right, (((1,), (1,)), ((), ())), preferred_element_type=jnp.float32
    )


def dot_plain(left, right):
    return jnp.dot(left, right, preferred_element_type=jnp.float32)


def run_tiles(body, count, ins, outs):
    pltpu.emit_pipeline(
        body,
        grid=(count,),
        in_specs=[pl.BlockSpec(block, index) for _, block, index in ins],
        out_specs=[pl.BlockSpec(block, index) for _, block, index in outs],
    )(*[ref for ref, _, _ in ins], *[ref for ref, _, _ in outs])


def by_rows(ref, size):
    if len(ref.shape) == 4:
        return (ref, (1,) + ref.shape[1:], lambda step: (step, 0, 0, 0))
    return (ref, (size, ref.shape[1]), lambda step: (step, 0))


def by_columns(ref, size):
    return (ref, (ref.shape[0], size), lambda step: (0, step))


def tile_rows(step, size):
    return pl.ds(pl.multiple_of(step * size, size), size)


def add_row(rows, which, values):
    rows[which : which + 1, :] += jnp.sum(values, axis=0, keepdims=True)


def split_heads(source, first, heads, width, count):
    height = source.shape[0]
    tile = min(height, ROW_TILE)

    def step(index, carry):
        rows = tile_rows(index, tile)
        for head in range(count):
            start = first + head * width
            heads[head, rows, 0:width] = source[rows, start : start + width]
        return carry

    lax.fori_loop(0, height // tile, step, 0)


def merge_heads(heads, target, first, width, count):
    height = target.shape[0]
    tile = min(height, ROW_TILE)

    def step(index, carry):
        rows = tile_rows(index, tile)
        joined = jnp.concatenate([heads[head, rows, 0:width] for head in range(count)], axis=1)
        target[rows, first : first + width * count] = joined
        return carry

    lax.fori_loop(0, height // tile, step, 0)


def attention_back(att_scale, queries, keys, values, mask, logsum, upstream, outs):
    out_queries, out_keys, out_values = outs
    count = queries.shape[0]

    def body(query, key, value):
        head = pl.program_id(0)
        query, key, value, given = query[0], key[0], value[0], upstream[head]
        scores = dot_rows(key, query) * att_scale
        if mask is not None:
            scores = scores + mask[:, 0:1]
        weights = jnp.exp(scores - logsum[head, 0:1, :])
        back_weights = dot_rows(value, given)
        inner = jnp.sum(back_weights * weights, axis=0, keepdims=True)
        back_scores = (weights * (back_weights - inner)).astype(jnp.bfloat16)
        out_values[head] = dot_plain(weights.astype(jnp.bfloat16), given).astype(jnp.bfloat16)
        out_keys[head] = (dot_plain(back_scores, query) * att_scale).astype(jnp.bfloat16)
        turned = lax.dot_general(
            key, back_scores, (((0,), (0,)), ((), ())), preferred_element_type=jnp.float32
        )
        out_queries[head] = (turned * att_scale).T.astype(jnp.bfloat16)

    per_head = lambda ref: (ref, (1,) + ref.shape[1:], lambda step: (step, 0, 0))
    run_tiles(body, count, [per_head(queries), per_head(keys), per_head(values)], [])


ROW = types.SimpleNamespace(
    shift_a=0, scale_a=1, gate_a=2, shift_m=3, scale_m=4, gate_m=5, condition=6, gate_t=7,
    spatial=8, cross=9, reduce=10, gain=11, shift=12, temporal=13, expand=14, high=24,
)


def back_stages(r, att_scale):
    width = r.running.shape[1]
    head_size = width // HEADS
    third = width // 3
    plain = jnp.float32

    def clear():
        r.row_sums[...] = jnp.zeros_like(r.row_sums)
        for heads in (r.head_in, r.head_query, r.head_key, r.head_value):
            heads[...] = jnp.zeros_like(heads)

    def feed_first():
        def body(cot, sent, branch):
            rows = tile_rows(pl.program_id(0), ROW_TILE)
            total = cot[...].astype(plain) + sent[...].reshape(cot.shape).astype(plain)
            r.running[rows, :] = total
            add_row(r.row_sums, ROW.gate_m, total * branch[...].astype(plain))
            down = (total * r.mods[5:6, :]).astype(jnp.bfloat16)
            r.low[rows, :] = down
            add_row(r.row_sums, ROW.reduce, down.astype(plain))

        ins = [by_rows(ref, ROW_TILE) for ref in (r.cotangent, r.back_sent, r.branch_feed)]
        run_tiles(body, r.low.shape[0] // ROW_TILE, ins, [])

    def part_by_rows(turned, right, target, size, place=0):
        def body(left, out):
            out[...] = dot_plain(left[...], right()).astype(jnp.bfloat16)

        run_tiles(
            body,
            turned.shape[0] // size,
            [by_rows(turned, size)],
            [(target, (size, width), lambda step: (step, place))],
        )

    def part_by_columns(turned, right, target, size, first=0, count=None):
        def body(left, out):
            columns = tile_rows(pl.program_id(0) + first, size)
            out[...] = dot_plain(left[...], right[:, columns]).astype(jnp.bfloat16)

        whole = (turned, turned.shape, lambda step: (0, 0))
        run_tiles(
            body,
            target.shape[1] // size if count is None else count,
            [whole],
            [(target, (target.shape[0], size), lambda step: (0, step + first))],
        )

    def reduce_part():
        part_by_rows(r.hidden_turned, lambda: r.low[...], r.part_reduce, 512)

    def feed_hidden():
        def body(weight, slope):
            columns = tile_rows(pl.program_id(0), 512)
            back = dot_rows(r.low[...], weight[...]) * slope[...].astype(plain)
            down = back.astype(jnp.bfloat16)
            r.broad[:, columns] = down

        run_tiles(
            body,
            r.broad.shape[1] // 512,
            [by_rows(r.whole_reduce, 512), by_columns(r.gelu_slope, 512)],
            [],
        )
        for unit in range(4):
            piece = r.broad[:, unit * width : (unit + 1) * width].astype(plain)
            add_row(r.row_sums, ROW.expand + unit, piece)

    def expand_part():
        part_by_columns(r.feed_turned, r.broad, r.part_expand, 512)

    def back_through(weight, block, place, source, target):
        def body(rows):
            columns = tile_rows(pl.program_id(0), third)
            target(columns, dot_rows(source(), rows[...]))

        run_tiles(body, 3, [(weight, (third, block), lambda step: (step, place))], [])

    def set_wide(columns, value):
        r.wide[:, columns] = value

    def add_running(columns, value):
        r.running[:, columns] += value

    def set_broad(columns, value):
        r.broad[:, columns] = value.astype(jnp.bfloat16)

    def back_three(weight):
        def body(*blocks):
            columns = tile_rows(pl.program_id(0), third)
            total = dot_rows(r.broad[:, 0:width], blocks[0][...])
            for place in (1, 2):
                total += dot_rows(
                    r.broad[:, place * width : (place + 1) * width], blocks[place][...]
                )
            r.wide[:, columns] = total

        block = lambda place: (weight, (third, width), lambda step: (step, place))
        run_tiles(body, 3, [block(0), block(1), block(2)], [])

    def feed_normed():
        back_through(r.whole_expand, 4 * width, 0, lambda: r.broad[...], set_wide)

    def norm_back(rows, normal, rate, shift_row, scale_row):
        back = r.wide[rows, :]
        normal = normal.astype(plain)
        add_row(r.row_sums, shift_row, back)
        add_row(r.row_sums, scale_row, back * normal)
        back = back * (1.0 + r.mods[scale_row : scale_row + 1, :])
        mean = jnp.mean(back, axis=1, keepdims=True)
        inner = jnp.mean(back * normal, axis=1, keepdims=True)
        return (back - mean - normal * inner) * rate[rows, 0:1]

    def feed_last():
        def body(normal):
            rows = tile_rows(pl.program_id(0), ROW_TILE)
            total = r.running[rows, :] + norm_back(rows, normal[...], r.feed_rate, 3, 4)
            r.running[rows, :] = total
            down = total.astype(jnp.bfloat16)
            r.low[rows, :] = down
            add_row(r.row_sums, ROW.cross, down.astype(plain))

        run_tiles(body, r.low.shape[0] // ROW_TILE, [by_rows(r.feed_normal, ROW_TILE)], [])

    def cross_part():
        part_by_rows(r.cross_turned, lambda: r.low[...], r.part_text.at[:, pl.ds(0, 4 * width)], third, 3)

    def cross_given():
        back_through(r.whole_text, width, 3, lambda: r.low[...], set_broad)
        split_heads(r.broad, 0, r.head_in, head_size, HEADS)

    def cross_attention():
        attention_back(
            att_scale,
            r.cross_queries,
            r.cross_keys,
            r.cross_values,
            r.text_mask,
            r.cross_logsum,
            r.head_in,
            (r.head_query, r.cross_key, r.cross_value),
        )
        merge_heads(r.head_query, r.broad, 0, head_size, HEADS)
        merge_heads(r.cross_key, r.memory, 0, head_size, HEADS)
        merge_heads(r.cross_value, r.memory, width, head_size, HEADS)

    def query_part():
        part_by_rows(r.after_turned, lambda: r.broad[:, 0:width], r.part_text.at[:, pl.ds(0, 4 * width)], third, 0)

    def memory_part():
        for place in range(2):
            part_by_rows(
                r.context_turned,
                lambda: r.memory[:, place * width : (place + 1) * width],
                r.part_text.at[:, pl.ds(0, 4 * width)],
                third,
                place + 1,
            )

    def context_back():
        def body(keys, values, out):
            back = dot_rows(r.memory[:, 0:width], keys[...])
            back = back + dot_rows(r.memory[:, width : 2 * width], values[...])
            out[...] = back.astype(jnp.bfloat16)

        run_tiles(
            body,
            3,
            [
                (r.whole_text, (third, width), lambda step: (step, 1)),
                (r.whole_text, (third, width), lambda step: (step, 2)),
            ],
            [by_columns(r.back_context, third)],
        )

    def query_back():
        back_through(r.whole_text, width, 0, lambda: r.broad[:, 0:width], add_running)

    def spatial_first():
        def body(branch):
            rows = tile_rows(pl.program_id(0), ROW_TILE)
            total = r.running[rows, :]
            add_row(r.row_sums, ROW.gate_a, total * branch[...].astype(plain))
            down = (total * r.mods[2:3, :]).astype(jnp.bfloat16)
            r.low[rows, :] = down
            add_row(r.row_sums, ROW.spatial, down.astype(plain))

        run_tiles(body, r.low.shape[0] // ROW_TILE, [by_rows(r.branch_attend, ROW_TILE)], [])

    def output_part():
        def body(left, out):
            out[:, 0:width] = dot_plain(left[...], r.low[...]).astype(jnp.bfloat16)
            out[:, width:] = jnp.zeros_like(out[:, width:])

        run_tiles(
            body,
            3,
            [by_rows(r.spatial_turned, third)],
            [(r.part_text, (third, width + third), lambda step: (step, 3))],
        )

    def spatial_given():
        back_through(r.whole_spatial, width, 3, lambda: r.low[...], set_broad)
        split_heads(r.broad, 0, r.head_in, head_size, HEADS)

    def spatial_attention():
        attention_back(
            att_scale,
            r.queries,
            r.keys,
            r.values,
            None,
            r.spatial_logsum,
            r.head_in,
            (r.head_query, r.head_key, r.head_value),
        )
        merge_heads(r.head_query, r.broad, 0, head_size, HEADS)
        merge_heads(r.head_key, r.broad, width, head_size, HEADS)
        merge_heads(r.head_value, r.broad, 2 * width, head_size, HEADS)

    def input_part(first=0, count=7):
        part_by_columns(r.attend_turned, r.broad, r.part_input, 512, first, count)

    def attend_normed():
        back_three(r.whole_spatial)

    def attend_last():
        def body(normal, out):
            rows = tile_rows(pl.program_id(0), ROW_TILE)
            total = r.running[rows, :] + norm_back(rows, normal[...], r.attend_rate, 0, 1)
            out[...] = total.astype(jnp.bfloat16)

        run_tiles(
            body,
            r.low.shape[0] // ROW_TILE,
            [by_rows(r.attend_normal, ROW_TILE)],
            [by_rows(r.tokens_out, ROW_TILE)],
        )

    tile = r.low.shape[0] // 4
    quads = [pl.ds(index * tile, tile) for index in range(4)]

    def by_blocks(ref):
        return (ref, (1,) + ref.shape[1:], lambda step: (step, 0, 0, 0))

    def turn(source, target):
        def step(index, carry):
            rows = tile_rows(index, tile)
            target[:, rows] = source[rows, :].astype(plain).T.astype(jnp.bfloat16)
            return carry

        lax.fori_loop(0, 4, step, 0)

    def time_first():
        def body(cols):
            rows = tile_rows(pl.program_id(0), tile)
            values = cols[...].reshape(tile, width).astype(plain)
            values = values - jnp.mean(values, axis=1, keepdims=True)
            rate = lax.rsqrt(jnp.mean(values * values, axis=1, keepdims=True) + eps_norm)
            normal = values * rate
            r.time_normal[rows, :] = normal.astype(jnp.bfloat16)
            r.time_rate[rows, :] = jnp.broadcast_to(rate, (tile, LANES))
            r.low[rows, :] = (normal * r.vectors[0:1, :] + r.vectors[1:2, :]).astype(jnp.bfloat16)

        run_tiles(body, 4, [by_blocks(r.time_cols)], [])
        turn(r.low, r.time_turned)

    def time_heads():
        def body(weight):
            columns = tile_rows(pl.program_id(0), third)
            r.broad[:, columns] = dot_plain(r.low[...], weight[...]).astype(jnp.bfloat16)

        run_tiles(body, 9, [by_columns(r.whole_time, third)], [])
        for place, heads in enumerate((r.head_query, r.head_key, r.head_value)):
            split_heads(r.broad, place * width, heads, head_size, HEADS)

    def time_attention():
        def step(pair, carry):
            spots = [(pair * 2 + index, rows) for index in range(2) for rows in quads]
            keys = [r.head_key[spot] for spot in spots]
            values = [r.head_value[spot] for spot in spots]
            scores = [
                dot_rows(key, r.head_query[spot]) * att_scale + r.time_mask[...]
                for key, spot in zip(keys, spots)
            ]
            largest = [jnp.max(score, axis=0, keepdims=True) for score in scores]
            logsums = [
                top + jnp.log(jnp.sum(jnp.exp(score - top), axis=0, keepdims=True))
                for score, top in zip(scores, largest)
            ]
            weights = [
                jnp.exp(score - logs).astype(jnp.bfloat16) for score, logs in zip(scores, logsums)
            ]
            turned = [
                lax.dot_general(
                    value, weight, (((0,), (0,)), ((), ())), preferred_element_type=plain
                )
                for value, weight in zip(values, weights)
            ]
            turned = [value.T.astype(jnp.bfloat16) for value in turned]
            for (head, rows), logs, value in zip(spots, logsums, turned):
                r.time_logsum[head, 0:1, rows] = logs
                r.head_in[head, rows, :] = value
            return carry

        lax.fori_loop(0, HEADS // 2, step, 0)
        merge_heads(r.head_in, r.middle, 0, head_size, HEADS)
        turn(r.middle, r.middle_turned)

    def time_result():
        def body(weight, out):
            columns = tile_rows(pl.program_id(0), third)
            value = dot_plain(r.middle[...], weight[...]) + r.vectors[2:3, columns]
            out[...] = value.astype(jnp.bfloat16).reshape(out.shape)

        shape = r.time_result.shape
        run_tiles(
            body,
            3,
            [(r.whole_time, (width, third), lambda step: (0, 9 + step))],
            [(r.time_result, shape[:3] + (third,), lambda step: (0, 0, 0, step))],
        )

    def time_given():
        def body(cols):
            rows = tile_rows(pl.program_id(0), tile)
            values = cols[...].reshape(tile, width).astype(plain)
            down = (values * (r.time_keep[rows, 0:1] * r.vectors[3:4, :])).astype(jnp.bfloat16)
            r.low[rows, :] = down
            add_row(r.row_sums, ROW.temporal, down.astype(plain))

        run_tiles(body, 4, [by_blocks(r.cot_cols)], [])
        back_through(r.whole_time, width, 3, lambda: r.low[...], set_broad)
        split_heads(r.broad, 0, r.head_in, head_size, HEADS)

    def time_out_part():
        def body(out):
            rows = tile_rows(pl.program_id(0), third)
            out[...] = dot_plain(r.middle_turned[rows, :], r.low[...]).astype(jnp.bfloat16)

        run_tiles(body, 3, [], [(r.part_time, (third, width), lambda step: (step, 3))])

    def time_attention_back():
        def step(pair, carry):
            spots = [(pair * 2 + index, rows) for index in range(2) for rows in quads]
            queries = [r.head_query[spot] for spot in spots]
            keys = [r.head_key[spot] for spot in spots]
            values = [r.head_value[spot] for spot in spots]
            givens = [r.head_in[spot] for spot in spots]
            weights = [
                jnp.exp(
                    dot_rows(key, query) * att_scale
                    + r.time_mask[...]
                    - r.time_logsum[head, 0:1, rows]
                )
                for key, query, (head, rows) in zip(keys, queries, spots)
            ]
            backs = [dot_rows(value, given) for value, given in zip(values, givens)]
            inner = [
                jnp.sum(back * weight, axis=0, keepdims=True)
                for back, weight in zip(backs, weights)
            ]
            backs = [
                (weight * (back - total)).astype(jnp.bfloat16)
                for weight, back, total in zip(weights, backs, inner)
            ]
            back_values = [
                dot_plain(weight.astype(jnp.bfloat16), given).astype(jnp.bfloat16)
                for weight, given in zip(weights, givens)
            ]
            back_keys = [
                (dot_plain(back, query) * att_scale).astype(jnp.bfloat16)
                for back, query in zip(backs, queries)
            ]
            turned = [
                lax.dot_general(key, back, (((0,), (0,)), ((), ())), preferred_element_type=plain)
                for key, back in zip(keys, backs)
            ]
            turned = [(value * att_scale).T.astype(jnp.bfloat16) for value in turned]
            for (head, rows), *outs in zip(spots, turned, back_keys, back_values):
                r.head_query[head, rows, :] = outs[0]
                r.head_key[head, rows, :] = outs[1]
                r.head_value[head, rows, :] = outs[2]
            return carry

        lax.fori_loop(0, HEADS // 2, step, 0)
        for place, heads in enumerate((r.head_query, r.head_key, r.head_value)):
            merge_heads(heads, r.broad, place * width, head_size, HEADS)

    def time_normed():
        back_three(r.whole_time)

    def time_last():
        def body(out):
            rows = tile_rows(pl.program_id(0), tile)
            back = r.wide[rows, :]
            normal = r.time_normal[rows, :].astype(plain)
            add_row(r.row_sums, ROW.shift, back)
            add_row(r.row_sums, ROW.gain, back * normal)
            back = back * r.vectors[0:1, :]
            mean = jnp.mean(back, axis=1, keepdims=True)
            inner = jnp.mean(back * normal, axis=1, keepdims=True)
            back = (back - mean - normal * inner) * r.time_rate[rows, 0:1]
            out[...] = back.astype(jnp.bfloat16).reshape(out.shape)

        run_tiles(body, 4, [], [by_blocks(r.time_back)])

    def time_in_part():
        def body(out):
            columns = tile_rows(pl.program_id(0), third)
            out[...] = dot_plain(r.time_turned[...], r.broad[:, columns]).astype(jnp.bfloat16)

        run_tiles(body, 9, [], [by_columns(r.part_time, third)])

    def block_last():
        def body(after, result, cot, out):
            value = result[...].reshape(cot.shape).astype(plain)
            add_row(r.row_sums, ROW.gate_t, cot[...].astype(plain) * value * r.vectors[5:6, :])
            out[...] = (after[...] + r.vectors[4:5, :] * value).astype(jnp.bfloat16)

        ins = [by_rows(ref, ROW_TILE) for ref in (r.after_feed, r.returned, r.cotangent)]
        run_tiles(body, r.low.shape[0] // ROW_TILE, ins, [by_rows(r.block_out, ROW_TILE)])

    return types.SimpleNamespace(**locals())


def back_kernel(together, att_scale, names, *refs):
    r = types.SimpleNamespace(**dict(zip(names, refs)))
    if together:
        r.back_sent, r.returned = r.back_sent_cols, r.returned_cols
    do = back_stages(r, att_scale)
    if not together:
        do.clear()
        do.feed_first()
        do.reduce_part()
        do.feed_hidden()
        do.expand_part()
        do.feed_normed()
        do.feed_last()
        do.cross_part()
        do.cross_given()
        do.cross_attention()
        do.query_part()
        do.memory_part()
        do.context_back()
        do.query_back()
        do.spatial_first()
        do.output_part()
        do.spatial_given()
        do.spatial_attention()
        do.input_part()
        do.attend_normed()
        do.attend_last()
        return
    column, frame, depth, core, across_x, across_y, sibling = neighbours()
    far = 3 - column
    frame_peers = [(column, (frame + shift) % 8) for shift in range(1, 8)]
    line_peers = [(column, ((depth + shift) % 4) * 2 + core) for shift in range(1, 4)]
    plane_peers = [(across_x, frame), (across_y, frame), (far, frame)]
    greet(frame_peers + plane_peers)
    copies = Copies(r.send_sems, r.recv_sems)
    talls, bundles = PART_TALLS, len(PART_TALLS)
    cut = lambda ref, *span: ref.at[:, pl.ds(*span)]
    parts = [
        r.part_time,
        r.part_reduce,
        cut(r.part_expand, 0, 3584),
        cut(r.part_expand, 3584, 1024),
        r.part_text,
        cut(r.part_input, 0, 2048),
        cut(r.part_input, 2048, 1536),
    ]
    many = lambda name: [vars(r)[f"{name}_{index}"] for index in range(bundles)]
    paired, halved, quartered, lined = (many(name) for name in LANDING)
    summed, crossed = halved, quartered
    outs = [
        r.share_time,
        r.share_reduce,
        cut(r.share_expand, 0, 3584),
        cut(r.share_expand, 3584, 1024),
        r.share_text,
        cut(r.share_input, 0, 2048),
        cut(r.share_input, 2048, 1536),
    ]

    def part_piece(index, unit, owner):
        return whole_unit(parts[index], talls[index], unit, owner)

    from_core = {}

    def send(index, units=range(4)):
        for slot in range(4):
            owner = slot * 2 + 1 - core
            for unit in units:
                from_core[index, slot, unit] = copies.start(
                    part_piece(index, unit, owner), paired[index].at[unit, slot], (column, sibling)
                )

    def stream(index, count, left_at, right_at, out_at):
        wide = pl.ds(0, paired[index].shape[-1])
        buffers = [ref.at[:, :, wide] for ref in (r.left_buf, r.right_buf, r.out_buf)]
        add_stream(count, left_at, right_at, out_at, *buffers, r.stream_sems)

    from_half, from_quarter, from_line, ends = {}, {}, {}, []

    def pair(index):
        for slot in range(4):
            for unit in range(4):
                from_core[index, slot, unit].wait_recv()
        place = lambda step: paired[index].at[step // 4, step % 4]
        stream(
            index, 16, lambda step: part_piece(index, step // 4, (step % 4) * 2 + core), place, place
        )
        if index == LINE_FIRST:
            for shift in range(1, 4):
                other = (depth + shift) % 4
                for unit in range(4):
                    from_line[index, shift, unit] = copies.start(
                        paired[index].at[unit, other],
                        lined[index].at[shift - 1, unit],
                        (column, other * 2 + core),
                    )
            return
        for slot in range(4):
            near = across_x if slot < 2 else across_y
            for which, unit in enumerate((near, far)):
                from_half[index, slot, which] = copies.start(
                    paired[index].at[unit, slot], halved[index].at[slot, which], (near, frame)
                )

    def half(index):
        for slot in range(4):
            for which in range(2):
                from_half[index, slot, which].wait_recv()

        def source(step):
            slot, which = step // 2, step % 2
            late = slot // 2
            unit = column + which * (
                (1 - late) * (across_y - column) + late * (across_x - column)
            )
            return paired[index].at[unit, slot]

        place = lambda step: halved[index].at[step // 2, step % 2]
        stream(index, 8, source, place, place)
        for slot in range(4):
            near = across_y if slot < 2 else across_x
            from_quarter[index, slot] = copies.start(
                halved[index].at[slot, 1], quartered[index].at[slot], (near, frame)
            )

    def quarter(index):
        for slot in range(4):
            from_quarter[index, slot].wait_recv()
        place = lambda slot: quartered[index].at[slot]
        stream(index, 4, lambda slot: halved[index].at[slot, 0], place, place)
        for shift in range(1, 4):
            other = (depth + shift) % 4
            from_line[index, shift] = copies.start(
                quartered[index].at[other], lined[index].at[shift - 1], (column, other * 2 + core)
            )

    def total_of_four(own, others, target, height, width):
        loads = [
            pltpu.make_async_copy(
                source,
                r.four_buf.at[slot, pl.ds(0, height), pl.ds(0, width)],
                r.stream_sems.at[0, slot],
            )
            for slot, source in enumerate([own] + others)
        ]
        for copy in loads:
            copy.start()
        for copy in loads:
            copy.wait()
        total = r.four_buf[0, 0:height, 0:width].astype(jnp.float32)
        for slot in range(1, 4):
            total = total + r.four_buf[slot, 0:height, 0:width].astype(jnp.float32)
        r.out_buf[0, 0:height, 0:width] = total.astype(jnp.bfloat16)
        copy = pltpu.make_async_copy(
            r.out_buf.at[0, pl.ds(0, height), pl.ds(0, width)], target, r.stream_sems.at[2, 0]
        )
        copy.start()
        copy.wait()

    spread, relayed = {}, []

    def hand_out(index):
        target = share_unit(outs[index], talls[index], column)
        spread[index] = [copies.start(target, target, peer) for peer in plane_peers[:2]]
        if index >= bundles - 2:
            ends.extend(spread[index])
            ends.append(copies.start(target, target, plane_peers[2]))

    def relay(index):
        x_first = index % 2 == 0
        first, second = spread[index] if x_first else spread[index][::-1]
        first.wait_recv()
        target = share_unit(outs[index], talls[index], across_x if x_first else across_y)
        ends.append(copies.start(target, target, plane_peers[1 if x_first else 0]))
        ends.append(second)

    def line_sums():
        index = LINE_FIRST
        for shift in range(1, 4):
            for unit in range(4):
                from_line[index, shift, unit].wait_recv()
        for unit in range(4):
            total_of_four(
                paired[index].at[unit, depth],
                [lined[index].at[slot, unit] for slot in range(3)],
                summed[index].at[unit],
                *paired[index].shape[2:],
            )
        for slot, peer in enumerate(plane_peers):
            from_half[index, slot] = copies.start(
                summed[index].at[peer[0]], crossed[index].at[slot], peer
            )

    def line_last():
        index = LINE_FIRST
        for slot in range(3):
            from_half[index, slot].wait_recv()
        total_of_four(
            summed[index].at[column],
            [crossed[index].at[slot] for slot in range(3)],
            share_unit(outs[index], talls[index], column),
            *paired[index].shape[2:],
        )
        hand_out(index)

    def line(index):
        for shift in range(1, 4):
            from_line[index, shift].wait_recv()
        total_of_four(
            quartered[index].at[depth],
            [lined[index].at[slot] for slot in range(3)],
            share_unit(outs[index], talls[index], column),
            *lined[index].shape[1:],
        )
        hand_out(index)

    contexts, paired_contexts, texts = [], [], []
    text_rows = r.text_part.shape[0] // 4

    def context_send():
        contexts.extend(
            copies.start(r.back_context, r.context_all.at[frame], peer) for peer in line_peers
        )
        paired_contexts.append(
            copies.start(r.back_context, r.context_all.at[frame], (column, sibling))
        )
        move(r.back_context, r.held_context, r.context_all.at[frame])

    def context_pair():
        for shift, copy in zip(range(1, 4), contexts):
            copy.wait_recv()
            place = r.context_all.at[((depth + 4 - shift) % 4) * 2 + core]
            paired_contexts.append(copies.start(place, place, (column, sibling)))

    def text_part():
        for copy in paired_contexts:
            copy.wait_recv()
        each = r.context_all.shape[1]

        def body(text, context, out):
            total = dot_plain(text[:, 0:each], context[0])
            for index in range(1, 8):
                total = total + dot_plain(text[:, index * each : (index + 1) * each], context[index])
            out[...] = total.astype(jnp.bfloat16)

        run_tiles(
            body,
            4,
            [
                by_rows(r.text_turned, text_rows),
                (r.context_all, r.context_all.shape, lambda step: (0, 0, 0)),
            ],
            [by_rows(r.text_part, text_rows)],
        )
        for slot, peer in enumerate(plane_peers):
            texts.append(
                copies.start(
                    rows_at(r.text_part, peer[0] * text_rows, text_rows, text_rows),
                    r.text_got.at[slot],
                    peer,
                )
            )

    def text_line():
        for copy in texts:
            copy.wait_recv()
        total_of_four(
            rows_at(r.text_part, column * text_rows, text_rows, text_rows),
            [r.text_got.at[slot] for slot in range(3)],
            rows_at(r.text_out, column * text_rows, text_rows, text_rows),
            *r.text_got.shape[1:],
        )
        target = rows_at(r.text_out, column * text_rows, text_rows, text_rows)
        for peer in plane_peers:
            ends.append(copies.start(target, target, peer))

    cots_got, back_got, result_got, rows_got, rows_paired = [], [], [], [], []
    here = r.local_sems

    def move(source, held, target):
        load = pltpu.make_async_copy(source, held, here.at[0])
        load.start()
        load.wait()
        store = pltpu.make_async_copy(held, target, here.at[0])
        store.start()
        store.wait()

    def cols_send(source, target, got):
        for peer in frame_peers:
            got.append(copies.start(source.at[peer[1]], target.at[:, frame], peer))
        move(source.at[frame], r.held_cols, target.at[:, frame])

    def return_send(source, target, got):
        for peer in frame_peers:
            got.append(copies.start(source.at[:, peer[1]], target.at[frame], peer))
        move(source.at[:, frame], r.held_cols, target.at[frame])

    def arrive(got):
        for copy in got:
            copy.wait_recv()

    def rows_send():
        for peer in line_peers:
            rows_got.append(copies.start(r.row_sums, r.rows_all.at[frame], peer))
        rows_paired.append(copies.start(r.row_sums, r.rows_all.at[frame], (column, sibling)))
        r.rows_all[frame] = r.row_sums[...]

    def rows_pair():
        for shift, copy in zip(range(1, 4), rows_got):
            copy.wait_recv()
            place = r.rows_all.at[((depth + 4 - shift) % 4) * 2 + core]
            rows_paired.append(copies.start(place, place, (column, sibling)))

    def rows_plane():
        arrive(rows_paired)
        mods = r.rows_all.at[:, pl.ds(0, 8)]
        own = [pltpu.make_async_copy(mods, r.mods_out.at[column], here.at[0])]
        for peer in plane_peers:
            ends.append(copies.start(mods, r.mods_out.at[column], peer))
        r.sums[...] = jnp.sum(r.rows_all[:, 8:, :], axis=0)
        own.append(pltpu.make_async_copy(r.sums, r.sums_out.at[column], here.at[1]))
        for copy in own:
            copy.start()
        for peer in plane_peers:
            ends.append(copies.start(r.sums, r.sums_out.at[column], peer))
        for copy in own:
            copy.wait()

    cols_send(r.cot_rows, r.cot_cols, cots_got)
    do.clear()
    r.row_sums[ROW.condition : ROW.condition + 1, :] = r.vectors[6:7, :]
    do.time_first()
    do.time_heads()
    do.time_attention()
    arrive(cots_got)
    do.time_given()
    do.time_attention_back()
    do.time_normed()
    do.time_last()
    return_send(r.time_back, r.back_sent_cols, back_got)
    do.time_in_part()
    do.time_out_part()
    send(0)
    do.time_result()
    arrive(back_got)
    return_send(r.time_result, r.returned_cols, result_got)
    do.feed_first()
    pair(0)
    do.reduce_part()
    send(1)
    do.feed_hidden()
    pair(1)
    half(0)
    do.expand_part()
    send(2)
    send(3)
    do.feed_normed()
    pair(2)
    pair(3)
    do.feed_last()
    half(1)
    do.cross_part()
    do.cross_given()
    quarter(0)
    arrive(result_got)
    do.block_last()
    do.cross_attention()
    half(2)
    line_sums()
    line(0)
    quarter(1)
    do.query_part()
    do.memory_part()
    do.context_back()
    context_send()
    do.query_back()
    do.spatial_first()
    do.output_part()
    send(4)
    relay(0)
    line(1)
    line_last()
    quarter(2)
    do.spatial_given()
    pair(4)
    do.spatial_attention()
    context_pair()
    relay(1)
    line(2)
    half(4)
    do.input_part(0, 4)
    send(5)
    do.input_part(4, 3)
    send(6)
    text_part()
    relay(3)
    quarter(4)
    pair(5)
    pair(6)
    do.attend_normed()
    do.attend_last()
    rows_send()
    relay(2)
    half(5)
    half(6)
    rows_pair()
    text_line()
    line(4)
    quarter(5)
    quarter(6)
    rows_plane()
    relay(4)
    line(5)
    line(6)
    for copy in ends:
        copy.wait_recv()
    copies.finish()


LANDING = ("paired", "halved", "quartered", "lined")
PART_TALLS = (False, True, False, False, False, False, False)
LINE_FIRST = 3


def backward(att_scale, together, o, text_turned):
    anywhere = pl.BlockSpec(memory_space=pl.ANY)
    inside = pl.BlockSpec(memory_space=pltpu.VMEM)
    tokens, width = o.cotangent.shape
    hidden = o.gelu_slope.shape[1]
    text_count = o.cross_keys.shape[1]
    low, full = jnp.bfloat16, jnp.float32
    shape = jax.ShapeDtypeStruct
    third = width // 3
    hbm_out = dict(
        part_reduce=shape((hidden, width), low),
        part_expand=shape((width, hidden), low),
        part_text=shape((width, 5 * width + third), low),
        part_input=shape((width, 3 * width + LANES), low),
        back_context=shape((text_count, width), low),
        tokens_out=shape((tokens, width), low),
    )
    scratch = dict(
        running=pltpu.VMEM((tokens, width), full),
        wide=pltpu.VMEM((tokens, width), full),
        low=pltpu.VMEM((tokens, width), low),
        broad=pltpu.VMEM((tokens, hidden), low),
        head_in=pltpu.VMEM((HEADS, tokens, HEAD_LANES), low),
        head_query=pltpu.VMEM((HEADS, tokens, HEAD_LANES), low),
        head_key=pltpu.VMEM((HEADS, tokens, HEAD_LANES), low),
        head_value=pltpu.VMEM((HEADS, tokens, HEAD_LANES), low),
        cross_key=pltpu.VMEM((HEADS, text_count, HEAD_LANES), low),
        cross_value=pltpu.VMEM((HEADS, text_count, HEAD_LANES), low),
        memory=pltpu.VMEM((text_count, 2 * width), low),
    )
    hbm_in = dict(
        whole_spatial=o.whole_spatial,
        whole_text=o.whole_text,
        whole_expand=o.whole_expand,
        whole_reduce=o.whole_reduce,
        cotangent=o.cotangent,
        branch_feed=o.branch_feed,
        hidden_turned=o.hidden_turned,
        gelu_slope=o.gelu_slope,
        feed_turned=o.feed_turned,
        feed_normal=o.feed_normal,
        cross_turned=o.cross_turned,
        cross_queries=o.cross_queries,
        cross_keys=o.cross_keys,
        cross_values=o.cross_values,
        after_turned=o.after_turned,
        context_turned=o.context_turned,
        branch_attend=o.branch_attend,
        spatial_turned=o.spatial_turned,
        queries=o.queries,
        keys=o.keys,
        values=o.values,
        attend_turned=o.attend_turned,
        attend_normal=o.attend_normal,
    )
    vmem_in = dict(
        mods=o.mods,
        feed_rate=o.feed_rate,
        attend_rate=o.attend_rate,
        cross_logsum=o.cross_logsum,
        spatial_logsum=o.spatial_logsum,
        text_mask=o.text_mask,
    )
    if not together:
        hbm_in.update(back_sent=o.back_sent)
    vmem_out = dict(row_sums=shape((ROW.high, width), full))
    if together:
        hbm_in.update(
            time_cols=o.time_cols,
            cot_rows=o.cot_rows,
            whole_time=o.whole_time,
            after_feed=o.after_feed,
            text_turned=text_turned,
        )
        vmem_in.update(vectors=o.vectors, time_keep=o.time_keep, time_mask=o.time_mask)
        rows = o.cot_rows.shape
        cols = (rows[1], rows[0]) + rows[2:]
        hbm_out.update(cot_cols=shape(cols, low))
        hbm_out.update(part_time=shape((width, 4 * width), low))
        hbm_out.update(time_result=shape(cols, low))
        hbm_out.update(time_back=shape(cols, low))
        hbm_out.update(back_sent_cols=shape(rows, low))
        hbm_out.update(returned_cols=shape(rows, low))
        hbm_out.update(block_out=shape((tokens, width), low))
        hbm_out.update(mods_out=shape((4, 8, 8, width), full))
        hbm_out.update(sums_out=shape((4, ROW.high - 8, width), full))
        high = width // 8
        wides = (width, width, 896, 256, width + third, 512, 384)
        high = width // 8
        for index, wide in enumerate(wides):
            piece = (high, wide)
            first = index == LINE_FIRST
            landing = [(4, 4), (4,) if first else (4, 2), (4,), (3, 4) if first else (3,)]
            for name, lead in zip(LANDING, landing):
                hbm_out[f"{name}_{index}"] = shape(lead + piece, low)
        hbm_out.update(
            share_time=shape((high, 4 * width), low),
            share_reduce=shape((4 * high, width), low),
            share_expand=shape((high, 4 * width), low),
            share_text=shape((high, 5 * width + third), low),
            share_input=shape((high, 3 * width + LANES), low),
        )
        text_shape = (text_turned.shape[0], width)
        hbm_out.update(context_all=shape((8, text_count, width), low))
        hbm_out.update(text_part=shape(text_shape, low))
        hbm_out.update(text_got=shape((3, text_shape[0] // 4, width), low))
        hbm_out.update(text_out=shape(text_shape, low))
        remote = len(PART_TALLS) * (16 + 8 + 4 + 3 + 3) + 7 + 3 + 3 + 4 * 7 + 6
        piece = (high, width + third)
        scratch.update(
            send_sems=pltpu.SemaphoreType.DMA((remote,)),
            recv_sems=pltpu.SemaphoreType.DMA((remote,)),
            stream_sems=pltpu.SemaphoreType.DMA((3, PIECE_SLOTS)),
            local_sems=pltpu.SemaphoreType.DMA((2,)),
            left_buf=pltpu.VMEM((PIECE_SLOTS,) + piece, low),
            right_buf=pltpu.VMEM((PIECE_SLOTS,) + piece, low),
            out_buf=pltpu.VMEM((PIECE_SLOTS,) + piece, low),
            four_buf=pltpu.VMEM((4,) + piece, low),
            rows_all=pltpu.VMEM((8, ROW.high, width), full),
            sums=pltpu.VMEM((ROW.high - 8, width), full),
            time_normal=pltpu.VMEM((tokens, width), low),
            time_rate=pltpu.VMEM((tokens, LANES), full),
            time_turned=pltpu.VMEM((width, tokens), low),
            time_logsum=pltpu.VMEM((HEADS, 8, tokens), full),
            held_cols=pltpu.VMEM((cols[0],) + cols[2:], low),
            held_context=pltpu.VMEM((text_count, width), low),
            middle=pltpu.VMEM((tokens, width), low),
            middle_turned=pltpu.VMEM((width, tokens), low),
        )
    names = list(hbm_in) + list(vmem_in) + list(hbm_out) + list(vmem_out) + list(scratch)
    results = pl.pallas_call(
        functools.partial(back_kernel, together, att_scale, names),
        out_shape=list(hbm_out.values()) + list(vmem_out.values()),
        in_specs=[anywhere] * len(hbm_in) + [inside] * len(vmem_in),
        out_specs=[anywhere] * len(hbm_out) + [inside] * len(vmem_out),
        scratch_shapes=list(scratch.values()),
        compiler_params=pltpu.CompilerParams(
            collective_id=1 if together else None,
            has_side_effects=True,
            vmem_limit_bytes=60 * 1024 * 1024,
        ),
        name="backward",
    )(*hbm_in.values(), *vmem_in.values())
    return types.SimpleNamespace(**dict(zip(list(hbm_out) + list(vmem_out), results)))


def one_slice():
    return lax.axis_size("clip") == 4 and lax.axis_size("frame") == 8


def sum_shares(group):
    def total(part):
        return lax.psum(lax.psum_scatter(part, "frame", scatter_dimension=0, tiled=True), "clip")

    return jnp.concatenate([total(part) for part in group], axis=1)


FORWARD_TALLS = (False, True, False, False, True, False)
VEC = types.SimpleNamespace(
    spatial=0, cross=1, reduce=2, gain=3, shift=4, temporal=5, gate=6, expand=7, high=16
)


def forward_stages(r, att_scale):
    tokens, width = r.low.shape
    head_size = width // HEADS
    third = width // 3
    tile = tokens // 4
    plain = jnp.float32
    row = lambda which: r.rows_low[which : which + 1, :]

    def clear():
        for heads in (r.head_query, r.head_key, r.head_value, r.cross_key, r.cross_value):
            heads[...] = jnp.zeros_like(heads)

    def sum_mods():
        r.mods[...] = jnp.sum(r.mods_got[...], axis=0)

    def sum_rows():
        r.rows_low[...] = jnp.sum(r.rows_got[...].astype(plain), axis=0)
        for unit in range(4):
            r.rows_expand[0:1, unit * width : (unit + 1) * width] = row(VEC.expand + unit)

    def turn_out(source, target):
        height = source.shape[0] // target.shape[1] * LANES

        def body(out):
            rows = tile_rows(pl.program_id(0), LANES)
            out[...] = source[rows, :].astype(plain).T.astype(jnp.bfloat16)

        run_tiles(body, target.shape[1] // LANES, [], [by_columns(target, LANES)])

    def normed(values, rate_out, rows, shift, scale):
        values = values - jnp.mean(values, axis=1, keepdims=True)
        rate = lax.rsqrt(jnp.mean(values * values, axis=1, keepdims=True) + eps_norm)
        normal = values * rate
        rate_out[rows, :] = jnp.broadcast_to(rate, (tile, LANES))
        shift, scale = (r.mods[which : which + 1, :] for which in (shift, scale))
        r.low[rows, :] = (normal * (1.0 + scale) + shift).astype(jnp.bfloat16)
        return normal.astype(jnp.bfloat16)

    def attend_first():
        def body(latents, out):
            rows = tile_rows(pl.program_id(0), tile)
            values = latents[...].astype(plain)
            out[...] = normed(values, r.attend_rate, rows, ROW.shift_a, ROW.scale_a)

        run_tiles(body, 4, [by_rows(r.latents, tile)], [by_rows(r.attend_normal, tile)])
        turn_out(r.low, r.attend_turned)

    def through(weight, place, count, left, target, size=third):
        def body(block):
            columns = tile_rows(pl.program_id(0), size)
            target(columns, dot_plain(left(), block[...]))

        high = weight.shape[0]
        run_tiles(body, count, [(weight, (high, size), lambda step: (0, place + step))], [])

    def set_broad(columns, value):
        r.broad[:, columns] = value.astype(jnp.bfloat16)

    def set_memory(columns, value):
        r.memory[:, columns] = value.astype(jnp.bfloat16)

    def attend_heads():
        through(r.whole_spatial, 0, 9, lambda: r.low[...], set_broad)
        for place, heads in enumerate((r.head_query, r.head_key, r.head_value)):
            split_heads(r.broad, place * width, heads, head_size, HEADS)

    def attention(queries, keys, values, mask, logsum, outs, first=0, last=HEADS):
        def step(head, carry):
            query, key, value = queries[head], keys[head], values[head]
            scores = dot_rows(key, query) * att_scale
            if mask is not None:
                scores = scores + mask[:, 0:1]
            largest = jnp.max(scores, axis=0, keepdims=True)
            total = jnp.sum(jnp.exp(scores - largest), axis=0, keepdims=True)
            logs = largest + jnp.log(total)
            logsum[head, 0:1, :] = logs
            weights = jnp.exp(scores - logs).astype(jnp.bfloat16)
            turned = lax.dot_general(
                value, weights, (((0,), (0,)), ((), ())), preferred_element_type=plain
            )
            outs[head] = turned.T.astype(jnp.bfloat16)
            return carry

        lax.fori_loop(first, last, step, 0)

    def attend_attention(half):
        attention(
            r.head_query,
            r.head_key,
            r.head_value,
            None,
            r.spatial_logsum,
            r.head_out,
            half * HEADS // 2,
            (half + 1) * HEADS // 2,
        )

    def attend_merge():
        merge_heads(r.head_out, r.middle, 0, head_size, HEADS)
        turn_out(r.middle, r.spatial_turned)

    def attend_last():
        def body(weight, latents, branch):
            columns = tile_rows(pl.program_id(0), third)
            value = dot_plain(r.middle[...], weight[...])
            value = value + r.rows_low[VEC.spatial : VEC.spatial + 1, columns]
            branch[...] = value.astype(jnp.bfloat16)
            after = latents[...].astype(plain)
            after = after + r.mods[ROW.gate_a : ROW.gate_a + 1, columns] * value
            r.running[:, columns] = after
            r.low[:, columns] = after.astype(jnp.bfloat16)

        run_tiles(
            body,
            3,
            [
                (r.whole_spatial, (width, third), lambda step: (0, 9 + step)),
                by_columns(r.latents, third),
            ],
            [by_columns(r.branch_attend, third)],
        )
        turn_out(r.low, r.after_turned)

    def context():
        def body(weight):
            columns = tile_rows(pl.program_id(0), third)
            r.context[:, columns] = dot_plain(r.own_text[...], weight[...]).astype(jnp.bfloat16)

        run_tiles(body, 3, [by_columns(r.whole_context, third)], [])
        turn_out(r.context, r.context_turned)

    def cross_heads():
        through(r.whole_text, 3, 6, lambda: r.context[...], set_memory)
        split_heads(r.memory, 0, r.cross_key, head_size, HEADS)
        split_heads(r.memory, width, r.cross_value, head_size, HEADS)
        through(r.whole_text, 0, 3, lambda: r.low[...], set_broad)
        split_heads(r.broad, 0, r.cross_query, head_size, HEADS)

    def cross_attention():
        attention(
            r.cross_query, r.cross_key, r.cross_value, r.text_mask, r.cross_logsum, r.head_out
        )
        merge_heads(r.head_out, r.middle, 0, head_size, HEADS)
        turn_out(r.middle, r.cross_turned)

    def add_cross(columns, value):
        r.running[:, columns] += value + r.rows_low[VEC.cross : VEC.cross + 1, columns]

    def cross_last():
        through(r.whole_text, 9, 3, lambda: r.middle[...], add_cross)

    def feed_first():
        def body(out):
            rows = tile_rows(pl.program_id(0), tile)
            out[...] = normed(r.running[rows, :], r.feed_rate, rows, ROW.shift_m, ROW.scale_m)

        run_tiles(body, 4, [], [by_rows(r.feed_normal, tile)])
        turn_out(r.low, r.feed_turned)

    def feed_hidden():
        size = 512

        def body(weight, slope, turned):
            columns = tile_rows(pl.program_id(0), size)
            values = dot_plain(r.low[...], weight[...]) + r.rows_expand[0:1, columns]
            inner = math.sqrt(2.0 / math.pi)
            square = values * values
            bent = jnp.tanh(inner * values * (1.0 + 0.044715 * square))
            half = 0.5 * (1.0 + bent)
            hidden = values * half
            steep = inner * (1.0 + 3.0 * 0.044715 * square)
            slope[...] = (half + 0.5 * values * (1.0 - bent * bent) * steep).astype(jnp.bfloat16)
            r.broad[:, columns] = hidden.astype(jnp.bfloat16)
            turned[...] = hidden.T.astype(jnp.bfloat16)

        run_tiles(
            body,
            r.broad.shape[1] // size,
            [by_columns(r.whole_expand, size)],
            [by_columns(r.gelu_slope, size), by_rows(r.hidden_turned, size)],
        )

    def feed_last():
        def body(weight, branch, after, sent):
            columns = tile_rows(pl.program_id(0), third)
            value = dot_plain(r.broad[...], weight[...])
            value = value + r.rows_low[VEC.reduce : VEC.reduce + 1, columns]
            branch[...] = value.astype(jnp.bfloat16)
            value = r.running[:, columns] + r.mods[ROW.gate_m : ROW.gate_m + 1, columns] * value
            after[...] = value
            sent[...] = value.astype(jnp.bfloat16).reshape(sent.shape)

        shape = r.sent.shape
        run_tiles(
            body,
            3,
            [by_columns(r.whole_reduce, third)],
            [
                by_columns(r.branch_feed, third),
                by_columns(r.after_feed, third),
                (r.sent, shape[:3] + (third,), lambda step: (0, 0, 0, step)),
            ],
        )

    return types.SimpleNamespace(**locals())


def forward_kernel(att_scale, names, *refs):
    r = types.SimpleNamespace(**dict(zip(names, refs)))
    r.held = [
        r.held_spatial, r.held_context, r.held_text, r.held_expand, r.held_reduce, r.held_time
    ]
    do = forward_stages(r, att_scale)
    shares = [
        r.share_spatial, r.share_context, r.share_text, r.share_expand, r.share_reduce, r.share_time
    ]
    wholes = [
        r.whole_spatial, r.whole_context, r.whole_text, r.whole_expand, r.whole_reduce, r.whole_time
    ]
    talls, count = FORWARD_TALLS, len(FORWARD_TALLS)
    column, frame, depth, core, across_x, across_y, sibling = neighbours()
    frame_peers = [(column, (frame + shift) % 8) for shift in range(1, 8)]
    greet(frame_peers + [(across_x, frame), (across_y, frame)])
    copies = Copies(r.send_sems, r.recv_sems)
    locals_started = []

    def local(source, target):
        copy = pltpu.make_async_copy(source, target, r.local_sems.at[len(locals_started)])
        copy.start()
        locals_started.append(copy)
        return copy

    mods, rows, arrivals = [], [], {index: [] for index in range(count)}
    from_x, from_y, from_far, own_place = {}, {}, {}, {}

    def send_mods():
        own = local(r.mod_parts.at[frame], r.mods_got.at[frame])
        for peer in frame_peers:
            mods.append(copies.start(r.mod_parts.at[peer[1]], r.mods_got.at[frame], peer))
        own.wait()

    def send_rows():
        own = local(r.row_parts, r.rows_got.at[frame])
        for peer in frame_peers:
            rows.append(copies.start(r.row_parts, r.rows_got.at[frame], peer))
        own.wait()

    def send(index):
        share, whole, tall = shares[index], wholes[index], talls[index]
        own = whole_share(whole, tall, frame)
        held = r.held[index]
        load = local(share, held)
        arrivals[index].append(copies.start(share, own, (column, sibling)))
        own_place[index] = (load, held, own)

    def place(index):
        load, held, own = own_place[index]
        load.wait()
        own_place[index] = local(held, own)

    order = (
        jnp.where(depth == 0, 3, 1),
        jnp.where((depth == 0) | (depth == 3), 2, 3),
        jnp.where(depth == 0, 1, jnp.where(depth == 3, 3, 2)),
    )

    def next_frame(step):
        return jnp.clip(depth + step, 0, 3) * 2 + core

    def send_depth(index):
        share, whole, tall = shares[index], wholes[index], talls[index]
        source = share_unit(share, tall, column)
        target = whole_unit(whole, tall, column, frame)
        for step, shift in ((1, 1), (-1, 3)):
            copies.start_if(
                (depth < 3) if step == 1 else (depth > 0),
                source,
                target,
                (column, next_frame(step)),
                r.depth_sems.at[index, shift],
            )

    def pass_depth(index, shift):
        source = ((depth + 4 - shift) % 4) * 2 + core
        piece = whole_unit(wholes[index], talls[index], column, source)
        copies.start_if(
            (depth >= shift) & (depth < 3),
            piece,
            piece,
            (column, next_frame(1)),
            r.depth_sems.at[index, (shift + 1) % 4],
        )
        copies.start_if(
            (depth < shift) & (depth > 0),
            piece,
            piece,
            (column, next_frame(-1)),
            r.depth_sems.at[index, shift - 1],
        )

    def wait_depth(index, shift):
        source = ((depth + 4 - shift) % 4) * 2 + core
        piece = whole_unit(wholes[index], talls[index], column, source)
        pltpu.make_async_remote_copy(
            src_ref=piece,
            dst_ref=piece,
            send_sem=r.send_sems.at[0],
            recv_sem=r.depth_sems.at[index, shift],
            device_id=(column, sibling),
            device_id_type=MESH_ID,
        ).wait_recv()

    def pass_on(index, turn, unit, device):
        source = ((depth + 4 - order[turn]) % 4) * 2 + core
        piece = whole_unit(wholes[index], talls[index], unit, source)
        return copies.start(piece, piece, device)

    def first(index, turns=(0, 1, 2)):
        for turn in turns:
            wait_depth(index, order[turn])
            pass_depth(index, order[turn])
            from_x[index, turn] = pass_on(index, turn, column, (across_x, frame))
            from_y[index, turn] = pass_on(index, turn, column, (across_y, frame))
            arrivals[index].append(pass_on(index, turn, column, (column, sibling)))
        if index + 2 < count and turns[-1] == 2:
            send(index + 2)
            send_depth(index + 2)

    def second(index):
        for turn in range(3):
            x_first = (index + turn) % 2 == 0
            from_x[index, turn].wait_recv()
            if x_first:
                from_far[index, turn] = pass_on(index, turn, across_x, (across_y, frame))
            arrivals[index].append(pass_on(index, turn, across_x, (column, sibling)))
            from_y[index, turn].wait_recv()
            if not x_first:
                from_far[index, turn] = pass_on(index, turn, across_y, (across_x, frame))
            arrivals[index].append(pass_on(index, turn, across_y, (column, sibling)))

    def third(index):
        for turn in range(3):
            from_far[index, turn].wait_recv()
            arrivals[index].append(pass_on(index, turn, 3 - column, (column, sibling)))

    def ready(index):
        place(index)
        for copy in arrivals[index]:
            copy.wait_recv()
        own_place[index].wait()

    def arrive(got):
        for copy in got:
            copy.wait_recv()

    send_mods()
    for index in (0, 1):
        send(index)
        send_depth(index)
    do.clear()
    arrive(mods)
    do.sum_mods()
    do.attend_first()
    first(0)
    send_rows()
    second(0)
    first(1)
    third(0)
    ready(0)
    do.attend_heads()
    kept = [
        local(r.head_query, r.queries),
        local(r.head_key, r.keys),
        local(r.head_value, r.values),
    ]
    second(1)
    first(2, (0, 1))
    do.attend_attention(0)
    third(1)
    first(2, (2,))
    do.attend_attention(1)
    do.attend_merge()
    first(3, (0, 1))
    second(2)
    arrive(rows)
    do.sum_rows()
    do.attend_last()
    first(3, (2,))
    third(2)
    ready(1)
    do.context()
    second(3)
    ready(2)
    do.cross_heads()
    kept += [
        local(r.cross_query, r.cross_queries),
        local(r.cross_key, r.cross_keys),
        local(r.cross_value, r.cross_values),
    ]
    first(4, (0, 1))
    third(3)
    do.cross_attention()
    first(4, (2,))
    second(4)
    do.cross_last()
    do.feed_first()
    first(5, (0, 1))
    ready(3)
    do.feed_hidden()
    third(4)
    first(5, (2,))
    ready(4)
    do.feed_last()
    cols = []
    own = local(r.sent.at[frame], r.held_cols)
    for peer in frame_peers:
        cols.append(copies.start(r.sent.at[peer[1]], r.time_cols.at[:, frame], peer))
    own.wait()
    own = local(r.held_cols, r.time_cols.at[:, frame])
    second(5)
    third(5)
    ready(5)
    arrive(cols)
    own.wait()
    copies.finish()
    for copy in kept:
        copy.wait()


def forward(att_scale, o):
    anywhere = pl.BlockSpec(memory_space=pl.ANY)
    inside = pl.BlockSpec(memory_space=pltpu.VMEM)
    tokens, width = o.latents.shape
    text_count = o.own_text.shape[0]
    hidden = 4 * width
    low, full = jnp.bfloat16, jnp.float32
    shape = jax.ShapeDtypeStruct
    hbm_in = dict(
        share_spatial=o.share_spatial,
        share_context=o.share_context,
        share_text=o.share_text,
        share_expand=o.share_expand,
        share_reduce=o.share_reduce,
        share_time=o.share_time,
        latents=o.latents,
        mod_parts=o.mod_parts,
        row_parts=o.row_parts,
    )
    vmem_in = dict(own_text=o.own_text, text_mask=o.text_mask)
    heads = (HEADS, tokens, HEAD_LANES)
    text_heads = (HEADS, text_count, HEAD_LANES)
    whole = lambda share: shape((8 * share.shape[0], share.shape[1]), low)
    hbm_out = dict(
        whole_spatial=whole(o.share_spatial),
        whole_context=whole(o.share_context),
        whole_text=whole(o.share_text),
        whole_expand=whole(o.share_expand),
        whole_reduce=whole(o.share_reduce),
        whole_time=whole(o.share_time),
    )
    hbm_out.update(
        attend_normal=shape((tokens, width), low),
        attend_turned=shape((width, tokens), low),
        queries=shape(heads, low),
        keys=shape(heads, low),
        values=shape(heads, low),
        spatial_turned=shape((width, tokens), low),
        branch_attend=shape((tokens, width), low),
        after_turned=shape((width, tokens), low),
        context_turned=shape((width, text_count), low),
        cross_queries=shape(heads, low),
        cross_keys=shape(text_heads, low),
        cross_values=shape(text_heads, low),
        cross_turned=shape((width, tokens), low),
        feed_normal=shape((tokens, width), low),
        feed_turned=shape((width, tokens), low),
        gelu_slope=shape((tokens, hidden), low),
        hidden_turned=shape((hidden, tokens), low),
        branch_feed=shape((tokens, width), low),
        after_feed=shape((tokens, width), full),
        sent=shape((8, tokens // (8 * 16), 16, width), low),
        time_cols=shape((tokens // (8 * 16), 8, 16, width), low),
    )
    vmem_out = dict(
        mods=shape((8, width), full),
        rows_low=shape((VEC.high, width), full),
        attend_rate=shape((tokens, LANES), full),
        feed_rate=shape((tokens, LANES), full),
        spatial_logsum=shape((HEADS, 8, tokens), full),
        cross_logsum=shape((HEADS, 8, tokens), full),
    )
    remote = 21 + len(FORWARD_TALLS) * 30
    held = lambda share: pltpu.VMEM(share.shape, low)
    scratch = dict(
        running=pltpu.VMEM((tokens, width), full),
        low=pltpu.VMEM((tokens, width), low),
        middle=pltpu.VMEM((tokens, width), low),
        broad=pltpu.VMEM((tokens, hidden), low),
        head_query=pltpu.VMEM(heads, low),
        head_key=pltpu.VMEM(heads, low),
        head_value=pltpu.VMEM(heads, low),
        head_out=pltpu.VMEM(heads, low),
        cross_query=pltpu.VMEM(heads, low),
        cross_key=pltpu.VMEM(text_heads, low),
        cross_value=pltpu.VMEM(text_heads, low),
        memory=pltpu.VMEM((text_count, 2 * width), low),
        context=pltpu.VMEM((text_count, width), low),
        rows_expand=pltpu.VMEM((8, hidden), full),
        held_spatial=held(o.share_spatial),
        held_context=held(o.share_context),
        held_text=held(o.share_text),
        held_expand=held(o.share_expand),
        held_reduce=held(o.share_reduce),
        held_time=held(o.share_time),
        held_cols=pltpu.VMEM((tokens // (8 * 16), 16, width), low),
        mods_got=pltpu.VMEM((8, 8, width), full),
        rows_got=pltpu.VMEM((8, VEC.high, width), low),
        send_sems=pltpu.SemaphoreType.DMA((remote,)),
        recv_sems=pltpu.SemaphoreType.DMA((remote,)),
        depth_sems=pltpu.SemaphoreType.DMA((len(FORWARD_TALLS), 4)),
        local_sems=pltpu.SemaphoreType.DMA((4 + 2 * len(FORWARD_TALLS) + 6,)),
    )
    names = list(hbm_in) + list(vmem_in) + list(hbm_out) + list(vmem_out) + list(scratch)
    results = pl.pallas_call(
        functools.partial(forward_kernel, att_scale, names),
        out_shape=list(hbm_out.values()) + list(vmem_out.values()),
        in_specs=[anywhere] * len(hbm_in) + [inside] * len(vmem_in),
        out_specs=[anywhere] * len(hbm_out) + [inside] * len(vmem_out),
        scratch_shapes=list(scratch.values()),
        compiler_params=pltpu.CompilerParams(
            collective_id=0, has_side_effects=True, vmem_limit_bytes=60 * 1024 * 1024
        ),
        name="forward",
    )(*hbm_in.values(), *vmem_in.values())
    return types.SimpleNamespace(**dict(zip(list(hbm_out) + list(vmem_out), results)))


def pack_rows(parts, rows):
    flat = jnp.concatenate(parts, axis=-1)
    flat = jnp.pad(flat, [(0, 0)] * (flat.ndim - 1) + [(0, rows * LANES - flat.shape[-1])])
    return flat.reshape(flat.shape[:-1] + (rows, LANES))


def results(
    block_output, input_gradient, mods, sums, totals, text_total, frame_index, row_count, bias_width
):
    model_width = mods.shape[-1]
    high = lambda part: part.astype(jnp.float32)
    total_time, total_reduce, total_expand, total_text, total_spatial = totals
    rows_gradient = mods[:, :6].reshape(-1, 6 * model_width)
    rows_condition = lax.dynamic_slice_in_dim(
        mods[:, ROW.condition], frame_index * row_count, row_count, 1
    )
    back_modulation_weight = jnp.einsum(
        "nd,ne->de", rows_condition, rows_gradient, precision=lax.Precision.HIGHEST
    )
    back_modulation_bias = jnp.sum(
        lax.dynamic_slice_in_dim(rows_gradient, frame_index * bias_width, bias_width, 1), axis=0
    )
    own_rows = lax.dynamic_slice_in_dim(sums, frame_index * row_count, row_count, 1)
    own_row = lambda which: own_rows[which - 8]
    own_expand = lax.dynamic_slice_in_dim(
        sums[ROW.expand - 8 : ROW.expand - 4].reshape(-1), frame_index * 4 * row_count, 4 * row_count, 0
    )
    own_gate = lax.dynamic_slice_in_dim(
        jnp.sum(mods[:, ROW.gate_t], axis=0), frame_index * row_count, row_count, 0
    )
    vec_total = (
        own_row(ROW.spatial),
        own_row(ROW.cross),
        own_expand,
        own_row(ROW.reduce),
        own_row(ROW.gain),
        own_row(ROW.shift),
        own_row(ROW.temporal),
        own_gate,
    )
    matrix_totals = (
        high(total_spatial[:, : 3 * model_width]),
        high(total_text[:, 4 * model_width : 5 * model_width]),
        high(total_text[:, :model_width]),
        high(total_text[:, model_width : 3 * model_width]),
        high(total_text[:, 3 * model_width : 4 * model_width]),
        high(total_expand),
        high(total_reduce),
        high(total_time[:, : 3 * model_width]),
        high(total_time[:, 3 * model_width :]),
    )
    others = (back_modulation_weight, back_modulation_bias, high(text_total)) + tuple(vec_total)
    return (
        block_output,
        input_gradient,
        others[0],
        others[1],
        matrix_totals[0],
        matrix_totals[1],
        others[3],
        others[2],
        matrix_totals[2],
        matrix_totals[3],
        matrix_totals[4],
        others[4],
        matrix_totals[5],
        others[5],
        matrix_totals[6],
        others[6],
        others[7],
        others[8],
        matrix_totals[7],
        matrix_totals[8],
        others[9],
        others[10],
    )


def on_device(
    latents,
    cotangent,
    text_tokens,
    text_lengths,
    clip_frames,
    timesteps,
    motion_free,
    modulation_weight,
    modulation_bias,
    spatial_input,
    spatial_output,
    spatial_bias,
    text_projection,
    cross_query,
    cross_memory,
    cross_output,
    cross_bias,
    expand_weight,
    expand_bias,
    reduce_weight,
    reduce_bias,
    temporal_gain,
    temporal_shift,
    temporal_input,
    temporal_output,
    temporal_bias,
    temporal_gate,
):
    frame_count = lax.axis_size("frame")
    frame_index = lax.axis_index("frame")
    patch_count = latents.shape[2]
    model_width = latents.shape[3]
    head_size = model_width // HEADS
    att_scale = 1.0 / math.sqrt(head_size)
    slot_count = clip_frames.shape[1]
    text_count = text_tokens.shape[2]
    frame_ids = jnp.arange(frame_count, dtype=jnp.int32)
    clip_ids = assign_clips(clip_frames[0], frame_count)
    slot_ids = jnp.arange(slot_count, dtype=jnp.int32)
    own_clip = jnp.sum(jnp.where(frame_ids == frame_index, clip_ids, 0))
    own_onehot = (slot_ids == own_clip).astype(jnp.float32)
    own_keep = 1.0 - jnp.sum(jnp.where(slot_ids == own_clip, motion_free[0], 0)).astype(jnp.float32)
    own_length = jnp.sum(jnp.where(slot_ids == own_clip, text_lengths[0], 0))
    conditioning = embed_time(timesteps[0], model_width).astype(jnp.bfloat16)
    row_count = modulation_weight.shape[0]
    cond_rows = lax.dynamic_slice_in_dim(conditioning, frame_index * row_count, row_count, 1)
    bias_width = modulation_bias.shape[0]
    bias_placed = lax.dynamic_update_slice_in_dim(
        jnp.zeros((6 * model_width,), jnp.float32),
        modulation_bias.astype(jnp.float32),
        frame_index * bias_width,
        0,
    )
    modulation_part = (
        jnp.dot(cond_rows, modulation_weight, preferred_element_type=jnp.float32)
        + bias_placed[None, :]
    )
    share_rows = text_projection.shape[0]
    if one_slice():
        near = 16
        text_high = -(-text_count // LANES) * LANES
        frame_onehot = (clip_ids[:, None] == slot_ids[None, :]).astype(jnp.float32)
        frame_modulation = jnp.sum(frame_onehot[:, :, None] * modulation_part[None], axis=1)
        frame_modulation = frame_modulation.reshape(frame_count, 6, model_width)
        here = (frame_ids == frame_index).astype(jnp.bfloat16)
        shares = jnp.stack(
            [
                spatial_bias,
                cross_bias,
                reduce_bias,
                temporal_gain,
                temporal_shift,
                temporal_bias,
                temporal_gate,
            ]
        )
        row_parts = jnp.concatenate(
            [
                (shares[:, None] * here[None, :, None]).reshape(-1, model_width),
                (expand_bias[None] * here[:, None]).reshape(-1, model_width),
            ]
        )
        own_text = lax.dynamic_index_in_dim(text_tokens[0], own_clip, 0, keepdims=False)
        text_places = jnp.arange(text_high, dtype=jnp.int32) < own_length
        tokens = latents[0, 0]
        operands = dict(
            share_spatial=jnp.concatenate([spatial_input, spatial_output], axis=1),
            share_context=text_projection,
            share_text=jnp.concatenate([cross_query, cross_memory, cross_output], axis=1),
            share_expand=expand_weight,
            share_reduce=reduce_weight,
            share_time=jnp.concatenate([temporal_input, temporal_output], axis=1),
            latents=tokens,
            mod_parts=jnp.pad(frame_modulation, ((0, 0), (0, 2), (0, 0))),
            row_parts=jnp.pad(row_parts, ((0, VEC.high - row_parts.shape[0]), (0, 0))),
            own_text=jnp.pad(own_text, ((0, text_high - text_count), (0, 0))),
            text_mask=jnp.broadcast_to(
                jnp.where(text_places, 0.0, big_negative)[:, None], (text_high, LANES)
            ),
        )
        operands = types.SimpleNamespace(**operands)
        vars(operands).update(vars(forward(att_scale, operands)))
        keep_frames = 1.0 - jnp.sum(
            frame_onehot * motion_free[0].astype(jnp.float32)[None, :], axis=1
        )
        sequence = jnp.arange(frame_count * near, dtype=jnp.int32)
        same = (sequence[:, None] % near == sequence[None, :] % near) & (
            jnp.repeat(clip_ids, near)[:, None] == jnp.repeat(clip_ids, near)[None, :]
        )
        row_keep = jnp.tile(jnp.repeat(keep_frames, near), patch_count // (frame_count * near))
        rows = operands.rows_low
        own_conditioning = jnp.sum(own_onehot[:, None] * conditioning.astype(jnp.float32), axis=0)
        vars(operands).update(
            cotangent=cotangent[0, 0],
            cot_rows=cotangent[0, 0].reshape(operands.sent.shape),
            vectors=jnp.stack(
                [
                    rows[VEC.gain],
                    rows[VEC.shift],
                    rows[VEC.temporal],
                    rows[VEC.gate],
                    rows[VEC.gate] * own_keep,
                    jnp.full((model_width,), own_keep),
                    own_conditioning,
                    jnp.zeros((model_width,), jnp.float32),
                ]
            ),
            time_keep=jnp.broadcast_to(row_keep[:, None], (patch_count, LANES)),
            time_mask=jnp.where(same, 0.0, big_negative),
        )
        text_share = lax.dynamic_slice_in_dim(
            text_tokens[0], frame_index * text_projection.shape[0], text_projection.shape[0], 2
        )
        frame_text = jnp.pad(text_share, ((0, 0), (0, text_high - text_count), (0, 0)))
        text_turned = jnp.einsum("fs,stk->kft", frame_onehot.astype(jnp.bfloat16), frame_text)
        text_turned = text_turned.reshape(text_projection.shape[0], -1)
        got = backward(att_scale, True, operands, text_turned)
        return results(
            got.block_out[None, None],
            got.tokens_out[None, None],
            got.mods_out.reshape(-1, 8, model_width),
            jnp.sum(got.sums_out, axis=0),
            [got.share_time, got.share_reduce, got.share_expand, got.share_text, got.share_input],
            got.text_out,
            frame_index,
            row_count,
            bias_width,
        )
    text_share = lax.dynamic_slice_in_dim(
        text_tokens[0], frame_index * text_projection.shape[0], text_projection.shape[0], 2
    )
    own_text = lax.dynamic_index_in_dim(text_tokens[0], own_clip, 0, keepdims=False)
    vectors = (
        spatial_bias,
        cross_bias,
        expand_bias,
        reduce_bias,
        temporal_gain,
        temporal_shift,
        temporal_bias,
        temporal_gate,
    )
    vector_sizes = [vector.shape[0] for vector in vectors]
    vector_rows = -(-sum(vector_sizes) // (8 * LANES)) * 8
    packed_vectors = pack_rows([vector.astype(jnp.float32) for vector in vectors], vector_rows)
    mod_rows_high = -(-(6 * model_width) // (8 * LANES)) * 8
    frame_onehot = (clip_ids[:, None] == slot_ids[None, :]).astype(jnp.float32)
    frame_modulation = jnp.sum(frame_onehot[:, :, None] * modulation_part[None], axis=1)
    wholes, vecs, mods = gather_all(
        (
            text_projection,
            jnp.concatenate([spatial_input, spatial_output], axis=1),
            jnp.concatenate([cross_query, cross_memory, cross_output], axis=1),
            expand_weight,
            reduce_weight,
            jnp.concatenate([temporal_input, temporal_output], axis=1),
        ),
        packed_vectors,
        pack_rows([frame_modulation], mod_rows_high),
    )
    projection, whole_spatial, whole_text, whole_expand, whole_reduce, whole_time = wholes
    context = jnp.dot(own_text, projection, preferred_element_type=jnp.float32)
    own_modulation = jnp.sum(mods, axis=0).reshape(-1)[: 6 * model_width]
    shift_attend, scale_attend, gate_attend, shift_feed, scale_feed, gate_feed = jnp.split(
        own_modulation, 6
    )
    vecs = vecs.reshape(frame_count, -1)[:, : sum(vector_sizes)]
    vector_ends = [sum(vector_sizes[: index + 1]) for index in range(len(vector_sizes) - 1)]
    (
        whole_bias,
        whole_cross_bias,
        whole_expand_bias,
        whole_reduce_bias,
        whole_gain,
        whole_shift,
        whole_temporal_bias,
        whole_gate,
    ) = [part.reshape(-1) for part in jnp.split(vecs, vector_ends, axis=1)]
    whole_input, whole_output = whole_spatial[:, : 3 * model_width], whole_spatial[:, 3 * model_width :]
    whole_query = whole_text[:, :model_width]
    whole_memory = whole_text[:, model_width : 3 * model_width]
    whole_cross = whole_text[:, 3 * model_width :]
    whole_temporal, whole_temporal_out = whole_time[:, : 3 * model_width], whole_time[:, 3 * model_width :]
    tokens = latents[0, 0].astype(jnp.float32)
    attend_normal, attend_rate = normal_parts(tokens)
    normed_attend = (attend_normal * (1.0 + scale_attend) + shift_attend).astype(jnp.bfloat16)
    spatial_heads = jnp.dot(normed_attend, whole_input, preferred_element_type=jnp.float32).astype(
        jnp.bfloat16
    )
    spatial_heads = spatial_heads.reshape(patch_count, 1, 3, HEADS, head_size)
    spatial_att, spatial_logsum = attend(
        spatial_heads[:, :, 0], spatial_heads[:, :, 1], spatial_heads[:, :, 2], None, att_scale
    )
    spatial_low = spatial_att.reshape(patch_count, model_width).astype(jnp.bfloat16)
    branch_attend = jnp.dot(
        spatial_low, whole_output, preferred_element_type=jnp.float32
    ) + whole_bias.astype(jnp.float32)
    after_attend = tokens + gate_attend * branch_attend
    after_low = after_attend.astype(jnp.bfloat16)
    cross_heads = jnp.dot(after_low, whole_query, preferred_element_type=jnp.float32).astype(
        jnp.bfloat16
    )
    cross_heads = cross_heads.reshape(patch_count, 1, HEADS, head_size)
    context_low = context.astype(jnp.bfloat16)
    memory_heads = jnp.dot(context_low, whole_memory, preferred_element_type=jnp.float32).astype(
        jnp.bfloat16
    )
    memory_heads = memory_heads.reshape(text_count, 1, 2, HEADS, head_size)
    text_mask = (jnp.arange(text_count, dtype=jnp.int32) < own_length)[None, None, None, :]
    cross_att, cross_logsum = attend(
        cross_heads, memory_heads[:, :, 0], memory_heads[:, :, 1], text_mask, att_scale
    )
    cross_low = cross_att.reshape(patch_count, model_width).astype(jnp.bfloat16)
    branch_cross = jnp.dot(
        cross_low, whole_cross, preferred_element_type=jnp.float32
    ) + whole_cross_bias.astype(jnp.float32)
    after_cross = after_attend + branch_cross
    feed_normal, feed_rate = normal_parts(after_cross)
    normed_feed = (feed_normal * (1.0 + scale_feed) + shift_feed).astype(jnp.bfloat16)
    hidden_pre = jnp.dot(
        normed_feed, whole_expand, preferred_element_type=jnp.float32
    ) + whole_expand_bias.astype(jnp.float32)
    hidden_low = smooth_gelu(hidden_pre).astype(jnp.bfloat16)
    gelu_slope = slope_gelu(hidden_pre).astype(jnp.bfloat16)
    branch_feed = jnp.dot(
        hidden_low, whole_reduce, preferred_element_type=jnp.float32
    ) + whole_reduce_bias.astype(jnp.float32)
    after_feed = after_cross + gate_feed * branch_feed
    sent_low = after_feed.astype(jnp.bfloat16)
    low = lambda part: part.astype(jnp.bfloat16)
    gate_keep = whole_gate.astype(jnp.float32) * own_keep
    upstream = cotangent[0, 0].astype(jnp.float32)
    keep_frames = 1.0 - jnp.sum(frame_onehot * motion_free[0].astype(jnp.float32)[None, :], axis=1)
    time_mask = (clip_ids[:, None] == clip_ids[None, :])[None, None]
    gain_float = whole_gain.astype(jnp.float32)
    shift_float = whole_shift.astype(jnp.float32)
    columns = lax.all_to_all(sent_low[None], "frame", split_axis=1, concat_axis=0, tiled=True)
    frames_here = columns.shape[0]
    positions = columns.shape[1]
    normed_time = affine_norm(columns.astype(jnp.float32), gain_float, shift_float).astype(
        jnp.bfloat16
    )
    time_heads = jnp.einsum(
        "fpd,de->fpe", normed_time, whole_temporal, preferred_element_type=jnp.float32
    )
    time_heads = time_heads.astype(jnp.bfloat16).reshape(
        frames_here, positions, 3, HEADS, head_size
    )
    time_att, time_logsum = attend(
        time_heads[:, :, 0], time_heads[:, :, 1], time_heads[:, :, 2], time_mask, att_scale
    )
    time_low = time_att.reshape(frames_here, positions, model_width).astype(jnp.bfloat16)
    result = jnp.einsum(
        "fpd,de->fpe", time_low, whole_temporal_out, preferred_element_type=jnp.float32
    )
    result = result + whole_temporal_bias.astype(jnp.float32)
    result_low = result.astype(jnp.bfloat16)
    kept_state = (normed_time, time_heads, time_low, time_logsum)
    back_sent = (upstream * gate_keep).astype(jnp.bfloat16)
    back_columns = lax.all_to_all(back_sent[None], "frame", split_axis=1, concat_axis=0, tiled=True)
    normed_time, time_heads, time_low, time_logsum = kept_state
    frames_here, positions = (columns.shape[0], columns.shape[1])
    back_temporal_bias = jnp.sum(back_columns.astype(jnp.float32), axis=(0, 1))
    back_temporal_out = jnp.einsum(
        "fpd,fpe->de", time_low, back_columns, preferred_element_type=jnp.float32
    )
    back_time_att = jnp.einsum(
        "fpe,de->fpd", back_columns, whole_temporal_out, preferred_element_type=jnp.float32
    )
    back_time_att = back_time_att.astype(jnp.bfloat16).reshape(
        frames_here, positions, HEADS, head_size
    )
    back_time_queries, back_time_keys, back_time_values = attend_back(
        time_heads[:, :, 0],
        time_heads[:, :, 1],
        time_heads[:, :, 2],
        time_mask,
        att_scale,
        time_logsum,
        back_time_att,
    )
    back_time_heads = jnp.stack([back_time_queries, back_time_keys, back_time_values], axis=2)
    back_time_heads = back_time_heads.reshape(frames_here, positions, 3 * model_width).astype(
        jnp.bfloat16
    )
    back_temporal = jnp.einsum(
        "fpd,fpe->de", normed_time, back_time_heads, preferred_element_type=jnp.float32
    )
    back_normed = jnp.einsum(
        "fpe,de->fpd", back_time_heads, whole_temporal, preferred_element_type=jnp.float32
    )
    unused_norm, norm_back = jax.vjp(
        affine_norm, columns.astype(jnp.float32), gain_float, shift_float
    )
    back_inputs, back_gain, back_shift = norm_back(back_normed)
    returned, back_return = jnp.split(
        lax.all_to_all(
            jnp.concatenate([result_low, back_inputs.astype(jnp.bfloat16)], axis=2),
            "frame",
            split_axis=0,
            concat_axis=1,
            tiled=True,
        ),
        2,
        axis=2,
    )
    temporal_value = returned[0].astype(jnp.float32)
    block_output = (after_feed + gate_keep * temporal_value).astype(jnp.bfloat16)[None, None]
    back_gate = jnp.sum(upstream * temporal_value, axis=0) * own_keep
    text_high = -(-text_count // LANES) * LANES

    def padded_heads(heads, high):
        heads = jnp.transpose(heads[:, 0], (1, 0, 2))
        return jnp.pad(heads, ((0, 0), (0, high - heads.shape[1]), (0, HEAD_LANES - head_size)))

    padded_context = jnp.pad(context_low, ((0, text_high - text_count), (0, 0)))
    text_places = jnp.arange(text_high, dtype=jnp.int32) < own_length
    operands = dict(
        whole_spatial=whole_spatial,
        whole_text=whole_text,
        whole_expand=whole_expand,
        whole_reduce=whole_reduce,
        cotangent=cotangent[0, 0],
        branch_feed=low(branch_feed),
        hidden_turned=hidden_low.T,
        gelu_slope=gelu_slope,
        feed_turned=normed_feed.T,
        feed_normal=low(feed_normal),
        cross_turned=cross_low.T,
        cross_queries=padded_heads(cross_heads, patch_count),
        cross_keys=padded_heads(memory_heads[:, :, 0], text_high),
        cross_values=padded_heads(memory_heads[:, :, 1], text_high),
        after_turned=after_low.T,
        context_turned=padded_context.T,
        branch_attend=low(branch_attend),
        spatial_turned=spatial_low.T,
        queries=padded_heads(spatial_heads[:, :, 0], patch_count),
        keys=padded_heads(spatial_heads[:, :, 1], patch_count),
        values=padded_heads(spatial_heads[:, :, 2], patch_count),
        attend_turned=normed_attend.T,
        attend_normal=low(attend_normal),
        mods=jnp.pad(own_modulation.reshape(6, model_width), ((0, 2), (0, 0))),
        feed_rate=jnp.broadcast_to(feed_rate, (patch_count, LANES)),
        attend_rate=jnp.broadcast_to(attend_rate, (patch_count, LANES)),
        cross_logsum=jnp.broadcast_to(
            cross_logsum[0, :, None, :, 0], (HEADS, 8, patch_count)
        ),
        spatial_logsum=jnp.broadcast_to(
            spatial_logsum[0, :, None, :, 0], (HEADS, 8, patch_count)
        ),
        text_mask=jnp.broadcast_to(
            jnp.where(text_places, 0.0, big_negative)[:, None], (text_high, LANES)
        ),
    )
    own_conditioning = jnp.sum(own_onehot[:, None] * conditioning.astype(jnp.float32), axis=0)
    operands.update(back_sent=back_return[0])
    got = backward(att_scale, False, types.SimpleNamespace(**operands), None)
    input_gradient = got.tokens_out[None, None]
    rows = got.row_sums
    rows = rows.at[ROW.condition].set(own_conditioning).at[ROW.gate_t].set(back_gate)
    rows = rows.at[ROW.gain].set(back_gain).at[ROW.shift].set(back_shift)
    rows = rows.at[ROW.temporal].set(back_temporal_bias)
    mods = lax.all_gather(rows[:8], ("clip", "frame"), axis=0)
    sums = lax.psum(rows[8:], ("clip", "frame"))
    all_context = lax.all_gather(got.back_context[:text_count], "frame", axis=0)
    context_total = jnp.einsum("fs,ftd->std", frame_onehot, all_context.astype(jnp.float32))
    text_total = lax.psum(
        jnp.einsum(
            "stk,std->kd",
            text_share,
            low(context_total),
            preferred_element_type=jnp.float32,
        ).astype(jnp.bfloat16),
        "clip",
    )
    totals = [
        sum_shares((low(back_temporal), low(back_temporal_out))),
        sum_shares((got.part_reduce,)),
        sum_shares((got.part_expand,)),
        sum_shares((got.part_text,)),
        sum_shares((got.part_input,)),
    ]
    return results(
        block_output,
        input_gradient,
        mods,
        sums,
        totals,
        text_total,
        frame_index,
        row_count,
        bias_width,
    )


def solution(mesh):
    placed = (
        P("clip", "frame", None, None),
        P("clip", "frame", None, None),
        P("clip", None, None, None),
        P("clip", None),
        P("clip", None),
        P("clip", None),
        P("clip", None),
        P("frame", None),
        P("frame"),
        P("frame", None),
        P("frame", None),
        P("frame"),
        P("frame", None),
        P("frame", None),
        P("frame", None),
        P("frame", None),
        P("frame"),
        P("frame", None),
        P("frame"),
        P("frame", None),
        P("frame"),
        P("frame"),
        P("frame"),
        P("frame", None),
        P("frame", None),
        P("frame"),
        P("frame"),
    )
    return jax.shard_map(
        on_device,
        mesh=mesh,
        in_specs=placed,
        out_specs=(
            P("clip", "frame", None, None),
            P("clip", "frame", None, None),
            P("frame", None),
            P("frame"),
            P("frame", None),
            P("frame", None),
            P("frame"),
            P("frame", None),
            P("frame", None),
            P("frame", None),
            P("frame", None),
            P("frame"),
            P("frame", None),
            P("frame"),
            P("frame", None),
            P("frame"),
            P("frame"),
            P("frame"),
            P("frame", None),
            P("frame", None),
            P("frame"),
            P("frame"),
        ),
        check_vma=False,
    )
```

```python
import functools
import math
import types

import jax
import jax.numpy as jnp
from jax import lax
from jax.experimental import pallas as pl
from jax.experimental.pallas import tpu as pltpu
from jax.sharding import PartitionSpec as P

HEADS = 16


eps_norm = 1e-06
big_negative = -1e30


def assign_clips(frame_counts, frame_count):
    slot_count = frame_counts.shape[0]
    slot_ids = jnp.arange(slot_count, dtype=jnp.int32)
    longest = jnp.max(frame_counts)
    long_slot = jnp.min(jnp.where(frame_counts == longest, slot_ids, slot_count))
    frame_ids = jnp.arange(frame_count, dtype=jnp.int32)
    long_gaps = jnp.maximum(longest - 1, 1)
    frame_gaps = frame_count - 1
    step_index = (frame_ids * long_gaps + frame_gaps - 1) // frame_gaps
    on_long = step_index * frame_gaps // long_gaps == frame_ids
    long_marks = on_long.astype(jnp.int32)
    before_count = jnp.cumsum(long_marks) - long_marks
    order_rank = frame_ids - before_count
    rest_counts = jnp.where(slot_ids == long_slot, 0, frame_counts)
    rest_ends = jnp.cumsum(rest_counts)
    rest_ids = jnp.sum((rest_ends[None, :] <= order_rank[:, None]).astype(jnp.int32), axis=1)
    return jnp.where(on_long, long_slot, rest_ids)


def normalize(values):
    average = jnp.mean(values, axis=-1, keepdims=True)
    centred = values - average
    spread = jnp.mean(centred * centred, axis=-1, keepdims=True)
    return centred * lax.rsqrt(spread + eps_norm)


def normal_parts(values):
    average = jnp.mean(values, axis=-1, keepdims=True)
    centred = values - average
    rate = lax.rsqrt(jnp.mean(centred * centred, axis=-1, keepdims=True) + eps_norm)
    return centred * rate, rate


def modulate(values, offset, scaling):
    return normalize(values) * (1.0 + scaling) + offset


def affine_norm(values, norm_gain, offset):
    return normalize(values) * norm_gain + offset


def smooth_gelu(values):
    return jax.nn.gelu(values, approximate=True)


def slope_gelu(values):
    inner = math.sqrt(2.0 / math.pi)
    bent = jnp.tanh(inner * (values + 0.044715 * values * values * values))
    steep = inner * (1.0 + 3.0 * 0.044715 * values * values)
    return 0.5 * (1.0 + bent) + 0.5 * values * (1.0 - bent * bent) * steep


def embed_time(time_steps, model_width):
    half_width = model_width // 2
    frequency = jnp.exp(-math.log(10000.0) * jnp.arange(half_width, dtype=jnp.float32) / half_width)
    angles = time_steps.astype(jnp.float32)[:, None] * frequency[None, :]
    return jax.nn.silu(jnp.concatenate([jnp.cos(angles), jnp.sin(angles)], axis=1))


def attend(queries, key_rows, values, valid_mask, att_scale):
    scores = (
        jnp.einsum("qbhd,kbhd->bhqk", queries, key_rows, preferred_element_type=jnp.float32)
        * att_scale
    )
    if valid_mask is not None:
        scores = jnp.where(valid_mask, scores, big_negative)
    largest = jnp.max(scores, axis=-1, keepdims=True)
    summed = jnp.sum(jnp.exp(scores - largest), axis=-1, keepdims=True)
    logsum = largest + jnp.log(summed)
    weights = jnp.exp(scores - logsum).astype(jnp.bfloat16)
    output = jnp.einsum("bhqk,kbhd->qbhd", weights, values, preferred_element_type=jnp.float32)
    return (output, logsum)


def attend_back(queries, key_rows, values, valid_mask, att_scale, logsum, upstream):
    scores = (
        jnp.einsum("qbhd,kbhd->bhqk", queries, key_rows, preferred_element_type=jnp.float32)
        * att_scale
    )
    if valid_mask is not None:
        scores = jnp.where(valid_mask, scores, big_negative)
    weights = jnp.exp(scores - logsum)
    back_weights = jnp.einsum(
        "qbhd,kbhd->bhqk", upstream, values, preferred_element_type=jnp.float32
    )
    back_values = jnp.einsum(
        "bhqk,qbhd->kbhd",
        weights.astype(jnp.bfloat16),
        upstream,
        preferred_element_type=jnp.float32,
    )
    inner_sum = jnp.sum(back_weights * weights, axis=-1, keepdims=True)
    back_scores = (weights * (back_weights - inner_sum)).astype(jnp.bfloat16)
    back_queries = (
        jnp.einsum("bhqk,kbhd->qbhd", back_scores, key_rows, preferred_element_type=jnp.float32)
        * att_scale
    )
    back_keys = (
        jnp.einsum("bhqk,qbhd->kbhd", back_scores, queries, preferred_element_type=jnp.float32)
        * att_scale
    )
    return (back_queries, back_keys, back_values)


MESH_ID = pl.DeviceIdType.MESH
LANES = 128
PIECE_SLOTS = 4


def neighbours():
    column = lax.axis_index("clip")
    frame = lax.axis_index("frame")
    depth = frame // 2
    core = frame % 2
    across_x = column + 1 - 2 * (column % 2)
    across_y = column + 2 - 4 * (column // 2)
    sibling = frame + 1 - 2 * core
    return column, frame, depth, core, across_x, across_y, sibling


def greet(peers):
    barrier = pltpu.get_barrier_semaphore()
    for peer in peers:
        pl.semaphore_signal(barrier, inc=1, device_id=peer, device_id_type=MESH_ID)
    pl.semaphore_wait(barrier, len(peers))


class Copies:
    def __init__(self, send_sems, recv_sems):
        self.send_sems, self.recv_sems, self.count, self.started = send_sems, recv_sems, 0, []
        self.maybe = []

    def start(self, source, target, device):
        copy = pltpu.make_async_remote_copy(
            src_ref=source,
            dst_ref=target,
            send_sem=self.send_sems.at[self.count],
            recv_sem=self.recv_sems.at[self.count],
            device_id=device,
            device_id_type=MESH_ID,
        )
        self.count += 1
        assert self.count <= self.send_sems.shape[0]
        copy.start()
        self.started.append(copy)
        return copy

    def start_if(self, condition, source, target, device, recv_sem):
        copy = pltpu.make_async_remote_copy(
            src_ref=source,
            dst_ref=target,
            send_sem=self.send_sems.at[self.count],
            recv_sem=recv_sem,
            device_id=device,
            device_id_type=MESH_ID,
        )
        self.count += 1
        assert self.count <= self.send_sems.shape[0]
        pl.when(condition)(copy.start)
        self.maybe.append((condition, copy))

    def release(self, copy):
        copy.wait_send()
        self.started = [other for other in self.started if other is not copy]

    def finish(self):
        for copy in self.started:
            copy.wait_send()
        for condition, copy in self.maybe:
            pl.when(condition)(copy.wait_send)


def rows_at(ref, start, size, step):
    return ref.at[pl.ds(pl.multiple_of(start, step), size), :]


def whole_unit(ref, tall, unit, frame):
    if tall:
        height = ref.shape[0] // 32
        return rows_at(ref, frame * (4 * height) + unit * height, height, height)
    height, width = ref.shape[0] // 8, ref.shape[1] // 4
    return ref.at[
        pl.ds(pl.multiple_of(frame * height, height), height),
        pl.ds(pl.multiple_of(unit * width, LANES), width),
    ]


def whole_share(ref, tall, frame):
    height = ref.shape[0] // 8
    return rows_at(ref, frame * height, height, height)


def share_unit(ref, tall, unit):
    if tall:
        height = ref.shape[0] // 4
        return rows_at(ref, unit * height, height, height)
    width = ref.shape[1] // 4
    return ref.at[:, pl.ds(pl.multiple_of(unit * width, LANES), width)]


def gather_all(shares, vec, mod_rows):
    wholes = [lax.all_gather(share, "frame", axis=0, tiled=True) for share in shares]
    vecs = lax.all_gather(vec, "frame", axis=0)
    mods = lax.all_to_all(mod_rows, "frame", split_axis=0, concat_axis=0, tiled=True)
    return wholes, vecs, mods


def add_stream(count, left_at, right_at, out_at, left_buf, right_buf, out_buf, sems):
    def loads(index):
        slot = index % PIECE_SLOTS
        return (
            pltpu.make_async_copy(left_at(index), left_buf.at[slot], sems.at[0, slot]),
            pltpu.make_async_copy(right_at(index), right_buf.at[slot], sems.at[1, slot]),
        )

    def store(index):
        slot = index % PIECE_SLOTS
        return pltpu.make_async_copy(out_buf.at[slot], out_at(index), sems.at[2, slot])

    ahead = min(PIECE_SLOTS - 1, count)
    for index in range(ahead):
        for copy in loads(index):
            copy.start()

    def step(index, carry):
        @pl.when(index + PIECE_SLOTS - 1 < count)
        def _():
            for copy in loads(index + PIECE_SLOTS - 1):
                copy.start()

        for copy in loads(index):
            copy.wait()

        @pl.when(index >= PIECE_SLOTS)
        def _():
            store(index - PIECE_SLOTS).wait()

        slot = index % PIECE_SLOTS
        out_buf[slot] = left_buf[slot] + right_buf[slot]
        store(index).start()
        return carry

    lax.fori_loop(0, count, step, 0)
    for index in range(max(0, count - PIECE_SLOTS), count):
        store(index).wait()


ROW_TILE = 128
HEAD_TILE = 64
HEAD_LANES = 128
MOD_ROWS = 6


def dot_rows(left, right):
    return lax.dot_general(
        left, right, (((1,), (1,)), ((), ())), preferred_element_type=jnp.float32
    )


def dot_plain(left, right):
    return jnp.dot(left, right, preferred_element_type=jnp.float32)


def run_tiles(body, count, ins, outs):
    pltpu.emit_pipeline(
        body,
        grid=(count,),
        in_specs=[pl.BlockSpec(block, index) for _, block, index in ins],
        out_specs=[pl.BlockSpec(block, index) for _, block, index in outs],
    )(*[ref for ref, _, _ in ins], *[ref for ref, _, _ in outs])


def by_rows(ref, size):
    if len(ref.shape) == 4:
        many = size // (ref.shape[1] * ref.shape[2])
        return (ref, (many,) + ref.shape[1:], lambda step: (step, 0, 0, 0))
    return (ref, (size, ref.shape[1]), lambda step: (step, 0))


def by_columns(ref, size):
    return (ref, (ref.shape[0], size), lambda step: (0, step))


def tile_rows(step, size):
    return pl.ds(pl.multiple_of(step * size, size), size)


def add_row(rows, which, values):
    rows[which : which + 1, :] += jnp.sum(values, axis=0, keepdims=True)


def split_heads(source, first, heads, width, count):
    height = source.shape[0]
    tile = min(height, HEAD_TILE)

    def step(index, carry):
        rows = tile_rows(index, tile)
        for head in range(count):
            start = first + head * width
            heads[head, rows, 0:width] = source[rows, start : start + width]
        return carry

    lax.fori_loop(0, height // tile, step, 0)


def merge_heads(heads, target, first, width, count):
    height = target.shape[0]
    tile = min(height, HEAD_TILE)

    def step(index, carry):
        rows = tile_rows(index, tile)
        joined = jnp.concatenate([heads[head, rows, 0:width] for head in range(count)], axis=1)
        target[rows, first : first + width * count] = joined
        return carry

    lax.fori_loop(0, height // tile, step, 0)


def attention_back(att_scale, queries, keys, values, mask, logsum, upstream, outs, group=1):
    out_queries, out_keys, out_values = outs
    count = queries.shape[0]

    def body(query, key, value):
        heads = [pl.program_id(0) * group + index for index in range(group)]
        query, key, value = ([ref[index] for index in range(group)] for ref in (query, key, value))
        given = [upstream[head] for head in heads]
        scores = [dot_rows(*pair) * att_scale for pair in zip(key, query)]
        if mask is not None:
            scores = [score + mask[:, 0:1] for score in scores]
        weights = [
            jnp.exp(score - logsum[head, 0:1, :]) for score, head in zip(scores, heads)
        ]
        backs = [dot_rows(*pair) for pair in zip(value, given)]
        inner = [
            jnp.sum(back * weight, axis=0, keepdims=True) for back, weight in zip(backs, weights)
        ]
        backs = [
            (weight * (back - total)).astype(jnp.bfloat16)
            for weight, back, total in zip(weights, backs, inner)
        ]
        back_values = [
            dot_plain(weight.astype(jnp.bfloat16), one).astype(jnp.bfloat16)
            for weight, one in zip(weights, given)
        ]
        back_keys = [
            (dot_plain(*pair) * att_scale).astype(jnp.bfloat16) for pair in zip(backs, query)
        ]
        turned = [
            lax.dot_general(*pair, (((0,), (0,)), ((), ())), preferred_element_type=jnp.float32)
            for pair in zip(key, backs)
        ]
        turned = [(one * att_scale).T.astype(jnp.bfloat16) for one in turned]
        for index, head in enumerate(heads):
            out_values[head] = back_values[index]
            out_keys[head] = back_keys[index]
            out_queries[head] = turned[index]

    per_head = lambda ref: (ref, (group,) + ref.shape[1:], lambda step: (step, 0, 0))
    run_tiles(body, count // group, [per_head(queries), per_head(keys), per_head(values)], [])


ROW = types.SimpleNamespace(
    shift_a=0, scale_a=1, gate_a=2, shift_m=3, scale_m=4, gate_m=5, condition=6, gate_t=7,
    spatial=8, cross=9, reduce=10, gain=11, shift=12, temporal=13, expand=14, high=24,
)


def back_stages(r, att_scale):
    width = r.running.shape[1]
    head_size = width // HEADS
    third = width // 3
    plain = jnp.float32

    def clear():
        r.row_sums[...] = jnp.zeros_like(r.row_sums)
        for heads in (r.head_in, r.head_query, r.head_key, r.head_value):
            heads[...] = jnp.zeros_like(heads)

    def feed_first():
        def body(cot, sent, branch):
            rows = tile_rows(pl.program_id(0), ROW_TILE)
            total = cot[...].astype(plain) + sent[...].reshape(cot.shape).astype(plain)
            r.running[rows, :] = total
            add_row(r.row_sums, ROW.gate_m, total * branch[...].astype(plain))
            down = (total * r.mods[5:6, :]).astype(jnp.bfloat16)
            r.low[rows, :] = down
            add_row(r.row_sums, ROW.reduce, down.astype(plain))

        ins = [by_rows(ref, ROW_TILE) for ref in (r.cotangent, r.back_sent, r.branch_feed)]
        run_tiles(body, r.low.shape[0] // ROW_TILE, ins, [])

    def part_by_rows(turned, right, target, size, place=0):
        def body(left, out):
            out[...] = dot_plain(left[...], right()).astype(jnp.bfloat16)

        run_tiles(
            body,
            turned.shape[0] // size,
            [by_rows(turned, size)],
            [(target, (size, width), lambda step: (step, place))],
        )

    def part_by_columns(turned, right, target, size, first=0, count=None):
        def body(left, out):
            columns = tile_rows(pl.program_id(0) + first, size)
            out[...] = dot_plain(left[...], right[:, columns]).astype(jnp.bfloat16)

        whole = (turned, turned.shape, lambda step: (0, 0))
        run_tiles(
            body,
            target.shape[1] // size if count is None else count,
            [whole],
            [(target, (target.shape[0], size), lambda step: (0, step + first))],
        )

    def reduce_part():
        part_by_rows(r.hidden_turned, lambda: r.low[...], r.part_reduce, 512)

    def feed_hidden():
        def body(weight, slope):
            columns = tile_rows(pl.program_id(0), 512)
            back = dot_rows(r.low[...], weight[...]) * slope[...].astype(plain)
            down = back.astype(jnp.bfloat16)
            r.broad[:, columns] = down

        run_tiles(
            body,
            r.broad.shape[1] // 512,
            [by_rows(r.whole_reduce, 512), by_columns(r.gelu_slope, 512)],
            [],
        )
        for unit in range(4):
            piece = r.broad[:, unit * width : (unit + 1) * width].astype(plain)
            add_row(r.row_sums, ROW.expand + unit, piece)

    def expand_part():
        part_by_columns(r.feed_turned, r.broad, r.part_expand, 512)

    def back_through(weight, block, place, source, target):
        def body(rows):
            columns = tile_rows(pl.program_id(0), third)
            target(columns, dot_rows(source(), rows[...]))

        run_tiles(body, 3, [(weight, (third, block), lambda step: (step, place))], [])

    def set_wide(columns, value):
        r.wide[:, columns] = value

    def add_running(columns, value):
        r.running[:, columns] += value

    def set_broad(columns, value):
        r.broad[:, columns] = value.astype(jnp.bfloat16)

    def back_three(weight):
        def body(*blocks):
            columns = tile_rows(pl.program_id(0), third)
            total = dot_rows(r.broad[:, 0:width], blocks[0][...])
            for place in (1, 2):
                total += dot_rows(
                    r.broad[:, place * width : (place + 1) * width], blocks[place][...]
                )
            r.wide[:, columns] = total

        block = lambda place: (weight, (third, width), lambda step: (step, place))
        run_tiles(body, 3, [block(0), block(1), block(2)], [])

    def feed_normed():
        back_through(r.whole_expand, 4 * width, 0, lambda: r.broad[...], set_wide)

    def norm_back(rows, normal, rate, shift_row, scale_row):
        back = r.wide[rows, :]
        normal = normal.astype(plain)
        add_row(r.row_sums, shift_row, back)
        add_row(r.row_sums, scale_row, back * normal)
        back = back * (1.0 + r.mods[scale_row : scale_row + 1, :])
        mean = jnp.mean(back, axis=1, keepdims=True)
        inner = jnp.mean(back * normal, axis=1, keepdims=True)
        return (back - mean - normal * inner) * rate[rows, 0:1]

    def feed_last():
        def body(normal):
            rows = tile_rows(pl.program_id(0), ROW_TILE)
            total = r.running[rows, :] + norm_back(rows, normal[...], r.feed_rate, 3, 4)
            r.running[rows, :] = total
            down = total.astype(jnp.bfloat16)
            r.low[rows, :] = down
            add_row(r.row_sums, ROW.cross, down.astype(plain))

        run_tiles(body, r.low.shape[0] // ROW_TILE, [by_rows(r.feed_normal, ROW_TILE)], [])

    def cross_part():
        part_by_rows(r.cross_turned, lambda: r.low[...], r.part_text.at[:, pl.ds(0, 4 * width)], third, 3)

    def cross_given():
        back_through(r.whole_text, width, 3, lambda: r.low[...], set_broad)
        split_heads(r.broad, 0, r.head_in, head_size, HEADS)

    def cross_attention():
        attention_back(
            att_scale,
            r.cross_queries,
            r.cross_keys,
            r.cross_values,
            r.text_mask,
            r.cross_logsum,
            r.head_in,
            (r.head_query, r.cross_key, r.cross_value),
            group=4,
        )
        merge_heads(r.head_query, r.broad, 0, head_size, HEADS)
        merge_heads(r.cross_key, r.memory, 0, head_size, HEADS)
        merge_heads(r.cross_value, r.memory, width, head_size, HEADS)

    def query_part():
        part_by_rows(r.after_turned, lambda: r.broad[:, 0:width], r.part_text.at[:, pl.ds(0, 4 * width)], third, 0)

    def memory_part():
        for place in range(2):
            part_by_rows(
                r.context_turned,
                lambda: r.memory[:, place * width : (place + 1) * width],
                r.part_text.at[:, pl.ds(0, 4 * width)],
                third,
                place + 1,
            )

    def context_back():
        def body(keys, values, out):
            back = dot_rows(r.memory[:, 0:width], keys[...])
            back = back + dot_rows(r.memory[:, width : 2 * width], values[...])
            out[...] = back.astype(jnp.bfloat16)

        run_tiles(
            body,
            3,
            [
                (r.whole_text, (third, width), lambda step: (step, 1)),
                (r.whole_text, (third, width), lambda step: (step, 2)),
            ],
            [by_columns(r.back_context, third)],
        )

    def query_back():
        back_through(r.whole_text, width, 0, lambda: r.broad[:, 0:width], add_running)

    def spatial_first():
        def body(branch):
            rows = tile_rows(pl.program_id(0), ROW_TILE)
            total = r.running[rows, :]
            add_row(r.row_sums, ROW.gate_a, total * branch[...].astype(plain))
            down = (total * r.mods[2:3, :]).astype(jnp.bfloat16)
            r.low[rows, :] = down
            add_row(r.row_sums, ROW.spatial, down.astype(plain))

        run_tiles(body, r.low.shape[0] // ROW_TILE, [by_rows(r.branch_attend, ROW_TILE)], [])

    def output_part():
        def body(left, out):
            out[:, 0:width] = dot_plain(left[...], r.low[...]).astype(jnp.bfloat16)
            out[:, width:] = jnp.zeros_like(out[:, width:])

        run_tiles(
            body,
            3,
            [by_rows(r.spatial_turned, third)],
            [(r.part_text, (third, width + third), lambda step: (step, 3))],
        )

    def spatial_given():
        back_through(r.whole_spatial, width, 3, lambda: r.low[...], set_broad)
        split_heads(r.broad, 0, r.head_in, head_size, HEADS)

    def spatial_attention():
        attention_back(
            att_scale,
            r.queries,
            r.keys,
            r.values,
            None,
            r.spatial_logsum,
            r.head_in,
            (r.head_query, r.head_key, r.head_value),
        )
        merge_heads(r.head_query, r.broad, 0, head_size, HEADS)
        merge_heads(r.head_key, r.broad, width, head_size, HEADS)
        merge_heads(r.head_value, r.broad, 2 * width, head_size, HEADS)

    def input_part(first=0, count=7):
        part_by_columns(r.attend_turned, r.broad, r.part_input, 512, first, count)

    def attend_normed():
        back_three(r.whole_spatial)

    def attend_last():
        def body(normal, out):
            rows = tile_rows(pl.program_id(0), ROW_TILE)
            total = r.running[rows, :] + norm_back(rows, normal[...], r.attend_rate, 0, 1)
            out[...] = total.astype(jnp.bfloat16)

        run_tiles(
            body,
            r.low.shape[0] // ROW_TILE,
            [by_rows(r.attend_normal, ROW_TILE)],
            [by_rows(r.tokens_out, ROW_TILE)],
        )

    tile = r.low.shape[0] // 4
    quads = [pl.ds(index * tile, tile) for index in range(4)]

    def by_blocks(ref):
        return (ref, (1,) + ref.shape[1:], lambda step: (step, 0, 0, 0))

    def turn(source, target):
        def step(index, carry):
            rows = tile_rows(index, tile)
            target[:, rows] = source[rows, :].astype(plain).T.astype(jnp.bfloat16)
            return carry

        lax.fori_loop(0, 4, step, 0)

    def time_first():
        def body(cols):
            rows = tile_rows(pl.program_id(0), tile)
            values = cols[...].reshape(tile, width).astype(plain)
            values = values - jnp.mean(values, axis=1, keepdims=True)
            rate = lax.rsqrt(jnp.mean(values * values, axis=1, keepdims=True) + eps_norm)
            normal = values * rate
            r.time_normal[rows, :] = normal.astype(jnp.bfloat16)
            r.time_rate[rows, :] = jnp.broadcast_to(rate, (tile, LANES))
            r.low[rows, :] = (normal * r.vectors[0:1, :] + r.vectors[1:2, :]).astype(jnp.bfloat16)

        run_tiles(body, 4, [by_blocks(r.time_cols)], [])
        turn(r.low, r.time_turned)

    def time_heads():
        def body(weight):
            columns = tile_rows(pl.program_id(0), third)
            r.broad[:, columns] = dot_plain(r.low[...], weight[...]).astype(jnp.bfloat16)

        run_tiles(body, 9, [by_columns(r.whole_time, third)], [])
        for place, heads in enumerate((r.head_query, r.head_key, r.head_value)):
            split_heads(r.broad, place * width, heads, head_size, HEADS)

    def time_attention():
        def step(pair, carry):
            spots = [(pair * 2 + index, rows) for index in range(2) for rows in quads]
            keys = [r.head_key[spot] for spot in spots]
            values = [r.head_value[spot] for spot in spots]
            scores = [
                dot_rows(key, r.head_query[spot]) * att_scale + r.time_mask[...]
                for key, spot in zip(keys, spots)
            ]
            largest = [jnp.max(score, axis=0, keepdims=True) for score in scores]
            logsums = [
                top + jnp.log(jnp.sum(jnp.exp(score - top), axis=0, keepdims=True))
                for score, top in zip(scores, largest)
            ]
            weights = [
                jnp.exp(score - logs).astype(jnp.bfloat16) for score, logs in zip(scores, logsums)
            ]
            turned = [
                lax.dot_general(
                    value, weight, (((0,), (0,)), ((), ())), preferred_element_type=plain
                )
                for value, weight in zip(values, weights)
            ]
            turned = [value.T.astype(jnp.bfloat16) for value in turned]
            for (head, rows), logs, value in zip(spots, logsums, turned):
                r.time_logsum[head, 0:1, rows] = logs
                r.head_in[head, rows, :] = value
            return carry

        lax.fori_loop(0, HEADS // 2, step, 0)
        merge_heads(r.head_in, r.middle, 0, head_size, HEADS)
        turn(r.middle, r.middle_turned)

    def time_result():
        def body(weight, out):
            columns = tile_rows(pl.program_id(0), third)
            value = dot_plain(r.middle[...], weight[...]) + r.vectors[2:3, columns]
            out[...] = value.astype(jnp.bfloat16).reshape(out.shape)

        shape = r.time_result.shape
        run_tiles(
            body,
            3,
            [(r.whole_time, (width, third), lambda step: (0, 9 + step))],
            [(r.time_result, shape[:3] + (third,), lambda step: (0, 0, 0, step))],
        )

    def time_given():
        def body(cols):
            rows = tile_rows(pl.program_id(0), tile)
            values = cols[...].reshape(tile, width).astype(plain)
            down = (values * (r.time_keep[rows, 0:1] * r.vectors[3:4, :])).astype(jnp.bfloat16)
            r.low[rows, :] = down
            add_row(r.row_sums, ROW.temporal, down.astype(plain))

        run_tiles(body, 4, [by_blocks(r.cot_cols)], [])
        back_through(r.whole_time, width, 3, lambda: r.low[...], set_broad)
        split_heads(r.broad, 0, r.head_in, head_size, HEADS)

    def time_out_part():
        def body(out):
            rows = tile_rows(pl.program_id(0), third)
            out[...] = dot_plain(r.middle_turned[rows, :], r.low[...]).astype(jnp.bfloat16)

        run_tiles(body, 3, [], [(r.part_time, (third, width), lambda step: (step, 3))])

    def time_attention_back():
        def step(pair, carry):
            spots = [(pair * 2 + index, rows) for index in range(2) for rows in quads]
            queries = [r.head_query[spot] for spot in spots]
            keys = [r.head_key[spot] for spot in spots]
            values = [r.head_value[spot] for spot in spots]
            givens = [r.head_in[spot] for spot in spots]
            weights = [
                jnp.exp(
                    dot_rows(key, query) * att_scale
                    + r.time_mask[...]
                    - r.time_logsum[head, 0:1, rows]
                )
                for key, query, (head, rows) in zip(keys, queries, spots)
            ]
            backs = [dot_rows(value, given) for value, given in zip(values, givens)]
            inner = [
                jnp.sum(back * weight, axis=0, keepdims=True)
                for back, weight in zip(backs, weights)
            ]
            backs = [
                (weight * (back - total)).astype(jnp.bfloat16)
                for weight, back, total in zip(weights, backs, inner)
            ]
            back_values = [
                dot_plain(weight.astype(jnp.bfloat16), given).astype(jnp.bfloat16)
                for weight, given in zip(weights, givens)
            ]
            back_keys = [
                (dot_plain(back, query) * att_scale).astype(jnp.bfloat16)
                for back, query in zip(backs, queries)
            ]
            turned = [
                lax.dot_general(key, back, (((0,), (0,)), ((), ())), preferred_element_type=plain)
                for key, back in zip(keys, backs)
            ]
            turned = [(value * att_scale).T.astype(jnp.bfloat16) for value in turned]
            for (head, rows), *outs in zip(spots, turned, back_keys, back_values):
                r.head_query[head, rows, :] = outs[0]
                r.head_key[head, rows, :] = outs[1]
                r.head_value[head, rows, :] = outs[2]
            return carry

        lax.fori_loop(0, HEADS // 2, step, 0)
        for place, heads in enumerate((r.head_query, r.head_key, r.head_value)):
            merge_heads(heads, r.broad, place * width, head_size, HEADS)

    def time_normed():
        back_three(r.whole_time)

    def time_last():
        def body(out):
            rows = tile_rows(pl.program_id(0), tile)
            back = r.wide[rows, :]
            normal = r.time_normal[rows, :].astype(plain)
            add_row(r.row_sums, ROW.shift, back)
            add_row(r.row_sums, ROW.gain, back * normal)
            back = back * r.vectors[0:1, :]
            mean = jnp.mean(back, axis=1, keepdims=True)
            inner = jnp.mean(back * normal, axis=1, keepdims=True)
            back = (back - mean - normal * inner) * r.time_rate[rows, 0:1]
            out[...] = back.astype(jnp.bfloat16).reshape(out.shape)

        run_tiles(body, 4, [], [by_blocks(r.time_back)])

    def time_in_part():
        def body(out):
            columns = tile_rows(pl.program_id(0), third)
            out[...] = dot_plain(r.time_turned[...], r.broad[:, columns]).astype(jnp.bfloat16)

        run_tiles(body, 9, [], [by_columns(r.part_time, third)])

    def block_last():
        def body(after, result, cot, out):
            value = result[...].reshape(cot.shape).astype(plain)
            add_row(r.row_sums, ROW.gate_t, cot[...].astype(plain) * value * r.vectors[5:6, :])
            out[...] = (after[...] + r.vectors[4:5, :] * value).astype(jnp.bfloat16)

        ins = [by_rows(ref, ROW_TILE) for ref in (r.after_feed, r.returned, r.cotangent)]
        run_tiles(body, r.low.shape[0] // ROW_TILE, ins, [by_rows(r.block_out, ROW_TILE)])

    return types.SimpleNamespace(**locals())


def back_kernel(together, att_scale, names, *refs):
    r = types.SimpleNamespace(**dict(zip(names, refs)))
    if together:
        r.back_sent, r.returned = r.back_sent_cols, r.returned_cols
    do = back_stages(r, att_scale)
    if not together:
        do.clear()
        do.feed_first()
        do.reduce_part()
        do.feed_hidden()
        do.expand_part()
        do.feed_normed()
        do.feed_last()
        do.cross_part()
        do.cross_given()
        do.cross_attention()
        do.query_part()
        do.memory_part()
        do.context_back()
        do.query_back()
        do.spatial_first()
        do.output_part()
        do.spatial_given()
        do.spatial_attention()
        do.input_part()
        do.attend_normed()
        do.attend_last()
        return
    column, frame, depth, core, across_x, across_y, sibling = neighbours()
    far = 3 - column
    frame_peers = [(column, (frame + shift) % 8) for shift in range(1, 8)]
    line_peers = [(column, ((depth + shift) % 4) * 2 + core) for shift in range(1, 4)]
    plane_peers = [(across_x, frame), (across_y, frame), (far, frame)]
    greet(frame_peers + plane_peers)
    copies = Copies(r.send_sems, r.recv_sems)
    talls, bundles = PART_TALLS, len(PART_TALLS)
    cut = lambda ref, *span: ref.at[:, pl.ds(*span)]
    parts = [
        r.part_time,
        r.part_reduce,
        cut(r.part_expand, 0, 3584),
        cut(r.part_expand, 3584, 1024),
        cut(r.part_text, 0, 4 * r.low.shape[1]),
        cut(r.part_text, 4 * r.low.shape[1], 1536),
        cut(r.part_input, 0, 2048),
        cut(r.part_input, 2048, 1536),
    ]
    many = lambda name: [vars(r)[f"{name}_{index}"] for index in range(bundles)]
    halved, quartered, lined = (many(name) for name in LANDING)
    summed, crossed = halved, quartered
    outs = [
        r.share_time,
        r.share_reduce,
        cut(r.share_expand, 0, 3584),
        cut(r.share_expand, 3584, 1024),
        cut(r.share_text, 0, 4 * r.low.shape[1]),
        cut(r.share_text, 4 * r.low.shape[1], 1536),
        cut(r.share_input, 0, 2048),
        cut(r.share_input, 2048, 1536),
    ]

    def part_piece(index, unit, slot):
        ref = parts[index]
        if talls[index]:
            high = ref.shape[0] // 16
            return rows_at(ref, slot * (4 * high) + unit * high, high, high)
        high, wide = ref.shape[0] // 4, ref.shape[1] // 4
        return ref.at[
            pl.ds(pl.multiple_of(slot * high, high), high),
            pl.ds(pl.multiple_of(unit * wide, LANES), wide),
        ]

    left_high = r.left_own.shape[0]
    piece_high = left_high // 4

    def swap_rows(source, target):
        high = source.shape[0] // 8
        return [
            copies.start(
                rows_at(source, (slot * 2 + 1 - core) * high, high, high),
                target.at[pl.ds(slot * high, high)],
                (column, sibling),
            )
            for slot in range(4)
        ]

    def swap(source, target):
        return copies.start(source, target, (column, sibling))

    def left_start(source, other, rows_got):
        arrive(rows_got)
        deep = pl.ds(0, source.shape[1])
        started = [
            pltpu.make_async_copy(
                rows_at(source, (slot * 2 + core) * piece_high, piece_high, piece_high),
                r.left_own.at[pl.ds(slot * piece_high, piece_high), deep],
                r.left_sems.at[slot],
            )
            for slot in range(4)
        ]
        started.append(pltpu.make_async_copy(other, r.left_other.at[:, deep], r.left_sems.at[4]))
        for copy in started:
            copy.start()
        return started

    def arrive(got):
        for copy in got:
            copy.wait_recv()

    def finish_left(started):
        for copy in started:
            copy.wait()

    def part(started, right, got, other, target, size, count, place, first=0, deep=None):
        finish_left(started)
        if got is not None:
            got.wait_recv()
        deep = r.left_own.shape[1] if deep is None else deep

        def body(block, out):
            columns = tile_rows(pl.program_id(0) + first, size)
            total = dot_plain(r.left_own[:, 0:deep], right[:, columns])
            total = total + dot_plain(r.left_other[:, 0:deep], block[...])
            out[...] = total.astype(jnp.bfloat16)

        run_tiles(
            body,
            count,
            [(other, (other.shape[0], size), lambda step: (0, step + first))],
            [(target, (left_high, size), lambda step: (0, step + place))],
        )

    def part_reduce(got):
        got.wait_recv()
        arrive(hidden_got)
        high = r.part_reduce.shape[0] // 4

        def body(own, other, given, out):
            total = dot_plain(own[...], r.low[...]) + dot_plain(other[...], given[...])
            out[...] = total.astype(jnp.bfloat16)

        own = r.hidden_turned.at[pl.ds(pl.multiple_of(core * high, high), 7 * high)]
        run_tiles(
            body,
            4,
            [
                (own, (high, own.shape[1]), lambda step: (2 * step, 0)),
                by_rows(r.other_hidden, high),
                (r.given_feed, r.given_feed.shape, lambda step: (0, 0)),
            ],
            [by_rows(r.part_reduce, high)],
        )

    def part_output(started, got):
        finish_left(started)
        got.wait_recv()
        width = r.low.shape[1]

        def body(given, out):
            total = dot_plain(r.left_own[...], r.low[...])
            total = total + dot_plain(r.left_other[...], given[...])
            out[:, 0:width] = total.astype(jnp.bfloat16)
            out[:, width:] = jnp.zeros_like(out[:, width:])

        wide = r.part_text.shape[1] // 4
        run_tiles(
            body,
            1,
            [(r.given_output, r.given_output.shape, lambda step: (0, 0))],
            [(r.part_text, (left_high, wide), lambda step: (0, 3))],
        )

    def stream(index, count, left_at, right_at, out_at):
        wide = pl.ds(0, halved[index].shape[-1])
        buffers = [ref.at[:, :, wide] for ref in (r.left_buf, r.right_buf, r.out_buf)]
        add_stream(count, left_at, right_at, out_at, *buffers, r.stream_sems)

    from_half, from_quarter, from_line, ends = {}, {}, {}, []

    def go(index):
        if index == LINE_FIRST:
            for shift in range(1, 4):
                other = (depth + shift) % 4
                for unit in range(4):
                    from_line[index, shift, unit] = copies.start(
                        part_piece(index, unit, other),
                        lined[index].at[shift - 1, unit],
                        (column, other * 2 + core),
                    )
            return
        for slot in range(4):
            near = across_x if slot < 2 else across_y
            for which, unit in enumerate((near, far)):
                from_half[index, slot, which] = copies.start(
                    part_piece(index, unit, slot), halved[index].at[slot, which], (near, frame)
                )

    def half(index):
        for slot in range(4):
            for which in range(2):
                from_half[index, slot, which].wait_recv()

        def source(step):
            slot, which = step // 2, step % 2
            late = slot // 2
            unit = column + which * (
                (1 - late) * (across_y - column) + late * (across_x - column)
            )
            return part_piece(index, unit, slot)

        place = lambda step: halved[index].at[step // 2, step % 2]
        stream(index, 8, source, place, place)
        for slot in range(4):
            near = across_y if slot < 2 else across_x
            from_quarter[index, slot] = copies.start(
                halved[index].at[slot, 1], quartered[index].at[slot], (near, frame)
            )

    def quarter(index):
        for slot in range(4):
            from_quarter[index, slot].wait_recv()
        place = lambda slot: quartered[index].at[slot]
        stream(index, 4, lambda slot: halved[index].at[slot, 0], place, place)
        for shift in range(1, 4):
            other = (depth + shift) % 4
            from_line[index, shift] = copies.start(
                quartered[index].at[other], lined[index].at[shift - 1], (column, other * 2 + core)
            )

    def totals_of_four(count, sources, target, height, width):
        box = (pl.ds(0, height), pl.ds(0, width))

        def loads(index):
            slot = index % 2
            return [
                pltpu.make_async_copy(
                    source, r.four_buf.at[(slot, place) + box], r.four_sems.at[slot, place]
                )
                for place, source in enumerate(sources(index))
            ]

        def store(index):
            slot = index % 2
            return pltpu.make_async_copy(
                r.out_buf.at[(slot,) + box], target(index), r.stream_sems.at[2, slot]
            )

        waiting = loads(0)
        for copy in waiting:
            copy.start()
        for index in range(count):
            ahead = loads(index + 1) if index + 1 < count else []
            for copy in ahead:
                copy.start()
            for copy in waiting:
                copy.wait()
            waiting = ahead
            if index >= 2:
                store(index - 2).wait()
            slot = index % 2
            total = r.four_buf[slot, 0, 0:height, 0:width].astype(jnp.float32)
            for place in range(1, 4):
                total = total + r.four_buf[slot, place, 0:height, 0:width].astype(jnp.float32)
            r.out_buf[slot, 0:height, 0:width] = total.astype(jnp.bfloat16)
            store(index).start()
        for index in range(max(0, count - 2), count):
            store(index).wait()

    def total_of_four(own, others, target, height, width):
        totals_of_four(1, lambda index: [own] + others, lambda index: target, height, width)

    spread, relayed = {}, []

    def hand_out(index):
        target = share_unit(outs[index], talls[index], column)
        spread[index] = [copies.start(target, target, peer) for peer in plane_peers[:2]]
        if index >= bundles - 3:
            ends.extend(spread[index])
            ends.append(copies.start(target, target, plane_peers[2]))

    def relay(index):
        x_first = index % 2 == 0
        first, second = spread[index] if x_first else spread[index][::-1]
        first.wait_recv()
        target = share_unit(outs[index], talls[index], across_x if x_first else across_y)
        ends.append(copies.start(target, target, plane_peers[1 if x_first else 0]))
        ends.append(second)

    def line_sums():
        index = LINE_FIRST
        for shift in range(1, 4):
            for unit in range(4):
                from_line[index, shift, unit].wait_recv()
        totals_of_four(
            4,
            lambda unit: [part_piece(index, unit, depth)]
            + [lined[index].at[slot, unit] for slot in range(3)],
            lambda unit: summed[index].at[unit],
            *lined[index].shape[2:],
        )
        for slot, peer in enumerate(plane_peers):
            from_half[index, slot] = copies.start(
                summed[index].at[peer[0]], crossed[index].at[slot], peer
            )

    def line_last():
        index = LINE_FIRST
        for slot in range(3):
            from_half[index, slot].wait_recv()
        total_of_four(
            summed[index].at[column],
            [crossed[index].at[slot] for slot in range(3)],
            share_unit(outs[index], talls[index], column),
            *lined[index].shape[2:],
        )
        hand_out(index)

    def line(index):
        for shift in range(1, 4):
            from_line[index, shift].wait_recv()
        total_of_four(
            quartered[index].at[depth],
            [lined[index].at[slot] for slot in range(3)],
            share_unit(outs[index], talls[index], column),
            *lined[index].shape[1:],
        )
        hand_out(index)

    contexts, paired_contexts, texts = [], [], []
    text_rows = r.text_part.shape[0] // 4

    def context_send():
        contexts.extend(
            copies.start(r.back_context, r.context_all.at[frame], peer) for peer in line_peers
        )
        paired_contexts.append(
            copies.start(r.back_context, r.context_all.at[frame], (column, sibling))
        )
        move(r.back_context, r.held_context, r.context_all.at[frame])

    def context_pair():
        for shift, copy in zip(range(1, 4), contexts):
            copy.wait_recv()
            place = r.context_all.at[((depth + 4 - shift) % 4) * 2 + core]
            paired_contexts.append(copies.start(place, place, (column, sibling)))

    def text_part():
        for copy in paired_contexts:
            copy.wait_recv()
        each = r.context_all.shape[1]

        def body(text, context, out):
            total = dot_plain(text[:, 0:each], context[0])
            for index in range(1, 8):
                total = total + dot_plain(text[:, index * each : (index + 1) * each], context[index])
            out[...] = total.astype(jnp.bfloat16)

        run_tiles(
            body,
            4,
            [
                by_rows(r.text_turned, text_rows),
                (r.context_all, r.context_all.shape, lambda step: (0, 0, 0)),
            ],
            [by_rows(r.text_part, text_rows)],
        )
        for slot, peer in enumerate(plane_peers):
            texts.append(
                copies.start(
                    rows_at(r.text_part, peer[0] * text_rows, text_rows, text_rows),
                    r.text_got.at[slot],
                    peer,
                )
            )

    def text_line():
        for copy in texts:
            copy.wait_recv()
        total_of_four(
            rows_at(r.text_part, column * text_rows, text_rows, text_rows),
            [r.text_got.at[slot] for slot in range(3)],
            rows_at(r.text_out, column * text_rows, text_rows, text_rows),
            *r.text_got.shape[1:],
        )
        target = rows_at(r.text_out, column * text_rows, text_rows, text_rows)
        for peer in plane_peers:
            ends.append(copies.start(target, target, peer))

    cots_got, back_got, result_got, rows_got, rows_paired = [], [], [], [], []
    here = r.local_sems

    def move(source, held, target):
        load = pltpu.make_async_copy(source, held, here.at[0])
        load.start()
        load.wait()
        store = pltpu.make_async_copy(held, target, here.at[0])
        store.start()
        store.wait()

    def cols_send(source, target, got):
        for peer in frame_peers:
            got.append(copies.start(source.at[peer[1]], target.at[:, frame], peer))
        move(source.at[frame], r.held_cols, target.at[:, frame])

    def return_send(source, target, got):
        for peer in frame_peers:
            got.append(copies.start(source.at[:, peer[1]], target.at[frame], peer))
        move(source.at[:, frame], r.held_cols, target.at[frame])

    def rows_send():
        for peer in line_peers:
            rows_got.append(copies.start(r.row_sums, r.rows_all.at[frame], peer))
        rows_paired.append(copies.start(r.row_sums, r.rows_all.at[frame], (column, sibling)))
        r.rows_all[frame] = r.row_sums[...]

    def rows_pair():
        for shift, copy in zip(range(1, 4), rows_got):
            copy.wait_recv()
            place = r.rows_all.at[((depth + 4 - shift) % 4) * 2 + core]
            rows_paired.append(copies.start(place, place, (column, sibling)))

    def rows_plane():
        arrive(rows_paired)
        mods = r.rows_all.at[:, pl.ds(0, 8)]
        own = [pltpu.make_async_copy(mods, r.mods_out.at[column], here.at[0])]
        for peer in plane_peers:
            ends.append(copies.start(mods, r.mods_out.at[column], peer))
        r.sums[...] = jnp.sum(r.rows_all[:, 8:, :], axis=0)
        own.append(pltpu.make_async_copy(r.sums, r.sums_out.at[column], here.at[1]))
        for copy in own:
            copy.start()
        for peer in plane_peers:
            ends.append(copies.start(r.sums, r.sums_out.at[column], peer))
        for copy in own:
            copy.wait()

    wide = r.low.shape[1]
    third = wide // 3
    cols_send(r.cot_rows, r.cot_cols, cots_got)
    hidden_got = swap_rows(r.hidden_turned, r.other_hidden)
    feed_got = swap_rows(r.feed_turned, r.other_feed)
    cross_got = swap_rows(r.cross_turned, r.other_cross)
    after_got = swap_rows(r.after_turned, r.other_after)
    text_got = swap_rows(r.context_turned, r.other_context)
    spatial_got = swap_rows(r.spatial_turned, r.other_spatial)
    attend_got = swap_rows(r.attend_turned, r.other_attend)
    do.clear()
    r.row_sums[ROW.condition : ROW.condition + 1, :] = r.vectors[6:7, :]
    do.time_first()
    time_got = swap_rows(r.time_turned, r.other_time)
    do.time_heads()
    do.time_attention()
    middle_got = swap_rows(r.middle_turned, r.other_middle)
    arrive(cots_got)
    do.time_given()
    time_out = swap(r.low, r.given_time_out)
    do.time_attention_back()
    time_in = swap(r.broad.at[:, pl.ds(0, 3 * wide)], r.given_time_in)
    do.time_normed()
    do.time_last()
    return_send(r.time_back, r.back_sent_cols, back_got)
    held = left_start(r.middle_turned, r.other_middle, middle_got)
    part(held, r.low, time_out, r.given_time_out, r.part_time, third, 3, 9)
    held = left_start(r.time_turned, r.other_time, time_got)
    part(held, r.broad, time_in, r.given_time_in, r.part_time, third, 9, 0)
    go(0)
    held = left_start(r.feed_turned, r.other_feed, feed_got)
    do.time_result()
    arrive(back_got)
    return_send(r.time_result, r.returned_cols, result_got)
    copies.release(time_out)
    do.feed_first()
    feed = swap(r.low, r.given_feed)
    part_reduce(feed)
    go(1)
    half(0)
    copies.release(time_in)
    do.feed_hidden()
    hidden = swap(r.broad, r.given_hidden)
    do.feed_normed()
    part(held, r.broad, hidden, r.given_hidden, r.part_expand, 512, 9, 0)
    go(2)
    go(3)
    quarter(0)
    half(1)
    held = left_start(r.cross_turned, r.other_cross, cross_got)
    copies.release(feed)
    do.feed_last()
    cross = swap(r.low, r.given_cross)
    copies.release(hidden)
    do.cross_given()
    part(held, r.low, cross, r.given_cross, r.part_text, third, 3, 9)
    held = left_start(r.after_turned, r.other_after, after_got)
    do.cross_attention()
    query = swap(r.broad.at[:, pl.ds(0, wide)], r.given_query)
    memory = swap(r.memory, r.given_memory)
    half(2)
    quarter(1)
    do.context_back()
    context_send()
    part(held, r.broad, query, r.given_query, r.part_text, third, 3, 0)
    held = left_start(r.context_turned, r.other_context, text_got)
    do.query_back()
    deep = r.memory.shape[0]
    part(held, r.memory, memory, r.given_memory, r.part_text, third, 6, 3, 0, deep)
    go(4)
    held = left_start(r.spatial_turned, r.other_spatial, spatial_got)
    line(0)
    copies.release(cross)
    do.spatial_first()
    output = swap(r.low, r.given_output)
    quarter(2)
    copies.release(query)
    do.spatial_given()
    part_output(held, output)
    go(5)
    held = left_start(r.attend_turned, r.other_attend, attend_got)
    line_sums()
    relay(0)
    line(1)
    do.spatial_attention()
    inputs = swap(r.broad.at[:, pl.ds(0, r.given_input.shape[1])], r.given_input)
    half(4)
    line_last()
    context_pair()
    do.attend_normed()
    part(held, r.broad, inputs, r.given_input, r.part_input, 512, 4, 0)
    go(6)
    part([], r.broad, None, r.given_input, r.part_input, 512, 3, 4, 4)
    go(7)
    half(5)
    quarter(4)
    arrive(result_got)
    do.block_last()
    do.attend_last()
    rows_send()
    line(2)
    relay(1)
    half(6)
    quarter(5)
    half(7)
    rows_pair()
    text_part()
    quarter(6)
    quarter(7)
    line(4)
    relay(2)
    relay(3)
    rows_plane()
    text_line()
    line(5)
    line(6)
    line(7)
    relay(4)
    for copy in ends:
        copy.wait_recv()
    copies.finish()


LANDING = ("halved", "quartered", "lined")
PART_TALLS = (False, True, False, False, False, False, False, False)
LINE_FIRST = 3


def backward(att_scale, together, o, text_turned):
    anywhere = pl.BlockSpec(memory_space=pl.ANY)
    inside = pl.BlockSpec(memory_space=pltpu.VMEM)
    tokens, width = o.cotangent.shape
    hidden = o.gelu_slope.shape[1]
    text_count = o.cross_keys.shape[1]
    low, full = jnp.bfloat16, jnp.float32
    shape = jax.ShapeDtypeStruct
    third = width // 3
    hbm_out = dict(
        part_reduce=shape((hidden, width), low),
        part_expand=shape((width, hidden), low),
        part_text=shape((width, 5 * width + third), low),
        part_input=shape((width, 3 * width + LANES), low),
        back_context=shape((text_count, width), low),
        tokens_out=shape((tokens, width), low),
    )
    scratch = dict(
        running=pltpu.VMEM((tokens, width), full),
        wide=pltpu.VMEM((tokens, width), full),
        low=pltpu.VMEM((tokens, width), low),
        broad=pltpu.VMEM((tokens, hidden), low),
        head_in=pltpu.VMEM((HEADS, tokens, HEAD_LANES), low),
        head_query=pltpu.VMEM((HEADS, tokens, HEAD_LANES), low),
        head_key=pltpu.VMEM((HEADS, tokens, HEAD_LANES), low),
        head_value=pltpu.VMEM((HEADS, tokens, HEAD_LANES), low),
        cross_key=pltpu.VMEM((HEADS, text_count, HEAD_LANES), low),
        cross_value=pltpu.VMEM((HEADS, text_count, HEAD_LANES), low),
        memory=pltpu.VMEM((text_count, 2 * width), low),
    )
    hbm_in = dict(
        whole_spatial=o.whole_spatial,
        whole_text=o.whole_text,
        whole_expand=o.whole_expand,
        whole_reduce=o.whole_reduce,
        cotangent=o.cotangent,
        branch_feed=o.branch_feed,
        hidden_turned=o.hidden_turned,
        gelu_slope=o.gelu_slope,
        feed_turned=o.feed_turned,
        feed_normal=o.feed_normal,
        cross_turned=o.cross_turned,
        cross_queries=o.cross_queries,
        cross_keys=o.cross_keys,
        cross_values=o.cross_values,
        after_turned=o.after_turned,
        context_turned=o.context_turned,
        branch_attend=o.branch_attend,
        spatial_turned=o.spatial_turned,
        queries=o.queries,
        keys=o.keys,
        values=o.values,
        attend_turned=o.attend_turned,
        attend_normal=o.attend_normal,
    )
    vmem_in = dict(
        mods=o.mods,
        feed_rate=o.feed_rate,
        attend_rate=o.attend_rate,
        cross_logsum=o.cross_logsum,
        spatial_logsum=o.spatial_logsum,
        text_mask=o.text_mask,
    )
    if not together:
        hbm_in.update(back_sent=o.back_sent)
    vmem_out = dict(row_sums=shape((ROW.high, width), full))
    if together:
        hbm_in.update(
            time_cols=o.time_cols,
            cot_rows=o.cot_rows,
            whole_time=o.whole_time,
            after_feed=o.after_feed,
            text_turned=text_turned,
        )
        vmem_in.update(vectors=o.vectors, time_keep=o.time_keep, time_mask=o.time_mask)
        rows = o.cot_rows.shape
        cols = (rows[1], rows[0]) + rows[2:]
        hbm_out.update(cot_cols=shape(cols, low))
        half = lambda full: shape((full.shape[0] // 2, full.shape[1]), low)
        hbm_out.update(
            part_time=shape((width // 2, 4 * width), low),
            part_reduce=half(hbm_out["part_reduce"]),
            part_expand=half(hbm_out["part_expand"]),
            part_text=half(hbm_out["part_text"]),
            part_input=half(hbm_out["part_input"]),
            other_time=shape((width // 2, tokens), low),
            other_middle=shape((width // 2, tokens), low),
            other_hidden=half(o.hidden_turned),
            other_feed=half(o.feed_turned),
            other_cross=half(o.cross_turned),
            other_after=half(o.after_turned),
            other_context=half(o.context_turned),
            other_spatial=half(o.spatial_turned),
            other_attend=half(o.attend_turned),
            given_time_out=shape((tokens, width), low),
            given_time_in=shape((tokens, 3 * width), low),
            given_feed=shape((tokens, width), low),
            given_hidden=shape((tokens, hidden), low),
            given_cross=shape((tokens, width), low),
            given_query=shape((tokens, width), low),
            given_memory=shape((text_count, 2 * width), low),
            given_output=shape((tokens, width), low),
            given_input=shape((tokens, 3 * width + LANES), low),
        )
        hbm_out.update(time_result=shape(cols, low))
        hbm_out.update(time_back=shape(cols, low))
        hbm_out.update(back_sent_cols=shape(rows, low))
        hbm_out.update(returned_cols=shape(rows, low))
        hbm_out.update(block_out=shape((tokens, width), low))
        hbm_out.update(mods_out=shape((4, 8, 8, width), full))
        hbm_out.update(sums_out=shape((4, ROW.high - 8, width), full))
        high = width // 8
        wides = (width, width, 896, 256, width, third, 512, 384)
        high = width // 8
        for index, wide in enumerate(wides):
            piece = (high, wide)
            first = index == LINE_FIRST
            landing = [(4,) if first else (4, 2), (4,), (3, 4) if first else (3,)]
            for name, lead in zip(LANDING, landing):
                hbm_out[f"{name}_{index}"] = shape(lead + piece, low)
        hbm_out.update(
            share_time=shape((high, 4 * width), low),
            share_reduce=shape((4 * high, width), low),
            share_expand=shape((high, 4 * width), low),
            share_text=shape((high, 5 * width + third), low),
            share_input=shape((high, 3 * width + LANES), low),
        )
        text_shape = (text_turned.shape[0], width)
        hbm_out.update(context_all=shape((8, text_count, width), low))
        hbm_out.update(text_part=shape(text_shape, low))
        hbm_out.update(text_got=shape((3, text_shape[0] // 4, width), low))
        hbm_out.update(text_out=shape(text_shape, low))
        remote = 240
        piece = (high, width + third)
        scratch.update(
            send_sems=pltpu.SemaphoreType.DMA((remote,)),
            recv_sems=pltpu.SemaphoreType.DMA((remote,)),
            stream_sems=pltpu.SemaphoreType.DMA((3, PIECE_SLOTS)),
            local_sems=pltpu.SemaphoreType.DMA((2,)),
            left_own=pltpu.VMEM((width // 2, tokens), low),
            left_other=pltpu.VMEM((width // 2, tokens), low),
            left_sems=pltpu.SemaphoreType.DMA((5,)),
            left_buf=pltpu.VMEM((PIECE_SLOTS,) + piece, low),
            right_buf=pltpu.VMEM((PIECE_SLOTS,) + piece, low),
            out_buf=pltpu.VMEM((PIECE_SLOTS,) + piece, low),
            four_buf=pltpu.VMEM((2, 4) + piece, low),
            four_sems=pltpu.SemaphoreType.DMA((2, 4)),
            rows_all=pltpu.VMEM((8, ROW.high, width), full),
            sums=pltpu.VMEM((ROW.high - 8, width), full),
            time_normal=pltpu.VMEM((tokens, width), low),
            time_rate=pltpu.VMEM((tokens, LANES), full),
            time_turned=pltpu.VMEM((width, tokens), low),
            time_logsum=pltpu.VMEM((HEADS, 8, tokens), full),
            held_cols=pltpu.VMEM((cols[0],) + cols[2:], low),
            held_context=pltpu.VMEM((text_count, width), low),
            middle=pltpu.VMEM((tokens, width), low),
            middle_turned=pltpu.VMEM((width, tokens), low),
        )
    names = list(hbm_in) + list(vmem_in) + list(hbm_out) + list(vmem_out) + list(scratch)
    results = pl.pallas_call(
        functools.partial(back_kernel, together, att_scale, names),
        out_shape=list(hbm_out.values()) + list(vmem_out.values()),
        in_specs=[anywhere] * len(hbm_in) + [inside] * len(vmem_in),
        out_specs=[anywhere] * len(hbm_out) + [inside] * len(vmem_out),
        scratch_shapes=list(scratch.values()),
        compiler_params=pltpu.CompilerParams(
            collective_id=1 if together else None,
            has_side_effects=True,
            vmem_limit_bytes=60 * 1024 * 1024,
        ),
        name="backward",
    )(*hbm_in.values(), *vmem_in.values())
    return types.SimpleNamespace(**dict(zip(list(hbm_out) + list(vmem_out), results)))


def one_slice():
    return lax.axis_size("clip") == 4 and lax.axis_size("frame") == 8


def sum_shares(group):
    def total(part):
        return lax.psum(lax.psum_scatter(part, "frame", scatter_dimension=0, tiled=True), "clip")

    return jnp.concatenate([total(part) for part in group], axis=1)


FORWARD_TALLS = (False, True, False, False, True, False)
VEC = types.SimpleNamespace(
    spatial=0, cross=1, reduce=2, gain=3, shift=4, temporal=5, gate=6, expand=7, high=16
)


def forward_stages(r, att_scale):
    tokens, width = r.low.shape
    head_size = width // HEADS
    third = width // 3
    tile = tokens // 4
    plain = jnp.float32
    row = lambda which: r.rows_low[which : which + 1, :]

    def clear():
        for heads in (r.head_query, r.head_key, r.head_value, r.cross_key, r.cross_value):
            heads[...] = jnp.zeros_like(heads)

    def sum_mods():
        r.mods[...] = jnp.sum(r.mods_got[...], axis=0)

    def sum_rows():
        r.rows_low[...] = jnp.sum(r.rows_got[...].astype(plain), axis=0)
        for unit in range(4):
            r.rows_expand[0:1, unit * width : (unit + 1) * width] = row(VEC.expand + unit)

    def turn_out(source, target):
        height = source.shape[0] // target.shape[1] * LANES

        def body(out):
            rows = tile_rows(pl.program_id(0), LANES)
            out[...] = source[rows, :].astype(plain).T.astype(jnp.bfloat16)

        run_tiles(body, target.shape[1] // LANES, [], [by_columns(target, LANES)])

    def normed(values, rate_out, rows, shift, scale):
        values = values - jnp.mean(values, axis=1, keepdims=True)
        rate = lax.rsqrt(jnp.mean(values * values, axis=1, keepdims=True) + eps_norm)
        normal = values * rate
        rate_out[rows, :] = jnp.broadcast_to(rate, (tile, LANES))
        shift, scale = (r.mods[which : which + 1, :] for which in (shift, scale))
        r.low[rows, :] = (normal * (1.0 + scale) + shift).astype(jnp.bfloat16)
        return normal.astype(jnp.bfloat16)

    def attend_first():
        def body(latents, out):
            rows = tile_rows(pl.program_id(0), tile)
            values = latents[...].astype(plain)
            out[...] = normed(values, r.attend_rate, rows, ROW.shift_a, ROW.scale_a)

        run_tiles(body, 4, [by_rows(r.latents, tile)], [by_rows(r.attend_normal, tile)])
        turn_out(r.low, r.attend_turned)

    def through(weight, place, count, left, target, size=third):
        def body(block):
            columns = tile_rows(pl.program_id(0), size)
            target(columns, dot_plain(left(), block[...]))

        high = weight.shape[0]
        run_tiles(body, count, [(weight, (high, size), lambda step: (0, place + step))], [])

    def set_broad(columns, value):
        r.broad[:, columns] = value.astype(jnp.bfloat16)

    def set_memory(columns, value):
        r.memory[:, columns] = value.astype(jnp.bfloat16)

    def attend_heads():
        through(r.whole_spatial, 0, 9, lambda: r.low[...], set_broad)
        for place, heads in enumerate((r.head_query, r.head_key, r.head_value)):
            split_heads(r.broad, place * width, heads, head_size, HEADS)

    def attention(queries, keys, values, mask, logsum, outs, first=0, last=HEADS):
        def step(head, carry):
            query, key, value = queries[head], keys[head], values[head]
            scores = dot_rows(key, query) * att_scale
            if mask is not None:
                scores = scores + mask[:, 0:1]
            largest = jnp.max(scores, axis=0, keepdims=True)
            total = jnp.sum(jnp.exp(scores - largest), axis=0, keepdims=True)
            logs = largest + jnp.log(total)
            logsum[head, 0:1, :] = logs
            weights = jnp.exp(scores - logs).astype(jnp.bfloat16)
            turned = lax.dot_general(
                value, weights, (((0,), (0,)), ((), ())), preferred_element_type=plain
            )
            outs[head] = turned.T.astype(jnp.bfloat16)
            return carry

        lax.fori_loop(first, last, step, 0)

    def attend_attention(half):
        attention(
            r.head_query,
            r.head_key,
            r.head_value,
            None,
            r.spatial_logsum,
            r.head_out,
            half * HEADS // 2,
            (half + 1) * HEADS // 2,
        )

    def attend_merge():
        merge_heads(r.head_out, r.middle, 0, head_size, HEADS)
        turn_out(r.middle, r.spatial_turned)

    def attend_last():
        def body(weight, latents, branch):
            columns = tile_rows(pl.program_id(0), third)
            value = dot_plain(r.middle[...], weight[...])
            value = value + r.rows_low[VEC.spatial : VEC.spatial + 1, columns]
            branch[...] = value.astype(jnp.bfloat16)
            after = latents[...].astype(plain)
            after = after + r.mods[ROW.gate_a : ROW.gate_a + 1, columns] * value
            r.running[:, columns] = after
            r.low[:, columns] = after.astype(jnp.bfloat16)

        run_tiles(
            body,
            3,
            [
                (r.whole_spatial, (width, third), lambda step: (0, 9 + step)),
                by_columns(r.latents, third),
            ],
            [by_columns(r.branch_attend, third)],
        )
        turn_out(r.low, r.after_turned)

    def context():
        def body(weight):
            columns = tile_rows(pl.program_id(0), third)
            r.context[:, columns] = dot_plain(r.own_text[...], weight[...]).astype(jnp.bfloat16)

        run_tiles(body, 3, [by_columns(r.whole_context, third)], [])
        turn_out(r.context, r.context_turned)

    def cross_heads():
        through(r.whole_text, 3, 6, lambda: r.context[...], set_memory)
        split_heads(r.memory, 0, r.cross_key, head_size, HEADS)
        split_heads(r.memory, width, r.cross_value, head_size, HEADS)
        through(r.whole_text, 0, 3, lambda: r.low[...], set_broad)
        split_heads(r.broad, 0, r.cross_query, head_size, HEADS)

    def cross_attention():
        attention(
            r.cross_query, r.cross_key, r.cross_value, r.text_mask, r.cross_logsum, r.head_out
        )
        merge_heads(r.head_out, r.middle, 0, head_size, HEADS)
        turn_out(r.middle, r.cross_turned)

    def add_cross(columns, value):
        r.running[:, columns] += value + r.rows_low[VEC.cross : VEC.cross + 1, columns]

    def cross_last():
        through(r.whole_text, 9, 3, lambda: r.middle[...], add_cross)

    def feed_first():
        def body(out):
            rows = tile_rows(pl.program_id(0), tile)
            out[...] = normed(r.running[rows, :], r.feed_rate, rows, ROW.shift_m, ROW.scale_m)

        run_tiles(body, 4, [], [by_rows(r.feed_normal, tile)])
        turn_out(r.low, r.feed_turned)

    def feed_hidden():
        size = 512

        def body(weight, slope, turned):
            columns = tile_rows(pl.program_id(0), size)
            values = dot_plain(r.low[...], weight[...]) + r.rows_expand[0:1, columns]
            inner = math.sqrt(2.0 / math.pi)
            square = values * values
            bent = jnp.tanh(inner * values * (1.0 + 0.044715 * square))
            half = 0.5 * (1.0 + bent)
            hidden = values * half
            steep = inner * (1.0 + 3.0 * 0.044715 * square)
            slope[...] = (half + 0.5 * values * (1.0 - bent * bent) * steep).astype(jnp.bfloat16)
            r.broad[:, columns] = hidden.astype(jnp.bfloat16)
            turned[...] = hidden.T.astype(jnp.bfloat16)

        run_tiles(
            body,
            r.broad.shape[1] // size,
            [by_columns(r.whole_expand, size)],
            [by_columns(r.gelu_slope, size), by_rows(r.hidden_turned, size)],
        )

    def feed_last():
        def body(weight, branch, after, sent):
            columns = tile_rows(pl.program_id(0), third)
            value = dot_plain(r.broad[...], weight[...])
            value = value + r.rows_low[VEC.reduce : VEC.reduce + 1, columns]
            branch[...] = value.astype(jnp.bfloat16)
            value = r.running[:, columns] + r.mods[ROW.gate_m : ROW.gate_m + 1, columns] * value
            after[...] = value
            sent[...] = value.astype(jnp.bfloat16).reshape(sent.shape)

        shape = r.sent.shape
        run_tiles(
            body,
            3,
            [by_columns(r.whole_reduce, third)],
            [
                by_columns(r.branch_feed, third),
                by_columns(r.after_feed, third),
                (r.sent, shape[:3] + (third,), lambda step: (0, 0, 0, step)),
            ],
        )

    return types.SimpleNamespace(**locals())


def forward_kernel(att_scale, names, *refs):
    r = types.SimpleNamespace(**dict(zip(names, refs)))
    r.held = [
        r.held_spatial, r.held_context, r.held_text, r.held_expand, r.held_reduce, r.held_time
    ]
    do = forward_stages(r, att_scale)
    shares = [
        r.share_spatial, r.share_context, r.share_text, r.share_expand, r.share_reduce, r.share_time
    ]
    wholes = [
        r.whole_spatial, r.whole_context, r.whole_text, r.whole_expand, r.whole_reduce, r.whole_time
    ]
    talls, count = FORWARD_TALLS, len(FORWARD_TALLS)
    column, frame, depth, core, across_x, across_y, sibling = neighbours()
    frame_peers = [(column, (frame + shift) % 8) for shift in range(1, 8)]
    greet(frame_peers + [(across_x, frame), (across_y, frame)])
    copies = Copies(r.send_sems, r.recv_sems)
    locals_started = []

    def local(source, target):
        copy = pltpu.make_async_copy(source, target, r.local_sems.at[len(locals_started)])
        copy.start()
        locals_started.append(copy)
        return copy

    mods, rows, arrivals = [], [], {index: [] for index in range(count)}
    from_x, from_y, from_far, own_place = {}, {}, {}, {}

    def send_mods():
        own = local(r.mod_parts.at[frame], r.mods_got.at[frame])
        for peer in frame_peers:
            mods.append(copies.start(r.mod_parts.at[peer[1]], r.mods_got.at[frame], peer))
        own.wait()

    def send_rows():
        own = local(r.row_parts, r.rows_got.at[frame])
        for peer in frame_peers:
            rows.append(copies.start(r.row_parts, r.rows_got.at[frame], peer))
        own.wait()

    def send(index):
        share, whole, tall = shares[index], wholes[index], talls[index]
        own = whole_share(whole, tall, frame)
        held = r.held[index]
        load = local(share, held)
        arrivals[index].append(copies.start(share, own, (column, sibling)))
        own_place[index] = (load, held, own)

    def place(index):
        load, held, own = own_place[index]
        load.wait()
        own_place[index] = local(held, own)

    order = (
        jnp.where(depth == 0, 3, 1),
        jnp.where((depth == 0) | (depth == 3), 2, 3),
        jnp.where(depth == 0, 1, jnp.where(depth == 3, 3, 2)),
    )

    def next_frame(step):
        return jnp.clip(depth + step, 0, 3) * 2 + core

    def send_depth(index):
        share, whole, tall = shares[index], wholes[index], talls[index]
        source = share_unit(share, tall, column)
        target = whole_unit(whole, tall, column, frame)
        for step, shift in ((1, 1), (-1, 3)):
            copies.start_if(
                (depth < 3) if step == 1 else (depth > 0),
                source,
                target,
                (column, next_frame(step)),
                r.depth_sems.at[index, shift],
            )

    def pass_depth(index, shift):
        source = ((depth + 4 - shift) % 4) * 2 + core
        piece = whole_unit(wholes[index], talls[index], column, source)
        copies.start_if(
            (depth >= shift) & (depth < 3),
            piece,
            piece,
            (column, next_frame(1)),
            r.depth_sems.at[index, (shift + 1) % 4],
        )
        copies.start_if(
            (depth < shift) & (depth > 0),
            piece,
            piece,
            (column, next_frame(-1)),
            r.depth_sems.at[index, shift - 1],
        )

    def wait_depth(index, shift):
        source = ((depth + 4 - shift) % 4) * 2 + core
        piece = whole_unit(wholes[index], talls[index], column, source)
        pltpu.make_async_remote_copy(
            src_ref=piece,
            dst_ref=piece,
            send_sem=r.send_sems.at[0],
            recv_sem=r.depth_sems.at[index, shift],
            device_id=(column, sibling),
            device_id_type=MESH_ID,
        ).wait_recv()

    def pass_on(index, turn, unit, device):
        source = ((depth + 4 - order[turn]) % 4) * 2 + core
        piece = whole_unit(wholes[index], talls[index], unit, source)
        return copies.start(piece, piece, device)

    def first(index, turns=(0, 1, 2)):
        for turn in turns:
            wait_depth(index, order[turn])
            pass_depth(index, order[turn])
            from_x[index, turn] = pass_on(index, turn, column, (across_x, frame))
            from_y[index, turn] = pass_on(index, turn, column, (across_y, frame))
            arrivals[index].append(pass_on(index, turn, column, (column, sibling)))
        if index + 2 < count and turns[-1] == 2:
            send(index + 2)
            send_depth(index + 2)

    def second(index):
        for turn in range(3):
            x_first = (index + turn) % 2 == 0
            from_x[index, turn].wait_recv()
            if x_first:
                from_far[index, turn] = pass_on(index, turn, across_x, (across_y, frame))
            arrivals[index].append(pass_on(index, turn, across_x, (column, sibling)))
            from_y[index, turn].wait_recv()
            if not x_first:
                from_far[index, turn] = pass_on(index, turn, across_y, (across_x, frame))
            arrivals[index].append(pass_on(index, turn, across_y, (column, sibling)))

    def third(index):
        for turn in range(3):
            from_far[index, turn].wait_recv()
            arrivals[index].append(pass_on(index, turn, 3 - column, (column, sibling)))

    def ready(index):
        place(index)
        for copy in arrivals[index]:
            copy.wait_recv()
        own_place[index].wait()

    def arrive(got):
        for copy in got:
            copy.wait_recv()

    send_mods()
    for index in (0, 1):
        send(index)
        send_depth(index)
    do.clear()
    arrive(mods)
    do.sum_mods()
    do.attend_first()
    first(0)
    send_rows()
    second(0)
    first(1)
    third(0)
    ready(0)
    do.attend_heads()
    kept = [
        local(r.head_query, r.queries),
        local(r.head_key, r.keys),
        local(r.head_value, r.values),
    ]
    second(1)
    first(2, (0, 1))
    do.attend_attention(0)
    third(1)
    first(2, (2,))
    do.attend_attention(1)
    do.attend_merge()
    first(3, (0, 1))
    second(2)
    arrive(rows)
    do.sum_rows()
    do.attend_last()
    first(3, (2,))
    third(2)
    ready(1)
    do.context()
    second(3)
    ready(2)
    do.cross_heads()
    kept += [
        local(r.cross_query, r.cross_queries),
        local(r.cross_key, r.cross_keys),
        local(r.cross_value, r.cross_values),
    ]
    first(4, (0, 1))
    third(3)
    do.cross_attention()
    first(4, (2,))
    second(4)
    do.cross_last()
    do.feed_first()
    first(5, (0, 1))
    ready(3)
    do.feed_hidden()
    third(4)
    first(5, (2,))
    ready(4)
    do.feed_last()
    cols = []
    own = local(r.sent.at[frame], r.held_cols)
    for peer in frame_peers:
        cols.append(copies.start(r.sent.at[peer[1]], r.time_cols.at[:, frame], peer))
    own.wait()
    own = local(r.held_cols, r.time_cols.at[:, frame])
    second(5)
    third(5)
    ready(5)
    arrive(cols)
    own.wait()
    copies.finish()
    for copy in kept:
        copy.wait()


def forward(att_scale, o):
    anywhere = pl.BlockSpec(memory_space=pl.ANY)
    inside = pl.BlockSpec(memory_space=pltpu.VMEM)
    tokens, width = o.latents.shape
    text_count = o.own_text.shape[0]
    hidden = 4 * width
    low, full = jnp.bfloat16, jnp.float32
    shape = jax.ShapeDtypeStruct
    hbm_in = dict(
        share_spatial=o.share_spatial,
        share_context=o.share_context,
        share_text=o.share_text,
        share_expand=o.share_expand,
        share_reduce=o.share_reduce,
        share_time=o.share_time,
        latents=o.latents,
        mod_parts=o.mod_parts,
        row_parts=o.row_parts,
    )
    vmem_in = dict(own_text=o.own_text, text_mask=o.text_mask)
    heads = (HEADS, tokens, HEAD_LANES)
    text_heads = (HEADS, text_count, HEAD_LANES)
    whole = lambda share: shape((8 * share.shape[0], share.shape[1]), low)
    hbm_out = dict(
        whole_spatial=whole(o.share_spatial),
        whole_context=whole(o.share_context),
        whole_text=whole(o.share_text),
        whole_expand=whole(o.share_expand),
        whole_reduce=whole(o.share_reduce),
        whole_time=whole(o.share_time),
    )
    hbm_out.update(
        attend_normal=shape((tokens, width), low),
        attend_turned=shape((width, tokens), low),
        queries=shape(heads, low),
        keys=shape(heads, low),
        values=shape(heads, low),
        spatial_turned=shape((width, tokens), low),
        branch_attend=shape((tokens, width), low),
        after_turned=shape((width, tokens), low),
        context_turned=shape((width, text_count), low),
        cross_queries=shape(heads, low),
        cross_keys=shape(text_heads, low),
        cross_values=shape(text_heads, low),
        cross_turned=shape((width, tokens), low),
        feed_normal=shape((tokens, width), low),
        feed_turned=shape((width, tokens), low),
        gelu_slope=shape((tokens, hidden), low),
        hidden_turned=shape((hidden, tokens), low),
        branch_feed=shape((tokens, width), low),
        after_feed=shape((tokens, width), full),
        sent=shape((8, tokens // (8 * 16), 16, width), low),
        time_cols=shape((tokens // (8 * 16), 8, 16, width), low),
    )
    vmem_out = dict(
        mods=shape((8, width), full),
        rows_low=shape((VEC.high, width), full),
        attend_rate=shape((tokens, LANES), full),
        feed_rate=shape((tokens, LANES), full),
        spatial_logsum=shape((HEADS, 8, tokens), full),
        cross_logsum=shape((HEADS, 8, tokens), full),
    )
    remote = 21 + len(FORWARD_TALLS) * 30
    held = lambda share: pltpu.VMEM(share.shape, low)
    scratch = dict(
        running=pltpu.VMEM((tokens, width), full),
        low=pltpu.VMEM((tokens, width), low),
        middle=pltpu.VMEM((tokens, width), low),
        broad=pltpu.VMEM((tokens, hidden), low),
        head_query=pltpu.VMEM(heads, low),
        head_key=pltpu.VMEM(heads, low),
        head_value=pltpu.VMEM(heads, low),
        head_out=pltpu.VMEM(heads, low),
        cross_query=pltpu.VMEM(heads, low),
        cross_key=pltpu.VMEM(text_heads, low),
        cross_value=pltpu.VMEM(text_heads, low),
        memory=pltpu.VMEM((text_count, 2 * width), low),
        context=pltpu.VMEM((text_count, width), low),
        rows_expand=pltpu.VMEM((8, hidden), full),
        held_spatial=held(o.share_spatial),
        held_context=held(o.share_context),
        held_text=held(o.share_text),
        held_expand=held(o.share_expand),
        held_reduce=held(o.share_reduce),
        held_time=held(o.share_time),
        held_cols=pltpu.VMEM((tokens // (8 * 16), 16, width), low),
        mods_got=pltpu.VMEM((8, 8, width), full),
        rows_got=pltpu.VMEM((8, VEC.high, width), low),
        send_sems=pltpu.SemaphoreType.DMA((remote,)),
        recv_sems=pltpu.SemaphoreType.DMA((remote,)),
        depth_sems=pltpu.SemaphoreType.DMA((len(FORWARD_TALLS), 4)),
        local_sems=pltpu.SemaphoreType.DMA((4 + 2 * len(FORWARD_TALLS) + 6,)),
    )
    names = list(hbm_in) + list(vmem_in) + list(hbm_out) + list(vmem_out) + list(scratch)
    results = pl.pallas_call(
        functools.partial(forward_kernel, att_scale, names),
        out_shape=list(hbm_out.values()) + list(vmem_out.values()),
        in_specs=[anywhere] * len(hbm_in) + [inside] * len(vmem_in),
        out_specs=[anywhere] * len(hbm_out) + [inside] * len(vmem_out),
        scratch_shapes=list(scratch.values()),
        compiler_params=pltpu.CompilerParams(
            collective_id=0, has_side_effects=True, vmem_limit_bytes=60 * 1024 * 1024
        ),
        name="forward",
    )(*hbm_in.values(), *vmem_in.values())
    return types.SimpleNamespace(**dict(zip(list(hbm_out) + list(vmem_out), results)))


def pack_rows(parts, rows):
    flat = jnp.concatenate(parts, axis=-1)
    flat = jnp.pad(flat, [(0, 0)] * (flat.ndim - 1) + [(0, rows * LANES - flat.shape[-1])])
    return flat.reshape(flat.shape[:-1] + (rows, LANES))


def results(
    block_output, input_gradient, mods, sums, totals, text_total, frame_index, row_count, bias_width
):
    model_width = mods.shape[-1]
    high = lambda part: part.astype(jnp.float32)
    total_time, total_reduce, total_expand, total_text, total_spatial = totals
    rows_gradient = mods[:, :6].reshape(-1, 6 * model_width)
    rows_condition = lax.dynamic_slice_in_dim(
        mods[:, ROW.condition], frame_index * row_count, row_count, 1
    )
    back_modulation_weight = jnp.einsum(
        "nd,ne->de", rows_condition, rows_gradient, precision=lax.Precision.HIGHEST
    )
    back_modulation_bias = jnp.sum(
        lax.dynamic_slice_in_dim(rows_gradient, frame_index * bias_width, bias_width, 1), axis=0
    )
    own_rows = lax.dynamic_slice_in_dim(sums, frame_index * row_count, row_count, 1)
    own_row = lambda which: own_rows[which - 8]
    own_expand = lax.dynamic_slice_in_dim(
        sums[ROW.expand - 8 : ROW.expand - 4].reshape(-1), frame_index * 4 * row_count, 4 * row_count, 0
    )
    own_gate = lax.dynamic_slice_in_dim(
        jnp.sum(mods[:, ROW.gate_t], axis=0), frame_index * row_count, row_count, 0
    )
    vec_total = (
        own_row(ROW.spatial),
        own_row(ROW.cross),
        own_expand,
        own_row(ROW.reduce),
        own_row(ROW.gain),
        own_row(ROW.shift),
        own_row(ROW.temporal),
        own_gate,
    )
    matrix_totals = (
        high(total_spatial[:, : 3 * model_width]),
        high(total_text[:, 4 * model_width : 5 * model_width]),
        high(total_text[:, :model_width]),
        high(total_text[:, model_width : 3 * model_width]),
        high(total_text[:, 3 * model_width : 4 * model_width]),
        high(total_expand),
        high(total_reduce),
        high(total_time[:, : 3 * model_width]),
        high(total_time[:, 3 * model_width :]),
    )
    others = (back_modulation_weight, back_modulation_bias, high(text_total)) + tuple(vec_total)
    return (
        block_output,
        input_gradient,
        others[0],
        others[1],
        matrix_totals[0],
        matrix_totals[1],
        others[3],
        others[2],
        matrix_totals[2],
        matrix_totals[3],
        matrix_totals[4],
        others[4],
        matrix_totals[5],
        others[5],
        matrix_totals[6],
        others[6],
        others[7],
        others[8],
        matrix_totals[7],
        matrix_totals[8],
        others[9],
        others[10],
    )


def on_device(
    latents,
    cotangent,
    text_tokens,
    text_lengths,
    clip_frames,
    timesteps,
    motion_free,
    modulation_weight,
    modulation_bias,
    spatial_input,
    spatial_output,
    spatial_bias,
    text_projection,
    cross_query,
    cross_memory,
    cross_output,
    cross_bias,
    expand_weight,
    expand_bias,
    reduce_weight,
    reduce_bias,
    temporal_gain,
    temporal_shift,
    temporal_input,
    temporal_output,
    temporal_bias,
    temporal_gate,
):
    frame_count = lax.axis_size("frame")
    frame_index = lax.axis_index("frame")
    patch_count = latents.shape[2]
    model_width = latents.shape[3]
    head_size = model_width // HEADS
    att_scale = 1.0 / math.sqrt(head_size)
    slot_count = clip_frames.shape[1]
    text_count = text_tokens.shape[2]
    frame_ids = jnp.arange(frame_count, dtype=jnp.int32)
    clip_ids = assign_clips(clip_frames[0], frame_count)
    slot_ids = jnp.arange(slot_count, dtype=jnp.int32)
    own_clip = jnp.sum(jnp.where(frame_ids == frame_index, clip_ids, 0))
    own_onehot = (slot_ids == own_clip).astype(jnp.float32)
    own_keep = 1.0 - jnp.sum(jnp.where(slot_ids == own_clip, motion_free[0], 0)).astype(jnp.float32)
    own_length = jnp.sum(jnp.where(slot_ids == own_clip, text_lengths[0], 0))
    conditioning = embed_time(timesteps[0], model_width).astype(jnp.bfloat16)
    row_count = modulation_weight.shape[0]
    cond_rows = lax.dynamic_slice_in_dim(conditioning, frame_index * row_count, row_count, 1)
    bias_width = modulation_bias.shape[0]
    bias_placed = lax.dynamic_update_slice_in_dim(
        jnp.zeros((6 * model_width,), jnp.float32),
        modulation_bias.astype(jnp.float32),
        frame_index * bias_width,
        0,
    )
    modulation_part = (
        jnp.dot(cond_rows, modulation_weight, preferred_element_type=jnp.float32)
        + bias_placed[None, :]
    )
    share_rows = text_projection.shape[0]
    if one_slice():
        near = 16
        text_high = -(-text_count // LANES) * LANES
        frame_onehot = (clip_ids[:, None] == slot_ids[None, :]).astype(jnp.float32)
        frame_modulation = jnp.sum(frame_onehot[:, :, None] * modulation_part[None], axis=1)
        frame_modulation = frame_modulation.reshape(frame_count, 6, model_width)
        here = (frame_ids == frame_index).astype(jnp.bfloat16)
        shares = jnp.stack(
            [
                spatial_bias,
                cross_bias,
                reduce_bias,
                temporal_gain,
                temporal_shift,
                temporal_bias,
                temporal_gate,
            ]
        )
        row_parts = jnp.concatenate(
            [
                (shares[:, None] * here[None, :, None]).reshape(-1, model_width),
                (expand_bias[None] * here[:, None]).reshape(-1, model_width),
            ]
        )
        own_text = lax.dynamic_index_in_dim(text_tokens[0], own_clip, 0, keepdims=False)
        text_places = jnp.arange(text_high, dtype=jnp.int32) < own_length
        tokens = latents[0, 0]
        operands = dict(
            share_spatial=jnp.concatenate([spatial_input, spatial_output], axis=1),
            share_context=text_projection,
            share_text=jnp.concatenate([cross_query, cross_memory, cross_output], axis=1),
            share_expand=expand_weight,
            share_reduce=reduce_weight,
            share_time=jnp.concatenate([temporal_input, temporal_output], axis=1),
            latents=tokens,
            mod_parts=jnp.pad(frame_modulation, ((0, 0), (0, 2), (0, 0))),
            row_parts=jnp.pad(row_parts, ((0, VEC.high - row_parts.shape[0]), (0, 0))),
            own_text=jnp.pad(own_text, ((0, text_high - text_count), (0, 0))),
            text_mask=jnp.broadcast_to(
                jnp.where(text_places, 0.0, big_negative)[:, None], (text_high, LANES)
            ),
        )
        operands = types.SimpleNamespace(**operands)
        vars(operands).update(vars(forward(att_scale, operands)))
        keep_frames = 1.0 - jnp.sum(
            frame_onehot * motion_free[0].astype(jnp.float32)[None, :], axis=1
        )
        sequence = jnp.arange(frame_count * near, dtype=jnp.int32)
        same = (sequence[:, None] % near == sequence[None, :] % near) & (
            jnp.repeat(clip_ids, near)[:, None] == jnp.repeat(clip_ids, near)[None, :]
        )
        row_keep = jnp.tile(jnp.repeat(keep_frames, near), patch_count // (frame_count * near))
        rows = operands.rows_low
        own_conditioning = jnp.sum(own_onehot[:, None] * conditioning.astype(jnp.float32), axis=0)
        vars(operands).update(
            cotangent=cotangent[0, 0],
            cot_rows=cotangent[0, 0].reshape(operands.sent.shape),
            vectors=jnp.stack(
                [
                    rows[VEC.gain],
                    rows[VEC.shift],
                    rows[VEC.temporal],
                    rows[VEC.gate],
                    rows[VEC.gate] * own_keep,
                    jnp.full((model_width,), own_keep),
                    own_conditioning,
                    jnp.zeros((model_width,), jnp.float32),
                ]
            ),
            time_keep=jnp.broadcast_to(row_keep[:, None], (patch_count, LANES)),
            time_mask=jnp.where(same, 0.0, big_negative),
        )
        text_share = lax.dynamic_slice_in_dim(
            text_tokens[0], frame_index * text_projection.shape[0], text_projection.shape[0], 2
        )
        frame_text = jnp.pad(text_share, ((0, 0), (0, text_high - text_count), (0, 0)))
        text_turned = jnp.einsum("fs,stk->kft", frame_onehot.astype(jnp.bfloat16), frame_text)
        text_turned = text_turned.reshape(text_projection.shape[0], -1)
        got = backward(att_scale, True, operands, text_turned)
        return results(
            got.block_out[None, None],
            got.tokens_out[None, None],
            got.mods_out.reshape(-1, 8, model_width),
            jnp.sum(got.sums_out, axis=0),
            [got.share_time, got.share_reduce, got.share_expand, got.share_text, got.share_input],
            got.text_out,
            frame_index,
            row_count,
            bias_width,
        )
    text_share = lax.dynamic_slice_in_dim(
        text_tokens[0], frame_index * text_projection.shape[0], text_projection.shape[0], 2
    )
    own_text = lax.dynamic_index_in_dim(text_tokens[0], own_clip, 0, keepdims=False)
    vectors = (
        spatial_bias,
        cross_bias,
        expand_bias,
        reduce_bias,
        temporal_gain,
        temporal_shift,
        temporal_bias,
        temporal_gate,
    )
    vector_sizes = [vector.shape[0] for vector in vectors]
    vector_rows = -(-sum(vector_sizes) // (8 * LANES)) * 8
    packed_vectors = pack_rows([vector.astype(jnp.float32) for vector in vectors], vector_rows)
    mod_rows_high = -(-(6 * model_width) // (8 * LANES)) * 8
    frame_onehot = (clip_ids[:, None] == slot_ids[None, :]).astype(jnp.float32)
    frame_modulation = jnp.sum(frame_onehot[:, :, None] * modulation_part[None], axis=1)
    wholes, vecs, mods = gather_all(
        (
            text_projection,
            jnp.concatenate([spatial_input, spatial_output], axis=1),
            jnp.concatenate([cross_query, cross_memory, cross_output], axis=1),
            expand_weight,
            reduce_weight,
            jnp.concatenate([temporal_input, temporal_output], axis=1),
        ),
        packed_vectors,
        pack_rows([frame_modulation], mod_rows_high),
    )
    projection, whole_spatial, whole_text, whole_expand, whole_reduce, whole_time = wholes
    context = jnp.dot(own_text, projection, preferred_element_type=jnp.float32)
    own_modulation = jnp.sum(mods, axis=0).reshape(-1)[: 6 * model_width]
    shift_attend, scale_attend, gate_attend, shift_feed, scale_feed, gate_feed = jnp.split(
        own_modulation, 6
    )
    vecs = vecs.reshape(frame_count, -1)[:, : sum(vector_sizes)]
    vector_ends = [sum(vector_sizes[: index + 1]) for index in range(len(vector_sizes) - 1)]
    (
        whole_bias,
        whole_cross_bias,
        whole_expand_bias,
        whole_reduce_bias,
        whole_gain,
        whole_shift,
        whole_temporal_bias,
        whole_gate,
    ) = [part.reshape(-1) for part in jnp.split(vecs, vector_ends, axis=1)]
    whole_input, whole_output = whole_spatial[:, : 3 * model_width], whole_spatial[:, 3 * model_width :]
    whole_query = whole_text[:, :model_width]
    whole_memory = whole_text[:, model_width : 3 * model_width]
    whole_cross = whole_text[:, 3 * model_width :]
    whole_temporal, whole_temporal_out = whole_time[:, : 3 * model_width], whole_time[:, 3 * model_width :]
    tokens = latents[0, 0].astype(jnp.float32)
    attend_normal, attend_rate = normal_parts(tokens)
    normed_attend = (attend_normal * (1.0 + scale_attend) + shift_attend).astype(jnp.bfloat16)
    spatial_heads = jnp.dot(normed_attend, whole_input, preferred_element_type=jnp.float32).astype(
        jnp.bfloat16
    )
    spatial_heads = spatial_heads.reshape(patch_count, 1, 3, HEADS, head_size)
    spatial_att, spatial_logsum = attend(
        spatial_heads[:, :, 0], spatial_heads[:, :, 1], spatial_heads[:, :, 2], None, att_scale
    )
    spatial_low = spatial_att.reshape(patch_count, model_width).astype(jnp.bfloat16)
    branch_attend = jnp.dot(
        spatial_low, whole_output, preferred_element_type=jnp.float32
    ) + whole_bias.astype(jnp.float32)
    after_attend = tokens + gate_attend * branch_attend
    after_low = after_attend.astype(jnp.bfloat16)
    cross_heads = jnp.dot(after_low, whole_query, preferred_element_type=jnp.float32).astype(
        jnp.bfloat16
    )
    cross_heads = cross_heads.reshape(patch_count, 1, HEADS, head_size)
    context_low = context.astype(jnp.bfloat16)
    memory_heads = jnp.dot(context_low, whole_memory, preferred_element_type=jnp.float32).astype(
        jnp.bfloat16
    )
    memory_heads = memory_heads.reshape(text_count, 1, 2, HEADS, head_size)
    text_mask = (jnp.arange(text_count, dtype=jnp.int32) < own_length)[None, None, None, :]
    cross_att, cross_logsum = attend(
        cross_heads, memory_heads[:, :, 0], memory_heads[:, :, 1], text_mask, att_scale
    )
    cross_low = cross_att.reshape(patch_count, model_width).astype(jnp.bfloat16)
    branch_cross = jnp.dot(
        cross_low, whole_cross, preferred_element_type=jnp.float32
    ) + whole_cross_bias.astype(jnp.float32)
    after_cross = after_attend + branch_cross
    feed_normal, feed_rate = normal_parts(after_cross)
    normed_feed = (feed_normal * (1.0 + scale_feed) + shift_feed).astype(jnp.bfloat16)
    hidden_pre = jnp.dot(
        normed_feed, whole_expand, preferred_element_type=jnp.float32
    ) + whole_expand_bias.astype(jnp.float32)
    hidden_low = smooth_gelu(hidden_pre).astype(jnp.bfloat16)
    gelu_slope = slope_gelu(hidden_pre).astype(jnp.bfloat16)
    branch_feed = jnp.dot(
        hidden_low, whole_reduce, preferred_element_type=jnp.float32
    ) + whole_reduce_bias.astype(jnp.float32)
    after_feed = after_cross + gate_feed * branch_feed
    sent_low = after_feed.astype(jnp.bfloat16)
    low = lambda part: part.astype(jnp.bfloat16)
    gate_keep = whole_gate.astype(jnp.float32) * own_keep
    upstream = cotangent[0, 0].astype(jnp.float32)
    keep_frames = 1.0 - jnp.sum(frame_onehot * motion_free[0].astype(jnp.float32)[None, :], axis=1)
    time_mask = (clip_ids[:, None] == clip_ids[None, :])[None, None]
    gain_float = whole_gain.astype(jnp.float32)
    shift_float = whole_shift.astype(jnp.float32)
    columns = lax.all_to_all(sent_low[None], "frame", split_axis=1, concat_axis=0, tiled=True)
    frames_here = columns.shape[0]
    positions = columns.shape[1]
    normed_time = affine_norm(columns.astype(jnp.float32), gain_float, shift_float).astype(
        jnp.bfloat16
    )
    time_heads = jnp.einsum(
        "fpd,de->fpe", normed_time, whole_temporal, preferred_element_type=jnp.float32
    )
    time_heads = time_heads.astype(jnp.bfloat16).reshape(
        frames_here, positions, 3, HEADS, head_size
    )
    time_att, time_logsum = attend(
        time_heads[:, :, 0], time_heads[:, :, 1], time_heads[:, :, 2], time_mask, att_scale
    )
    time_low = time_att.reshape(frames_here, positions, model_width).astype(jnp.bfloat16)
    result = jnp.einsum(
        "fpd,de->fpe", time_low, whole_temporal_out, preferred_element_type=jnp.float32
    )
    result = result + whole_temporal_bias.astype(jnp.float32)
    result_low = result.astype(jnp.bfloat16)
    kept_state = (normed_time, time_heads, time_low, time_logsum)
    back_sent = (upstream * gate_keep).astype(jnp.bfloat16)
    back_columns = lax.all_to_all(back_sent[None], "frame", split_axis=1, concat_axis=0, tiled=True)
    normed_time, time_heads, time_low, time_logsum = kept_state
    frames_here, positions = (columns.shape[0], columns.shape[1])
    back_temporal_bias = jnp.sum(back_columns.astype(jnp.float32), axis=(0, 1))
    back_temporal_out = jnp.einsum(
        "fpd,fpe->de", time_low, back_columns, preferred_element_type=jnp.float32
    )
    back_time_att = jnp.einsum(
        "fpe,de->fpd", back_columns, whole_temporal_out, preferred_element_type=jnp.float32
    )
    back_time_att = back_time_att.astype(jnp.bfloat16).reshape(
        frames_here, positions, HEADS, head_size
    )
    back_time_queries, back_time_keys, back_time_values = attend_back(
        time_heads[:, :, 0],
        time_heads[:, :, 1],
        time_heads[:, :, 2],
        time_mask,
        att_scale,
        time_logsum,
        back_time_att,
    )
    back_time_heads = jnp.stack([back_time_queries, back_time_keys, back_time_values], axis=2)
    back_time_heads = back_time_heads.reshape(frames_here, positions, 3 * model_width).astype(
        jnp.bfloat16
    )
    back_temporal = jnp.einsum(
        "fpd,fpe->de", normed_time, back_time_heads, preferred_element_type=jnp.float32
    )
    back_normed = jnp.einsum(
        "fpe,de->fpd", back_time_heads, whole_temporal, preferred_element_type=jnp.float32
    )
    unused_norm, norm_back = jax.vjp(
        affine_norm, columns.astype(jnp.float32), gain_float, shift_float
    )
    back_inputs, back_gain, back_shift = norm_back(back_normed)
    returned, back_return = jnp.split(
        lax.all_to_all(
            jnp.concatenate([result_low, back_inputs.astype(jnp.bfloat16)], axis=2),
            "frame",
            split_axis=0,
            concat_axis=1,
            tiled=True,
        ),
        2,
        axis=2,
    )
    temporal_value = returned[0].astype(jnp.float32)
    block_output = (after_feed + gate_keep * temporal_value).astype(jnp.bfloat16)[None, None]
    back_gate = jnp.sum(upstream * temporal_value, axis=0) * own_keep
    text_high = -(-text_count // LANES) * LANES

    def padded_heads(heads, high):
        heads = jnp.transpose(heads[:, 0], (1, 0, 2))
        return jnp.pad(heads, ((0, 0), (0, high - heads.shape[1]), (0, HEAD_LANES - head_size)))

    padded_context = jnp.pad(context_low, ((0, text_high - text_count), (0, 0)))
    text_places = jnp.arange(text_high, dtype=jnp.int32) < own_length
    operands = dict(
        whole_spatial=whole_spatial,
        whole_text=whole_text,
        whole_expand=whole_expand,
        whole_reduce=whole_reduce,
        cotangent=cotangent[0, 0],
        branch_feed=low(branch_feed),
        hidden_turned=hidden_low.T,
        gelu_slope=gelu_slope,
        feed_turned=normed_feed.T,
        feed_normal=low(feed_normal),
        cross_turned=cross_low.T,
        cross_queries=padded_heads(cross_heads, patch_count),
        cross_keys=padded_heads(memory_heads[:, :, 0], text_high),
        cross_values=padded_heads(memory_heads[:, :, 1], text_high),
        after_turned=after_low.T,
        context_turned=padded_context.T,
        branch_attend=low(branch_attend),
        spatial_turned=spatial_low.T,
        queries=padded_heads(spatial_heads[:, :, 0], patch_count),
        keys=padded_heads(spatial_heads[:, :, 1], patch_count),
        values=padded_heads(spatial_heads[:, :, 2], patch_count),
        attend_turned=normed_attend.T,
        attend_normal=low(attend_normal),
        mods=jnp.pad(own_modulation.reshape(6, model_width), ((0, 2), (0, 0))),
        feed_rate=jnp.broadcast_to(feed_rate, (patch_count, LANES)),
        attend_rate=jnp.broadcast_to(attend_rate, (patch_count, LANES)),
        cross_logsum=jnp.broadcast_to(
            cross_logsum[0, :, None, :, 0], (HEADS, 8, patch_count)
        ),
        spatial_logsum=jnp.broadcast_to(
            spatial_logsum[0, :, None, :, 0], (HEADS, 8, patch_count)
        ),
        text_mask=jnp.broadcast_to(
            jnp.where(text_places, 0.0, big_negative)[:, None], (text_high, LANES)
        ),
    )
    own_conditioning = jnp.sum(own_onehot[:, None] * conditioning.astype(jnp.float32), axis=0)
    operands.update(back_sent=back_return[0])
    got = backward(att_scale, False, types.SimpleNamespace(**operands), None)
    input_gradient = got.tokens_out[None, None]
    rows = got.row_sums
    rows = rows.at[ROW.condition].set(own_conditioning).at[ROW.gate_t].set(back_gate)
    rows = rows.at[ROW.gain].set(back_gain).at[ROW.shift].set(back_shift)
    rows = rows.at[ROW.temporal].set(back_temporal_bias)
    mods = lax.all_gather(rows[:8], ("clip", "frame"), axis=0)
    sums = lax.psum(rows[8:], ("clip", "frame"))
    all_context = lax.all_gather(got.back_context[:text_count], "frame", axis=0)
    context_total = jnp.einsum("fs,ftd->std", frame_onehot, all_context.astype(jnp.float32))
    text_total = lax.psum(
        jnp.einsum(
            "stk,std->kd",
            text_share,
            low(context_total),
            preferred_element_type=jnp.float32,
        ).astype(jnp.bfloat16),
        "clip",
    )
    totals = [
        sum_shares((low(back_temporal), low(back_temporal_out))),
        sum_shares((got.part_reduce,)),
        sum_shares((got.part_expand,)),
        sum_shares((got.part_text,)),
        sum_shares((got.part_input,)),
    ]
    return results(
        block_output,
        input_gradient,
        mods,
        sums,
        totals,
        text_total,
        frame_index,
        row_count,
        bias_width,
    )


def solution(mesh):
    placed = (
        P("clip", "frame", None, None),
        P("clip", "frame", None, None),
        P("clip", None, None, None),
        P("clip", None),
        P("clip", None),
        P("clip", None),
        P("clip", None),
        P("frame", None),
        P("frame"),
        P("frame", None),
        P("frame", None),
        P("frame"),
        P("frame", None),
        P("frame", None),
        P("frame", None),
        P("frame", None),
        P("frame"),
        P("frame", None),
        P("frame"),
        P("frame", None),
        P("frame"),
        P("frame"),
        P("frame"),
        P("frame", None),
        P("frame", None),
        P("frame"),
        P("frame"),
    )
    return jax.shard_map(
        on_device,
        mesh=mesh,
        in_specs=placed,
        out_specs=(
            P("clip", "frame", None, None),
            P("clip", "frame", None, None),
            P("frame", None),
            P("frame"),
            P("frame", None),
            P("frame", None),
            P("frame"),
            P("frame", None),
            P("frame", None),
            P("frame", None),
            P("frame", None),
            P("frame"),
            P("frame", None),
            P("frame"),
            P("frame", None),
            P("frame"),
            P("frame"),
            P("frame"),
            P("frame", None),
            P("frame", None),
            P("frame"),
            P("frame"),
        ),
        check_vma=False,
    )
```

```python
import functools
import math
import types

import jax
import jax.numpy as jnp
from jax import lax
from jax.experimental import pallas as pl
from jax.experimental.pallas import tpu as pltpu
from jax.sharding import PartitionSpec as P

HEADS = 16


eps_norm = 1e-06
big_negative = -1e30


def assign_clips(frame_counts, frame_count):
    slot_count = frame_counts.shape[0]
    slot_ids = jnp.arange(slot_count, dtype=jnp.int32)
    longest = jnp.max(frame_counts)
    long_slot = jnp.min(jnp.where(frame_counts == longest, slot_ids, slot_count))
    frame_ids = jnp.arange(frame_count, dtype=jnp.int32)
    long_gaps = jnp.maximum(longest - 1, 1)
    frame_gaps = frame_count - 1
    step_index = (frame_ids * long_gaps + frame_gaps - 1) // frame_gaps
    on_long = step_index * frame_gaps // long_gaps == frame_ids
    long_marks = on_long.astype(jnp.int32)
    before_count = jnp.cumsum(long_marks) - long_marks
    order_rank = frame_ids - before_count
    rest_counts = jnp.where(slot_ids == long_slot, 0, frame_counts)
    rest_ends = jnp.cumsum(rest_counts)
    rest_ids = jnp.sum((rest_ends[None, :] <= order_rank[:, None]).astype(jnp.int32), axis=1)
    return jnp.where(on_long, long_slot, rest_ids)


def normalize(values):
    average = jnp.mean(values, axis=-1, keepdims=True)
    centred = values - average
    spread = jnp.mean(centred * centred, axis=-1, keepdims=True)
    return centred * lax.rsqrt(spread + eps_norm)


def normal_parts(values):
    average = jnp.mean(values, axis=-1, keepdims=True)
    centred = values - average
    rate = lax.rsqrt(jnp.mean(centred * centred, axis=-1, keepdims=True) + eps_norm)
    return centred * rate, rate


def modulate(values, offset, scaling):
    return normalize(values) * (1.0 + scaling) + offset


def affine_norm(values, norm_gain, offset):
    return normalize(values) * norm_gain + offset


def smooth_gelu(values):
    return jax.nn.gelu(values, approximate=True)


def slope_gelu(values):
    inner = math.sqrt(2.0 / math.pi)
    bent = jnp.tanh(inner * (values + 0.044715 * values * values * values))
    steep = inner * (1.0 + 3.0 * 0.044715 * values * values)
    return 0.5 * (1.0 + bent) + 0.5 * values * (1.0 - bent * bent) * steep


def embed_time(time_steps, model_width):
    half_width = model_width // 2
    frequency = jnp.exp(-math.log(10000.0) * jnp.arange(half_width, dtype=jnp.float32) / half_width)
    angles = time_steps.astype(jnp.float32)[:, None] * frequency[None, :]
    return jax.nn.silu(jnp.concatenate([jnp.cos(angles), jnp.sin(angles)], axis=1))


def attend(queries, key_rows, values, valid_mask, att_scale):
    scores = (
        jnp.einsum("qbhd,kbhd->bhqk", queries, key_rows, preferred_element_type=jnp.float32)
        * att_scale
    )
    if valid_mask is not None:
        scores = jnp.where(valid_mask, scores, big_negative)
    largest = jnp.max(scores, axis=-1, keepdims=True)
    summed = jnp.sum(jnp.exp(scores - largest), axis=-1, keepdims=True)
    logsum = largest + jnp.log(summed)
    weights = jnp.exp(scores - logsum).astype(jnp.bfloat16)
    output = jnp.einsum("bhqk,kbhd->qbhd", weights, values, preferred_element_type=jnp.float32)
    return (output, logsum)


def attend_back(queries, key_rows, values, valid_mask, att_scale, logsum, upstream):
    scores = (
        jnp.einsum("qbhd,kbhd->bhqk", queries, key_rows, preferred_element_type=jnp.float32)
        * att_scale
    )
    if valid_mask is not None:
        scores = jnp.where(valid_mask, scores, big_negative)
    weights = jnp.exp(scores - logsum)
    back_weights = jnp.einsum(
        "qbhd,kbhd->bhqk", upstream, values, preferred_element_type=jnp.float32
    )
    back_values = jnp.einsum(
        "bhqk,qbhd->kbhd",
        weights.astype(jnp.bfloat16),
        upstream,
        preferred_element_type=jnp.float32,
    )
    inner_sum = jnp.sum(back_weights * weights, axis=-1, keepdims=True)
    back_scores = (weights * (back_weights - inner_sum)).astype(jnp.bfloat16)
    back_queries = (
        jnp.einsum("bhqk,kbhd->qbhd", back_scores, key_rows, preferred_element_type=jnp.float32)
        * att_scale
    )
    back_keys = (
        jnp.einsum("bhqk,qbhd->kbhd", back_scores, queries, preferred_element_type=jnp.float32)
        * att_scale
    )
    return (back_queries, back_keys, back_values)


MESH_ID = pl.DeviceIdType.MESH
LANES = 128
PIECE_SLOTS = 4


def neighbours():
    column = lax.axis_index("clip")
    frame = lax.axis_index("frame")
    depth = frame // 2
    core = frame % 2
    across_x = column + 1 - 2 * (column % 2)
    across_y = column + 2 - 4 * (column // 2)
    sibling = frame + 1 - 2 * core
    return column, frame, depth, core, across_x, across_y, sibling


def greet(peers):
    barrier = pltpu.get_barrier_semaphore()
    for peer in peers:
        pl.semaphore_signal(barrier, inc=1, device_id=peer, device_id_type=MESH_ID)
    pl.semaphore_wait(barrier, len(peers))


class Copies:
    def __init__(self, send_sems, recv_sems):
        self.send_sems, self.recv_sems, self.count, self.started = send_sems, recv_sems, 0, []
        self.maybe = []

    def start(self, source, target, device):
        copy = pltpu.make_async_remote_copy(
            src_ref=source,
            dst_ref=target,
            send_sem=self.send_sems.at[self.count],
            recv_sem=self.recv_sems.at[self.count],
            device_id=device,
            device_id_type=MESH_ID,
        )
        self.count += 1
        assert self.count <= self.send_sems.shape[0]
        copy.start()
        self.started.append(copy)
        return copy

    def start_if(self, condition, source, target, device, recv_sem):
        copy = pltpu.make_async_remote_copy(
            src_ref=source,
            dst_ref=target,
            send_sem=self.send_sems.at[self.count],
            recv_sem=recv_sem,
            device_id=device,
            device_id_type=MESH_ID,
        )
        self.count += 1
        assert self.count <= self.send_sems.shape[0]
        pl.when(condition)(copy.start)
        self.maybe.append((condition, copy))

    def release(self, copy):
        copy.wait_send()
        self.started = [other for other in self.started if other is not copy]

    def finish(self):
        for copy in self.started:
            copy.wait_send()
        for condition, copy in self.maybe:
            pl.when(condition)(copy.wait_send)


def rows_at(ref, start, size, step):
    return ref.at[pl.ds(pl.multiple_of(start, step), size), :]


def whole_unit(ref, tall, unit, frame):
    if tall:
        height = ref.shape[0] // 32
        return rows_at(ref, frame * (4 * height) + unit * height, height, height)
    height, width = ref.shape[0] // 8, ref.shape[1] // 4
    return ref.at[
        pl.ds(pl.multiple_of(frame * height, height), height),
        pl.ds(pl.multiple_of(unit * width, LANES), width),
    ]


def whole_share(ref, tall, frame):
    height = ref.shape[0] // 8
    return rows_at(ref, frame * height, height, height)


def share_unit(ref, tall, unit):
    if tall:
        height = ref.shape[0] // 4
        return rows_at(ref, unit * height, height, height)
    width = ref.shape[1] // 4
    return ref.at[:, pl.ds(pl.multiple_of(unit * width, LANES), width)]


def gather_all(shares, vec, mod_rows):
    wholes = [lax.all_gather(share, "frame", axis=0, tiled=True) for share in shares]
    vecs = lax.all_gather(vec, "frame", axis=0)
    mods = lax.all_to_all(mod_rows, "frame", split_axis=0, concat_axis=0, tiled=True)
    return wholes, vecs, mods


def add_stream(count, left_at, right_at, out_at, left_buf, right_buf, out_buf, sems):
    def loads(index):
        slot = index % PIECE_SLOTS
        return (
            pltpu.make_async_copy(left_at(index), left_buf.at[slot], sems.at[0, slot]),
            pltpu.make_async_copy(right_at(index), right_buf.at[slot], sems.at[1, slot]),
        )

    def store(index):
        slot = index % PIECE_SLOTS
        return pltpu.make_async_copy(out_buf.at[slot], out_at(index), sems.at[2, slot])

    ahead = min(PIECE_SLOTS - 1, count)
    for index in range(ahead):
        for copy in loads(index):
            copy.start()

    def step(index, carry):
        @pl.when(index + PIECE_SLOTS - 1 < count)
        def _():
            for copy in loads(index + PIECE_SLOTS - 1):
                copy.start()

        for copy in loads(index):
            copy.wait()

        @pl.when(index >= PIECE_SLOTS)
        def _():
            store(index - PIECE_SLOTS).wait()

        slot = index % PIECE_SLOTS
        out_buf[slot] = left_buf[slot] + right_buf[slot]
        store(index).start()
        return carry

    lax.fori_loop(0, count, step, 0)
    for index in range(max(0, count - PIECE_SLOTS), count):
        store(index).wait()


ROW_TILE = 128
HEAD_TILE = 64
HEAD_LANES = 128
MOD_ROWS = 6


def dot_rows(left, right):
    return lax.dot_general(
        left, right, (((1,), (1,)), ((), ())), preferred_element_type=jnp.float32
    )


def dot_plain(left, right):
    return jnp.dot(left, right, preferred_element_type=jnp.float32)


def run_tiles(body, count, ins, outs):
    pltpu.emit_pipeline(
        body,
        grid=(count,),
        in_specs=[pl.BlockSpec(block, index) for _, block, index in ins],
        out_specs=[pl.BlockSpec(block, index) for _, block, index in outs],
    )(*[ref for ref, _, _ in ins], *[ref for ref, _, _ in outs])


def by_rows(ref, size):
    if len(ref.shape) == 4:
        many = size // (ref.shape[1] * ref.shape[2])
        return (ref, (many,) + ref.shape[1:], lambda step: (step, 0, 0, 0))
    return (ref, (size, ref.shape[1]), lambda step: (step, 0))


def by_columns(ref, size):
    return (ref, (ref.shape[0], size), lambda step: (0, step))


def tile_rows(step, size):
    return pl.ds(pl.multiple_of(step * size, size), size)


def add_row(rows, which, values):
    rows[which : which + 1, :] += jnp.sum(values, axis=0, keepdims=True)


def split_heads(source, first, heads, width, count):
    height = source.shape[0]
    tile = min(height, HEAD_TILE)

    def step(index, carry):
        rows = tile_rows(index, tile)
        for head in range(count):
            start = first + head * width
            heads[head, rows, 0:width] = source[rows, start : start + width]
        return carry

    lax.fori_loop(0, height // tile, step, 0)


def merge_heads(heads, target, first, width, count):
    height = target.shape[0]
    tile = min(height, HEAD_TILE)

    def step(index, carry):
        rows = tile_rows(index, tile)
        joined = jnp.concatenate([heads[head, rows, 0:width] for head in range(count)], axis=1)
        target[rows, first : first + width * count] = joined
        return carry

    lax.fori_loop(0, height // tile, step, 0)


def attention_back(att_scale, queries, keys, values, mask, logsum, upstream, outs, group=1):
    out_queries, out_keys, out_values = outs
    count = queries.shape[0]

    def body(query, key, value):
        heads = [pl.program_id(0) * group + index for index in range(group)]
        query, key, value = ([ref[index] for index in range(group)] for ref in (query, key, value))
        given = [upstream[head] for head in heads]
        scores = [dot_rows(*pair) * att_scale for pair in zip(key, query)]
        if mask is not None:
            scores = [score + mask[:, 0:1] for score in scores]
        weights = [
            jnp.exp(score - logsum[head, 0:1, :]) for score, head in zip(scores, heads)
        ]
        backs = [dot_rows(*pair) for pair in zip(value, given)]
        inner = [
            jnp.sum(back * weight, axis=0, keepdims=True) for back, weight in zip(backs, weights)
        ]
        backs = [
            (weight * (back - total)).astype(jnp.bfloat16)
            for weight, back, total in zip(weights, backs, inner)
        ]
        back_values = [
            dot_plain(weight.astype(jnp.bfloat16), one).astype(jnp.bfloat16)
            for weight, one in zip(weights, given)
        ]
        back_keys = [
            (dot_plain(*pair) * att_scale).astype(jnp.bfloat16) for pair in zip(backs, query)
        ]
        turned = [
            lax.dot_general(*pair, (((0,), (0,)), ((), ())), preferred_element_type=jnp.float32)
            for pair in zip(key, backs)
        ]
        turned = [(one * att_scale).T.astype(jnp.bfloat16) for one in turned]
        for index, head in enumerate(heads):
            out_values[head] = back_values[index]
            out_keys[head] = back_keys[index]
            out_queries[head] = turned[index]

    per_head = lambda ref: (ref, (group,) + ref.shape[1:], lambda step: (step, 0, 0))
    run_tiles(body, count // group, [per_head(queries), per_head(keys), per_head(values)], [])


ROW = types.SimpleNamespace(
    shift_a=0, scale_a=1, gate_a=2, shift_m=3, scale_m=4, gate_m=5, condition=6, gate_t=7,
    spatial=8, cross=9, reduce=10, gain=11, shift=12, temporal=13, expand=14, high=24,
)


def back_stages(r, att_scale):
    width = r.running.shape[1]
    head_size = width // HEADS
    third = width // 3
    plain = jnp.float32

    def clear():
        r.row_sums[...] = jnp.zeros_like(r.row_sums)
        for heads in (r.head_in, r.head_query, r.head_key, r.head_value):
            heads[...] = jnp.zeros_like(heads)

    def feed_first():
        def body(cot, sent, branch):
            rows = tile_rows(pl.program_id(0), ROW_TILE)
            total = cot[...].astype(plain) + sent[...].reshape(cot.shape).astype(plain)
            r.running[rows, :] = total
            add_row(r.row_sums, ROW.gate_m, total * branch[...].astype(plain))
            down = (total * r.mods[5:6, :]).astype(jnp.bfloat16)
            r.low[rows, :] = down
            add_row(r.row_sums, ROW.reduce, down.astype(plain))

        ins = [by_rows(ref, ROW_TILE) for ref in (r.cotangent, r.back_sent, r.branch_feed)]
        run_tiles(body, r.low.shape[0] // ROW_TILE, ins, [])

    def part_by_rows(turned, right, target, size, place=0):
        def body(left, out):
            out[...] = dot_plain(left[...], right()).astype(jnp.bfloat16)

        run_tiles(
            body,
            turned.shape[0] // size,
            [by_rows(turned, size)],
            [(target, (size, width), lambda step: (step, place))],
        )

    def part_by_columns(turned, right, target, size, first=0, count=None):
        def body(left, out):
            columns = tile_rows(pl.program_id(0) + first, size)
            out[...] = dot_plain(left[...], right[:, columns]).astype(jnp.bfloat16)

        whole = (turned, turned.shape, lambda step: (0, 0))
        run_tiles(
            body,
            target.shape[1] // size if count is None else count,
            [whole],
            [(target, (target.shape[0], size), lambda step: (0, step + first))],
        )

    def reduce_part():
        part_by_rows(r.hidden_turned, lambda: r.low[...], r.part_reduce, 512)

    def feed_hidden():
        def body(weight, slope):
            columns = tile_rows(pl.program_id(0), 512)
            back = dot_rows(r.low[...], weight[...]) * slope[...].astype(plain)
            down = back.astype(jnp.bfloat16)
            r.broad[:, columns] = down

        run_tiles(
            body,
            r.broad.shape[1] // 512,
            [by_rows(r.whole_reduce, 512), by_columns(r.gelu_slope, 512)],
            [],
        )
        for unit in range(4):
            piece = r.broad[:, unit * width : (unit + 1) * width].astype(plain)
            add_row(r.row_sums, ROW.expand + unit, piece)

    def expand_part():
        part_by_columns(r.feed_turned, r.broad, r.part_expand, 512)

    def back_through(weight, block, place, source, target):
        def body(rows):
            columns = tile_rows(pl.program_id(0), third)
            target(columns, dot_rows(source(), rows[...]))

        run_tiles(body, 3, [(weight, (third, block), lambda step: (step, place))], [])

    def set_wide(columns, value):
        r.wide[:, columns] = value

    def add_running(columns, value):
        r.running[:, columns] += value

    def set_broad(columns, value):
        r.broad[:, columns] = value.astype(jnp.bfloat16)

    def back_three(weight):
        def body(*blocks):
            columns = tile_rows(pl.program_id(0), third)
            total = dot_rows(r.broad[:, 0:width], blocks[0][...])
            for place in (1, 2):
                total += dot_rows(
                    r.broad[:, place * width : (place + 1) * width], blocks[place][...]
                )
            r.wide[:, columns] = total

        block = lambda place: (weight, (third, width), lambda step: (step, place))
        run_tiles(body, 3, [block(0), block(1), block(2)], [])

    def feed_normed():
        back_through(r.whole_expand, 4 * width, 0, lambda: r.broad[...], set_wide)

    def norm_back(rows, normal, rate, shift_row, scale_row):
        back = r.wide[rows, :]
        normal = normal.astype(plain)
        add_row(r.row_sums, shift_row, back)
        add_row(r.row_sums, scale_row, back * normal)
        back = back * (1.0 + r.mods[scale_row : scale_row + 1, :])
        mean = jnp.mean(back, axis=1, keepdims=True)
        inner = jnp.mean(back * normal, axis=1, keepdims=True)
        return (back - mean - normal * inner) * rate[rows, 0:1]

    def feed_last():
        def body(normal):
            rows = tile_rows(pl.program_id(0), ROW_TILE)
            total = r.running[rows, :] + norm_back(rows, normal[...], r.feed_rate, 3, 4)
            r.running[rows, :] = total
            down = total.astype(jnp.bfloat16)
            r.low[rows, :] = down
            add_row(r.row_sums, ROW.cross, down.astype(plain))

        run_tiles(body, r.low.shape[0] // ROW_TILE, [by_rows(r.feed_normal, ROW_TILE)], [])

    def cross_part():
        part_by_rows(r.cross_turned, lambda: r.low[...], r.part_text.at[:, pl.ds(0, 4 * width)], third, 3)

    def cross_given():
        back_through(r.whole_text, width, 3, lambda: r.low[...], set_broad)
        split_heads(r.broad, 0, r.head_in, head_size, HEADS)

    def cross_attention():
        attention_back(
            att_scale,
            r.cross_queries,
            r.cross_keys,
            r.cross_values,
            r.text_mask,
            r.cross_logsum,
            r.head_in,
            (r.head_query, r.cross_key, r.cross_value),
            group=4,
        )
        merge_heads(r.head_query, r.broad, 0, head_size, HEADS)
        merge_heads(r.cross_key, r.memory, 0, head_size, HEADS)
        merge_heads(r.cross_value, r.memory, width, head_size, HEADS)

    def query_part():
        part_by_rows(r.after_turned, lambda: r.broad[:, 0:width], r.part_text.at[:, pl.ds(0, 4 * width)], third, 0)

    def memory_part():
        for place in range(2):
            part_by_rows(
                r.context_turned,
                lambda: r.memory[:, place * width : (place + 1) * width],
                r.part_text.at[:, pl.ds(0, 4 * width)],
                third,
                place + 1,
            )

    def context_back():
        def body(keys, values, out):
            back = dot_rows(r.memory[:, 0:width], keys[...])
            back = back + dot_rows(r.memory[:, width : 2 * width], values[...])
            out[...] = back.astype(jnp.bfloat16)

        run_tiles(
            body,
            3,
            [
                (r.whole_text, (third, width), lambda step: (step, 1)),
                (r.whole_text, (third, width), lambda step: (step, 2)),
            ],
            [by_columns(r.back_context, third)],
        )

    def query_back():
        back_through(r.whole_text, width, 0, lambda: r.broad[:, 0:width], add_running)

    def spatial_first():
        def body(branch):
            rows = tile_rows(pl.program_id(0), ROW_TILE)
            total = r.running[rows, :]
            add_row(r.row_sums, ROW.gate_a, total * branch[...].astype(plain))
            down = (total * r.mods[2:3, :]).astype(jnp.bfloat16)
            r.low[rows, :] = down
            add_row(r.row_sums, ROW.spatial, down.astype(plain))

        run_tiles(body, r.low.shape[0] // ROW_TILE, [by_rows(r.branch_attend, ROW_TILE)], [])

    def output_part():
        def body(left, out):
            out[:, 0:width] = dot_plain(left[...], r.low[...]).astype(jnp.bfloat16)
            out[:, width:] = jnp.zeros_like(out[:, width:])

        run_tiles(
            body,
            3,
            [by_rows(r.spatial_turned, third)],
            [(r.part_text, (third, width + third), lambda step: (step, 3))],
        )

    def spatial_given():
        back_through(r.whole_spatial, width, 3, lambda: r.low[...], set_broad)
        split_heads(r.broad, 0, r.head_in, head_size, HEADS)

    def spatial_attention():
        attention_back(
            att_scale,
            r.queries,
            r.keys,
            r.values,
            None,
            r.spatial_logsum,
            r.head_in,
            (r.head_query, r.head_key, r.head_value),
        )
        merge_heads(r.head_query, r.broad, 0, head_size, HEADS)
        merge_heads(r.head_key, r.broad, width, head_size, HEADS)
        merge_heads(r.head_value, r.broad, 2 * width, head_size, HEADS)

    def input_part(first=0, count=7):
        part_by_columns(r.attend_turned, r.broad, r.part_input, 512, first, count)

    def attend_normed():
        back_three(r.whole_spatial)

    def attend_last():
        def body(normal, out):
            rows = tile_rows(pl.program_id(0), ROW_TILE)
            total = r.running[rows, :] + norm_back(rows, normal[...], r.attend_rate, 0, 1)
            out[...] = total.astype(jnp.bfloat16)

        run_tiles(
            body,
            r.low.shape[0] // ROW_TILE,
            [by_rows(r.attend_normal, ROW_TILE)],
            [by_rows(r.tokens_out, ROW_TILE)],
        )

    tile = r.low.shape[0] // 4
    quads = [pl.ds(index * tile, tile) for index in range(4)]

    def by_blocks(ref):
        return (ref, (1,) + ref.shape[1:], lambda step: (step, 0, 0, 0))

    def turn(source, target):
        def step(index, carry):
            rows = tile_rows(index, tile)
            target[:, rows] = source[rows, :].astype(plain).T.astype(jnp.bfloat16)
            return carry

        lax.fori_loop(0, 4, step, 0)

    def time_first():
        def body(cols):
            rows = tile_rows(pl.program_id(0), tile)
            values = cols[...].reshape(tile, width).astype(plain)
            values = values - jnp.mean(values, axis=1, keepdims=True)
            rate = lax.rsqrt(jnp.mean(values * values, axis=1, keepdims=True) + eps_norm)
            normal = values * rate
            r.time_normal[rows, :] = normal.astype(jnp.bfloat16)
            r.time_rate[rows, :] = jnp.broadcast_to(rate, (tile, LANES))
            r.low[rows, :] = (normal * r.vectors[0:1, :] + r.vectors[1:2, :]).astype(jnp.bfloat16)

        run_tiles(body, 4, [by_blocks(r.time_cols)], [])
        turn(r.low, r.time_turned)

    def time_heads():
        def body(weight):
            columns = tile_rows(pl.program_id(0), third)
            r.broad[:, columns] = dot_plain(r.low[...], weight[...]).astype(jnp.bfloat16)

        run_tiles(body, 9, [by_columns(r.whole_time, third)], [])
        for place, heads in enumerate((r.head_query, r.head_key, r.head_value)):
            split_heads(r.broad, place * width, heads, head_size, HEADS)

    def time_attention():
        def step(pair, carry):
            spots = [(pair * 2 + index, rows) for index in range(2) for rows in quads]
            keys = [r.head_key[spot] for spot in spots]
            values = [r.head_value[spot] for spot in spots]
            scores = [
                dot_rows(key, r.head_query[spot]) * att_scale + r.time_mask[...]
                for key, spot in zip(keys, spots)
            ]
            largest = [jnp.max(score, axis=0, keepdims=True) for score in scores]
            logsums = [
                top + jnp.log(jnp.sum(jnp.exp(score - top), axis=0, keepdims=True))
                for score, top in zip(scores, largest)
            ]
            weights = [
                jnp.exp(score - logs).astype(jnp.bfloat16) for score, logs in zip(scores, logsums)
            ]
            turned = [
                lax.dot_general(
                    value, weight, (((0,), (0,)), ((), ())), preferred_element_type=plain
                )
                for value, weight in zip(values, weights)
            ]
            turned = [value.T.astype(jnp.bfloat16) for value in turned]
            for (head, rows), logs, value in zip(spots, logsums, turned):
                r.time_logsum[head, 0:1, rows] = logs
                r.head_in[head, rows, :] = value
            return carry

        lax.fori_loop(0, HEADS // 2, step, 0)
        merge_heads(r.head_in, r.middle, 0, head_size, HEADS)
        turn(r.middle, r.middle_turned)

    def time_result():
        def body(weight, out):
            columns = tile_rows(pl.program_id(0), third)
            value = dot_plain(r.middle[...], weight[...]) + r.vectors[2:3, columns]
            out[...] = value.astype(jnp.bfloat16).reshape(out.shape)

        shape = r.time_result.shape
        run_tiles(
            body,
            3,
            [(r.whole_time, (width, third), lambda step: (0, 9 + step))],
            [(r.time_result, shape[:3] + (third,), lambda step: (0, 0, 0, step))],
        )

    def time_given():
        def body(cols):
            rows = tile_rows(pl.program_id(0), tile)
            values = cols[...].reshape(tile, width).astype(plain)
            down = (values * (r.time_keep[rows, 0:1] * r.vectors[3:4, :])).astype(jnp.bfloat16)
            r.low[rows, :] = down
            add_row(r.row_sums, ROW.temporal, down.astype(plain))

        run_tiles(body, 4, [by_blocks(r.cot_cols)], [])
        back_through(r.whole_time, width, 3, lambda: r.low[...], set_broad)
        split_heads(r.broad, 0, r.head_in, head_size, HEADS)

    def time_out_part():
        def body(out):
            rows = tile_rows(pl.program_id(0), third)
            out[...] = dot_plain(r.middle_turned[rows, :], r.low[...]).astype(jnp.bfloat16)

        run_tiles(body, 3, [], [(r.part_time, (third, width), lambda step: (step, 3))])

    def time_attention_back():
        def step(pair, carry):
            spots = [(pair * 2 + index, rows) for index in range(2) for rows in quads]
            queries = [r.head_query[spot] for spot in spots]
            keys = [r.head_key[spot] for spot in spots]
            values = [r.head_value[spot] for spot in spots]
            givens = [r.head_in[spot] for spot in spots]
            weights = [
                jnp.exp(
                    dot_rows(key, query) * att_scale
                    + r.time_mask[...]
                    - r.time_logsum[head, 0:1, rows]
                )
                for key, query, (head, rows) in zip(keys, queries, spots)
            ]
            backs = [dot_rows(value, given) for value, given in zip(values, givens)]
            inner = [
                jnp.sum(back * weight, axis=0, keepdims=True)
                for back, weight in zip(backs, weights)
            ]
            backs = [
                (weight * (back - total)).astype(jnp.bfloat16)
                for weight, back, total in zip(weights, backs, inner)
            ]
            back_values = [
                dot_plain(weight.astype(jnp.bfloat16), given).astype(jnp.bfloat16)
                for weight, given in zip(weights, givens)
            ]
            back_keys = [
                (dot_plain(back, query) * att_scale).astype(jnp.bfloat16)
                for back, query in zip(backs, queries)
            ]
            turned = [
                lax.dot_general(key, back, (((0,), (0,)), ((), ())), preferred_element_type=plain)
                for key, back in zip(keys, backs)
            ]
            turned = [(value * att_scale).T.astype(jnp.bfloat16) for value in turned]
            for (head, rows), *outs in zip(spots, turned, back_keys, back_values):
                r.head_query[head, rows, :] = outs[0]
                r.head_key[head, rows, :] = outs[1]
                r.head_value[head, rows, :] = outs[2]
            return carry

        lax.fori_loop(0, HEADS // 2, step, 0)
        for place, heads in enumerate((r.head_query, r.head_key, r.head_value)):
            merge_heads(heads, r.broad, place * width, head_size, HEADS)

    def time_normed():
        back_three(r.whole_time)

    def time_last():
        def body(out):
            rows = tile_rows(pl.program_id(0), tile)
            back = r.wide[rows, :]
            normal = r.time_normal[rows, :].astype(plain)
            add_row(r.row_sums, ROW.shift, back)
            add_row(r.row_sums, ROW.gain, back * normal)
            back = back * r.vectors[0:1, :]
            mean = jnp.mean(back, axis=1, keepdims=True)
            inner = jnp.mean(back * normal, axis=1, keepdims=True)
            back = (back - mean - normal * inner) * r.time_rate[rows, 0:1]
            out[...] = back.astype(jnp.bfloat16).reshape(out.shape)

        run_tiles(body, 4, [], [by_blocks(r.time_back)])

    def time_in_part():
        def body(out):
            columns = tile_rows(pl.program_id(0), third)
            out[...] = dot_plain(r.time_turned[...], r.broad[:, columns]).astype(jnp.bfloat16)

        run_tiles(body, 9, [], [by_columns(r.part_time, third)])

    def block_last():
        def body(after, result, cot, out):
            value = result[...].reshape(cot.shape).astype(plain)
            add_row(r.row_sums, ROW.gate_t, cot[...].astype(plain) * value * r.vectors[5:6, :])
            out[...] = (after[...] + r.vectors[4:5, :] * value).astype(jnp.bfloat16)

        ins = [by_rows(ref, ROW_TILE) for ref in (r.after_feed, r.returned, r.cotangent)]
        run_tiles(body, r.low.shape[0] // ROW_TILE, ins, [by_rows(r.block_out, ROW_TILE)])

    return types.SimpleNamespace(**locals())


def back_kernel(together, att_scale, names, *refs):
    r = types.SimpleNamespace(**dict(zip(names, refs)))
    if together:
        r.back_sent, r.returned = r.back_sent_cols, r.returned_cols
    do = back_stages(r, att_scale)
    if not together:
        do.clear()
        do.feed_first()
        do.reduce_part()
        do.feed_hidden()
        do.expand_part()
        do.feed_normed()
        do.feed_last()
        do.cross_part()
        do.cross_given()
        do.cross_attention()
        do.query_part()
        do.memory_part()
        do.context_back()
        do.query_back()
        do.spatial_first()
        do.output_part()
        do.spatial_given()
        do.spatial_attention()
        do.input_part()
        do.attend_normed()
        do.attend_last()
        return
    column, frame, depth, core, across_x, across_y, sibling = neighbours()
    far = 3 - column
    frame_peers = [(column, (frame + shift) % 8) for shift in range(1, 8)]
    line_peers = [(column, ((depth + shift) % 4) * 2 + core) for shift in range(1, 4)]
    plane_peers = [(across_x, frame), (across_y, frame), (far, frame)]
    greet(frame_peers + plane_peers)
    copies = Copies(r.send_sems, r.recv_sems)
    talls, bundles = PART_TALLS, len(PART_TALLS)
    cut = lambda ref, *span: ref.at[:, pl.ds(*span)]
    parts = [
        r.part_time,
        r.part_reduce,
        cut(r.part_expand, 0, 3584),
        cut(r.part_expand, 3584, 1024),
        cut(r.part_text, 0, 4 * r.low.shape[1]),
        cut(r.part_text, 4 * r.low.shape[1], 1536),
        cut(r.part_input, 0, 2048),
        cut(r.part_input, 2048, 1536),
    ]
    many = lambda name: [vars(r)[f"{name}_{index}"] for index in range(bundles)]
    halved, quartered, lined = (many(name) for name in LANDING)
    summed, crossed = halved, quartered
    outs = [
        r.share_time,
        r.share_reduce,
        cut(r.share_expand, 0, 3584),
        cut(r.share_expand, 3584, 1024),
        cut(r.share_text, 0, 4 * r.low.shape[1]),
        cut(r.share_text, 4 * r.low.shape[1], 1536),
        cut(r.share_input, 0, 2048),
        cut(r.share_input, 2048, 1536),
    ]

    def part_piece(index, unit, slot):
        ref = parts[index]
        if talls[index]:
            high = ref.shape[0] // 16
            return rows_at(ref, slot * (4 * high) + unit * high, high, high)
        high, wide = ref.shape[0] // 4, ref.shape[1] // 4
        return ref.at[
            pl.ds(pl.multiple_of(slot * high, high), high),
            pl.ds(pl.multiple_of(unit * wide, LANES), wide),
        ]

    left_high = r.left_own.shape[0]
    piece_high = left_high // 4

    def swap_rows(source, target):
        high = source.shape[0] // 8
        return [
            copies.start(
                rows_at(source, (slot * 2 + 1 - core) * high, high, high),
                target.at[pl.ds(slot * high, high)],
                (column, sibling),
            )
            for slot in range(4)
        ]

    def swap(source, target):
        return copies.start(source, target, (column, sibling))

    def left_start(source, other, rows_got):
        arrive(rows_got)
        deep = pl.ds(0, source.shape[1])
        started = [
            pltpu.make_async_copy(
                rows_at(source, (slot * 2 + core) * piece_high, piece_high, piece_high),
                r.left_own.at[pl.ds(slot * piece_high, piece_high), deep],
                r.left_sems.at[slot],
            )
            for slot in range(4)
        ]
        started.append(pltpu.make_async_copy(other, r.left_other.at[:, deep], r.left_sems.at[4]))
        for copy in started:
            copy.start()
        return started

    def arrive(got):
        for copy in got:
            copy.wait_recv()

    def finish_left(started):
        for copy in started:
            copy.wait()

    def part(started, right, got, other, target, size, count, place, first=0, deep=None):
        finish_left(started)
        if got is not None:
            got.wait_recv()
        deep = r.left_own.shape[1] if deep is None else deep

        def body(block, out):
            columns = tile_rows(pl.program_id(0) + first, size)
            total = dot_plain(r.left_own[:, 0:deep], right[:, columns])
            total = total + dot_plain(r.left_other[:, 0:deep], block[...])
            out[...] = total.astype(jnp.bfloat16)

        run_tiles(
            body,
            count,
            [(other, (other.shape[0], size), lambda step: (0, step + first))],
            [(target, (left_high, size), lambda step: (0, step + place))],
        )

    def part_reduce(got):
        got.wait_recv()
        arrive(hidden_got)
        high = r.part_reduce.shape[0] // 4

        def body(own, other, given, out):
            total = dot_plain(own[...], r.low[...]) + dot_plain(other[...], given[...])
            out[...] = total.astype(jnp.bfloat16)

        own = r.hidden_turned.at[pl.ds(pl.multiple_of(core * high, high), 7 * high)]
        run_tiles(
            body,
            4,
            [
                (own, (high, own.shape[1]), lambda step: (2 * step, 0)),
                by_rows(r.other_hidden, high),
                (r.given_feed, r.given_feed.shape, lambda step: (0, 0)),
            ],
            [by_rows(r.part_reduce, high)],
        )

    def part_output(started, got):
        finish_left(started)
        got.wait_recv()
        width = r.low.shape[1]

        def body(given, out):
            total = dot_plain(r.left_own[...], r.low[...])
            total = total + dot_plain(r.left_other[...], given[...])
            out[:, 0:width] = total.astype(jnp.bfloat16)
            out[:, width:] = jnp.zeros_like(out[:, width:])

        wide = r.part_text.shape[1] // 4
        run_tiles(
            body,
            1,
            [(r.given_output, r.given_output.shape, lambda step: (0, 0))],
            [(r.part_text, (left_high, wide), lambda step: (0, 3))],
        )

    def stream(index, count, left_at, right_at, out_at):
        wide = pl.ds(0, halved[index].shape[-1])
        buffers = [ref.at[:, :, wide] for ref in (r.left_buf, r.right_buf, r.out_buf)]
        add_stream(count, left_at, right_at, out_at, *buffers, r.stream_sems)

    from_half, from_quarter, from_line, ends = {}, {}, {}, []

    def go(index):
        if index == LINE_FIRST:
            for shift in range(1, 4):
                other = (depth + shift) % 4
                for unit in range(4):
                    from_line[index, shift, unit] = copies.start(
                        part_piece(index, unit, other),
                        lined[index].at[shift - 1, unit],
                        (column, other * 2 + core),
                    )
            return
        for slot in range(4):
            near = across_x if slot < 2 else across_y
            for which, unit in enumerate((near, far)):
                from_half[index, slot, which] = copies.start(
                    part_piece(index, unit, slot), halved[index].at[slot, which], (near, frame)
                )

    def half(index):
        for slot in range(4):
            for which in range(2):
                from_half[index, slot, which].wait_recv()

        def source(step):
            slot, which = step // 2, step % 2
            late = slot // 2
            unit = column + which * (
                (1 - late) * (across_y - column) + late * (across_x - column)
            )
            return part_piece(index, unit, slot)

        place = lambda step: halved[index].at[step // 2, step % 2]
        stream(index, 8, source, place, place)
        for slot in range(4):
            near = across_y if slot < 2 else across_x
            from_quarter[index, slot] = copies.start(
                halved[index].at[slot, 1], quartered[index].at[slot], (near, frame)
            )

    def quarter(index):
        for slot in range(4):
            from_quarter[index, slot].wait_recv()
        place = lambda slot: quartered[index].at[slot]
        stream(index, 4, lambda slot: halved[index].at[slot, 0], place, place)
        for shift in range(1, 4):
            other = (depth + shift) % 4
            from_line[index, shift] = copies.start(
                quartered[index].at[other], lined[index].at[shift - 1], (column, other * 2 + core)
            )

    def totals_of_four(count, sources, target, height, width):
        box = (pl.ds(0, height), pl.ds(0, width))

        def loads(index):
            slot = index % 2
            return [
                pltpu.make_async_copy(
                    source, r.four_buf.at[(slot, place) + box], r.four_sems.at[slot, place]
                )
                for place, source in enumerate(sources(index))
            ]

        def store(index):
            slot = index % 2
            return pltpu.make_async_copy(
                r.out_buf.at[(slot,) + box], target(index), r.stream_sems.at[2, slot]
            )

        waiting = loads(0)
        for copy in waiting:
            copy.start()
        for index in range(count):
            ahead = loads(index + 1) if index + 1 < count else []
            for copy in ahead:
                copy.start()
            for copy in waiting:
                copy.wait()
            waiting = ahead
            if index >= 2:
                store(index - 2).wait()
            slot = index % 2
            total = r.four_buf[slot, 0, 0:height, 0:width].astype(jnp.float32)
            for place in range(1, 4):
                total = total + r.four_buf[slot, place, 0:height, 0:width].astype(jnp.float32)
            r.out_buf[slot, 0:height, 0:width] = total.astype(jnp.bfloat16)
            store(index).start()
        for index in range(max(0, count - 2), count):
            store(index).wait()

    def total_of_four(own, others, target, height, width):
        totals_of_four(1, lambda index: [own] + others, lambda index: target, height, width)

    spread, relayed = {}, []

    def hand_out(index):
        target = share_unit(outs[index], talls[index], column)
        spread[index] = [copies.start(target, target, peer) for peer in plane_peers[:2]]
        if index >= bundles - 3:
            ends.extend(spread[index])
            ends.append(copies.start(target, target, plane_peers[2]))

    def relay(index):
        x_first = index % 2 == 0
        first, second = spread[index] if x_first else spread[index][::-1]
        first.wait_recv()
        target = share_unit(outs[index], talls[index], across_x if x_first else across_y)
        ends.append(copies.start(target, target, plane_peers[1 if x_first else 0]))
        ends.append(second)

    def line_sums():
        index = LINE_FIRST
        for shift in range(1, 4):
            for unit in range(4):
                from_line[index, shift, unit].wait_recv()
        totals_of_four(
            4,
            lambda unit: [part_piece(index, unit, depth)]
            + [lined[index].at[slot, unit] for slot in range(3)],
            lambda unit: summed[index].at[unit],
            *lined[index].shape[2:],
        )
        for slot, peer in enumerate(plane_peers):
            from_half[index, slot] = copies.start(
                summed[index].at[peer[0]], crossed[index].at[slot], peer
            )

    def line_last():
        index = LINE_FIRST
        for slot in range(3):
            from_half[index, slot].wait_recv()
        total_of_four(
            summed[index].at[column],
            [crossed[index].at[slot] for slot in range(3)],
            share_unit(outs[index], talls[index], column),
            *lined[index].shape[2:],
        )
        hand_out(index)

    def line(index):
        for shift in range(1, 4):
            from_line[index, shift].wait_recv()
        total_of_four(
            quartered[index].at[depth],
            [lined[index].at[slot] for slot in range(3)],
            share_unit(outs[index], talls[index], column),
            *lined[index].shape[1:],
        )
        hand_out(index)

    contexts, paired_contexts, texts = [], [], []
    text_rows = r.text_part.shape[0] // 4

    def context_send():
        contexts.extend(
            copies.start(r.back_context, r.context_all.at[frame], peer) for peer in line_peers
        )
        paired_contexts.append(
            copies.start(r.back_context, r.context_all.at[frame], (column, sibling))
        )
        move(r.back_context, r.held_context, r.context_all.at[frame])

    def context_pair():
        for shift, copy in zip(range(1, 4), contexts):
            copy.wait_recv()
            place = r.context_all.at[((depth + 4 - shift) % 4) * 2 + core]
            paired_contexts.append(copies.start(place, place, (column, sibling)))

    def text_part():
        for copy in paired_contexts:
            copy.wait_recv()
        each = r.context_all.shape[1]

        def body(text, context, out):
            total = dot_plain(text[:, 0:each], context[0])
            for index in range(1, 8):
                total = total + dot_plain(text[:, index * each : (index + 1) * each], context[index])
            out[...] = total.astype(jnp.bfloat16)

        run_tiles(
            body,
            4,
            [
                by_rows(r.text_turned, text_rows),
                (r.context_all, r.context_all.shape, lambda step: (0, 0, 0)),
            ],
            [by_rows(r.text_part, text_rows)],
        )
        for slot, peer in enumerate(plane_peers):
            texts.append(
                copies.start(
                    rows_at(r.text_part, peer[0] * text_rows, text_rows, text_rows),
                    r.text_got.at[slot],
                    peer,
                )
            )

    def text_line():
        for copy in texts:
            copy.wait_recv()
        total_of_four(
            rows_at(r.text_part, column * text_rows, text_rows, text_rows),
            [r.text_got.at[slot] for slot in range(3)],
            rows_at(r.text_out, column * text_rows, text_rows, text_rows),
            *r.text_got.shape[1:],
        )
        target = rows_at(r.text_out, column * text_rows, text_rows, text_rows)
        for peer in plane_peers:
            ends.append(copies.start(target, target, peer))

    cots_got, back_got, result_got, rows_got, rows_paired = [], [], [], [], []
    here = r.local_sems

    def move(source, held, target):
        load = pltpu.make_async_copy(source, held, here.at[0])
        load.start()
        load.wait()
        store = pltpu.make_async_copy(held, target, here.at[0])
        store.start()
        store.wait()

    def cols_send(source, target, got):
        for peer in frame_peers:
            got.append(copies.start(source.at[peer[1]], target.at[:, frame], peer))
        move(source.at[frame], r.held_cols, target.at[:, frame])

    def return_send(source, target, got):
        for peer in frame_peers:
            got.append(copies.start(source.at[:, peer[1]], target.at[frame], peer))
        move(source.at[:, frame], r.held_cols, target.at[frame])

    def rows_send():
        for peer in line_peers:
            rows_got.append(copies.start(r.row_sums, r.rows_all.at[frame], peer))
        rows_paired.append(copies.start(r.row_sums, r.rows_all.at[frame], (column, sibling)))
        r.rows_all[frame] = r.row_sums[...]

    def rows_pair():
        for shift, copy in zip(range(1, 4), rows_got):
            copy.wait_recv()
            place = r.rows_all.at[((depth + 4 - shift) % 4) * 2 + core]
            rows_paired.append(copies.start(place, place, (column, sibling)))

    def rows_plane():
        arrive(rows_paired)
        mods = r.rows_all.at[:, pl.ds(0, 8)]
        own = [pltpu.make_async_copy(mods, r.mods_out.at[column], here.at[0])]
        for peer in plane_peers:
            ends.append(copies.start(mods, r.mods_out.at[column], peer))
        r.sums[...] = jnp.sum(r.rows_all[:, 8:, :], axis=0)
        own.append(pltpu.make_async_copy(r.sums, r.sums_out.at[column], here.at[1]))
        for copy in own:
            copy.start()
        for peer in plane_peers:
            ends.append(copies.start(r.sums, r.sums_out.at[column], peer))
        for copy in own:
            copy.wait()

    wide = r.low.shape[1]
    third = wide // 3
    cols_send(r.cot_rows, r.cot_cols, cots_got)
    hidden_got = swap_rows(r.hidden_turned, r.other_hidden)
    feed_got = swap_rows(r.feed_turned, r.other_feed)
    cross_got = swap_rows(r.cross_turned, r.other_cross)
    after_got = swap_rows(r.after_turned, r.other_after)
    text_got = swap_rows(r.context_turned, r.other_context)
    spatial_got = swap_rows(r.spatial_turned, r.other_spatial)
    attend_got = swap_rows(r.attend_turned, r.other_attend)
    do.clear()
    r.row_sums[ROW.condition : ROW.condition + 1, :] = r.vectors[6:7, :]
    do.time_first()
    time_got = swap_rows(r.time_turned, r.other_time)
    do.time_heads()
    do.time_attention()
    middle_got = swap_rows(r.middle_turned, r.other_middle)
    arrive(cots_got)
    do.time_given()
    time_out = swap(r.low, r.given_time_out)
    do.time_attention_back()
    time_in = swap(r.broad.at[:, pl.ds(0, 3 * wide)], r.given_time_in)
    do.time_normed()
    do.time_last()
    return_send(r.time_back, r.back_sent_cols, back_got)
    held = left_start(r.middle_turned, r.other_middle, middle_got)
    part(held, r.low, time_out, r.given_time_out, r.part_time, third, 3, 9)
    held = left_start(r.time_turned, r.other_time, time_got)
    part(held, r.broad, time_in, r.given_time_in, r.part_time, third, 9, 0)
    go(0)
    held = left_start(r.feed_turned, r.other_feed, feed_got)
    do.time_result()
    arrive(back_got)
    return_send(r.time_result, r.returned_cols, result_got)
    copies.release(time_out)
    do.feed_first()
    feed = swap(r.low, r.given_feed)
    part_reduce(feed)
    go(1)
    half(0)
    copies.release(time_in)
    do.feed_hidden()
    hidden = swap(r.broad, r.given_hidden)
    do.feed_normed()
    part(held, r.broad, hidden, r.given_hidden, r.part_expand, 512, 9, 0)
    go(2)
    go(3)
    quarter(0)
    half(1)
    held = left_start(r.cross_turned, r.other_cross, cross_got)
    copies.release(feed)
    do.feed_last()
    cross = swap(r.low, r.given_cross)
    copies.release(hidden)
    do.cross_given()
    part(held, r.low, cross, r.given_cross, r.part_text, third, 3, 9)
    held = left_start(r.after_turned, r.other_after, after_got)
    do.cross_attention()
    query = swap(r.broad.at[:, pl.ds(0, wide)], r.given_query)
    memory = swap(r.memory, r.given_memory)
    half(2)
    quarter(1)
    do.context_back()
    context_send()
    part(held, r.broad, query, r.given_query, r.part_text, third, 3, 0)
    held = left_start(r.context_turned, r.other_context, text_got)
    do.query_back()
    deep = r.memory.shape[0]
    part(held, r.memory, memory, r.given_memory, r.part_text, third, 6, 3, 0, deep)
    go(4)
    held = left_start(r.spatial_turned, r.other_spatial, spatial_got)
    line(0)
    copies.release(cross)
    do.spatial_first()
    output = swap(r.low, r.given_output)
    quarter(2)
    copies.release(query)
    do.spatial_given()
    part_output(held, output)
    go(5)
    held = left_start(r.attend_turned, r.other_attend, attend_got)
    line_sums()
    relay(0)
    line(1)
    do.spatial_attention()
    inputs = swap(r.broad.at[:, pl.ds(0, r.given_input.shape[1])], r.given_input)
    half(4)
    line_last()
    context_pair()
    do.attend_normed()
    part(held, r.broad, inputs, r.given_input, r.part_input, 512, 4, 0)
    go(6)
    part([], r.broad, None, r.given_input, r.part_input, 512, 3, 4, 4)
    go(7)
    half(5)
    quarter(4)
    arrive(result_got)
    do.block_last()
    do.attend_last()
    rows_send()
    text_part()
    half(6)
    quarter(5)
    half(7)
    line(2)
    relay(1)
    quarter(6)
    quarter(7)
    rows_pair()
    line(4)
    relay(2)
    relay(3)
    rows_plane()
    text_line()
    line(5)
    line(6)
    line(7)
    relay(4)
    for copy in ends:
        copy.wait_recv()
    copies.finish()


LANDING = ("halved", "quartered", "lined")
PART_TALLS = (False, True, False, False, False, False, False, False)
LINE_FIRST = 3


def backward(att_scale, together, o, text_turned):
    anywhere = pl.BlockSpec(memory_space=pl.ANY)
    inside = pl.BlockSpec(memory_space=pltpu.VMEM)
    tokens, width = o.cotangent.shape
    hidden = o.gelu_slope.shape[1]
    text_count = o.cross_keys.shape[1]
    low, full = jnp.bfloat16, jnp.float32
    shape = jax.ShapeDtypeStruct
    third = width // 3
    hbm_out = dict(
        part_reduce=shape((hidden, width), low),
        part_expand=shape((width, hidden), low),
        part_text=shape((width, 5 * width + third), low),
        part_input=shape((width, 3 * width + LANES), low),
        back_context=shape((text_count, width), low),
        tokens_out=shape((tokens, width), low),
    )
    scratch = dict(
        running=pltpu.VMEM((tokens, width), full),
        wide=pltpu.VMEM((tokens, width), full),
        low=pltpu.VMEM((tokens, width), low),
        broad=pltpu.VMEM((tokens, hidden), low),
        head_in=pltpu.VMEM((HEADS, tokens, HEAD_LANES), low),
        head_query=pltpu.VMEM((HEADS, tokens, HEAD_LANES), low),
        head_key=pltpu.VMEM((HEADS, tokens, HEAD_LANES), low),
        head_value=pltpu.VMEM((HEADS, tokens, HEAD_LANES), low),
        cross_key=pltpu.VMEM((HEADS, text_count, HEAD_LANES), low),
        cross_value=pltpu.VMEM((HEADS, text_count, HEAD_LANES), low),
        memory=pltpu.VMEM((text_count, 2 * width), low),
    )
    hbm_in = dict(
        whole_spatial=o.whole_spatial,
        whole_text=o.whole_text,
        whole_expand=o.whole_expand,
        whole_reduce=o.whole_reduce,
        cotangent=o.cotangent,
        branch_feed=o.branch_feed,
        hidden_turned=o.hidden_turned,
        gelu_slope=o.gelu_slope,
        feed_turned=o.feed_turned,
        feed_normal=o.feed_normal,
        cross_turned=o.cross_turned,
        cross_queries=o.cross_queries,
        cross_keys=o.cross_keys,
        cross_values=o.cross_values,
        after_turned=o.after_turned,
        context_turned=o.context_turned,
        branch_attend=o.branch_attend,
        spatial_turned=o.spatial_turned,
        queries=o.queries,
        keys=o.keys,
        values=o.values,
        attend_turned=o.attend_turned,
        attend_normal=o.attend_normal,
    )
    vmem_in = dict(
        mods=o.mods,
        feed_rate=o.feed_rate,
        attend_rate=o.attend_rate,
        cross_logsum=o.cross_logsum,
        spatial_logsum=o.spatial_logsum,
        text_mask=o.text_mask,
    )
    if not together:
        hbm_in.update(back_sent=o.back_sent)
    vmem_out = dict(row_sums=shape((ROW.high, width), full))
    if together:
        hbm_in.update(
            time_cols=o.time_cols,
            cot_rows=o.cot_rows,
            whole_time=o.whole_time,
            after_feed=o.after_feed,
            text_turned=text_turned,
        )
        vmem_in.update(vectors=o.vectors, time_keep=o.time_keep, time_mask=o.time_mask)
        rows = o.cot_rows.shape
        cols = (rows[1], rows[0]) + rows[2:]
        hbm_out.update(cot_cols=shape(cols, low))
        half = lambda full: shape((full.shape[0] // 2, full.shape[1]), low)
        hbm_out.update(
            part_time=shape((width // 2, 4 * width), low),
            part_reduce=half(hbm_out["part_reduce"]),
            part_expand=half(hbm_out["part_expand"]),
            part_text=half(hbm_out["part_text"]),
            part_input=half(hbm_out["part_input"]),
            other_time=shape((width // 2, tokens), low),
            other_middle=shape((width // 2, tokens), low),
            other_hidden=half(o.hidden_turned),
            other_feed=half(o.feed_turned),
            other_cross=half(o.cross_turned),
            other_after=half(o.after_turned),
            other_context=half(o.context_turned),
            other_spatial=half(o.spatial_turned),
            other_attend=half(o.attend_turned),
            given_time_out=shape((tokens, width), low),
            given_time_in=shape((tokens, 3 * width), low),
            given_feed=shape((tokens, width), low),
            given_hidden=shape((tokens, hidden), low),
            given_cross=shape((tokens, width), low),
            given_query=shape((tokens, width), low),
            given_memory=shape((text_count, 2 * width), low),
            given_output=shape((tokens, width), low),
            given_input=shape((tokens, 3 * width + LANES), low),
        )
        hbm_out.update(time_result=shape(cols, low))
        hbm_out.update(time_back=shape(cols, low))
        hbm_out.update(back_sent_cols=shape(rows, low))
        hbm_out.update(returned_cols=shape(rows, low))
        hbm_out.update(block_out=shape((tokens, width), low))
        hbm_out.update(mods_out=shape((4, 8, 8, width), full))
        hbm_out.update(sums_out=shape((4, ROW.high - 8, width), full))
        high = width // 8
        wides = (width, width, 896, 256, width, third, 512, 384)
        high = width // 8
        for index, wide in enumerate(wides):
            piece = (high, wide)
            first = index == LINE_FIRST
            landing = [(4,) if first else (4, 2), (4,), (3, 4) if first else (3,)]
            for name, lead in zip(LANDING, landing):
                hbm_out[f"{name}_{index}"] = shape(lead + piece, low)
        hbm_out.update(
            share_time=shape((high, 4 * width), low),
            share_reduce=shape((4 * high, width), low),
            share_expand=shape((high, 4 * width), low),
            share_text=shape((high, 5 * width + third), low),
            share_input=shape((high, 3 * width + LANES), low),
        )
        text_shape = (text_turned.shape[0], width)
        hbm_out.update(context_all=shape((8, text_count, width), low))
        hbm_out.update(text_part=shape(text_shape, low))
        hbm_out.update(text_got=shape((3, text_shape[0] // 4, width), low))
        hbm_out.update(text_out=shape(text_shape, low))
        remote = 240
        piece = (high, width + third)
        scratch.update(
            send_sems=pltpu.SemaphoreType.DMA((remote,)),
            recv_sems=pltpu.SemaphoreType.DMA((remote,)),
            stream_sems=pltpu.SemaphoreType.DMA((3, PIECE_SLOTS)),
            local_sems=pltpu.SemaphoreType.DMA((2,)),
            left_own=pltpu.VMEM((width // 2, tokens), low),
            left_other=pltpu.VMEM((width // 2, tokens), low),
            left_sems=pltpu.SemaphoreType.DMA((5,)),
            left_buf=pltpu.VMEM((PIECE_SLOTS,) + piece, low),
            right_buf=pltpu.VMEM((PIECE_SLOTS,) + piece, low),
            out_buf=pltpu.VMEM((PIECE_SLOTS,) + piece, low),
            four_buf=pltpu.VMEM((2, 4) + piece, low),
            four_sems=pltpu.SemaphoreType.DMA((2, 4)),
            rows_all=pltpu.VMEM((8, ROW.high, width), full),
            sums=pltpu.VMEM((ROW.high - 8, width), full),
            time_normal=pltpu.VMEM((tokens, width), low),
            time_rate=pltpu.VMEM((tokens, LANES), full),
            time_turned=pltpu.VMEM((width, tokens), low),
            time_logsum=pltpu.VMEM((HEADS, 8, tokens), full),
            held_cols=pltpu.VMEM((cols[0],) + cols[2:], low),
            held_context=pltpu.VMEM((text_count, width), low),
            middle=pltpu.VMEM((tokens, width), low),
            middle_turned=pltpu.VMEM((width, tokens), low),
        )
    names = list(hbm_in) + list(vmem_in) + list(hbm_out) + list(vmem_out) + list(scratch)
    results = pl.pallas_call(
        functools.partial(back_kernel, together, att_scale, names),
        out_shape=list(hbm_out.values()) + list(vmem_out.values()),
        in_specs=[anywhere] * len(hbm_in) + [inside] * len(vmem_in),
        out_specs=[anywhere] * len(hbm_out) + [inside] * len(vmem_out),
        scratch_shapes=list(scratch.values()),
        compiler_params=pltpu.CompilerParams(
            collective_id=1 if together else None,
            has_side_effects=True,
            vmem_limit_bytes=60 * 1024 * 1024,
        ),
        name="backward",
    )(*hbm_in.values(), *vmem_in.values())
    return types.SimpleNamespace(**dict(zip(list(hbm_out) + list(vmem_out), results)))


def one_slice():
    return lax.axis_size("clip") == 4 and lax.axis_size("frame") == 8


def sum_shares(group):
    def total(part):
        return lax.psum(lax.psum_scatter(part, "frame", scatter_dimension=0, tiled=True), "clip")

    return jnp.concatenate([total(part) for part in group], axis=1)


FORWARD_TALLS = (False, True, False, False, True, False)
VEC = types.SimpleNamespace(
    spatial=0, cross=1, reduce=2, gain=3, shift=4, temporal=5, gate=6, expand=7, high=16
)


def forward_stages(r, att_scale):
    tokens, width = r.low.shape
    head_size = width // HEADS
    third = width // 3
    tile = tokens // 4
    plain = jnp.float32
    row = lambda which: r.rows_low[which : which + 1, :]

    def clear():
        for heads in (r.head_query, r.head_key, r.head_value, r.cross_key, r.cross_value):
            heads[...] = jnp.zeros_like(heads)

    def sum_mods():
        r.mods[...] = jnp.sum(r.mods_got[...], axis=0)

    def sum_rows():
        r.rows_low[...] = jnp.sum(r.rows_got[...].astype(plain), axis=0)
        for unit in range(4):
            r.rows_expand[0:1, unit * width : (unit + 1) * width] = row(VEC.expand + unit)

    def turn_out(source, target):
        height = source.shape[0] // target.shape[1] * LANES

        def body(out):
            rows = tile_rows(pl.program_id(0), LANES)
            out[...] = source[rows, :].astype(plain).T.astype(jnp.bfloat16)

        run_tiles(body, target.shape[1] // LANES, [], [by_columns(target, LANES)])

    def normed(values, rate_out, rows, shift, scale):
        values = values - jnp.mean(values, axis=1, keepdims=True)
        rate = lax.rsqrt(jnp.mean(values * values, axis=1, keepdims=True) + eps_norm)
        normal = values * rate
        rate_out[rows, :] = jnp.broadcast_to(rate, (tile, LANES))
        shift, scale = (r.mods[which : which + 1, :] for which in (shift, scale))
        r.low[rows, :] = (normal * (1.0 + scale) + shift).astype(jnp.bfloat16)
        return normal.astype(jnp.bfloat16)

    def attend_first():
        def body(latents, out):
            rows = tile_rows(pl.program_id(0), tile)
            values = latents[...].astype(plain)
            out[...] = normed(values, r.attend_rate, rows, ROW.shift_a, ROW.scale_a)

        run_tiles(body, 4, [by_rows(r.latents, tile)], [by_rows(r.attend_normal, tile)])
        turn_out(r.low, r.attend_turned)

    def through(weight, place, count, left, target, size=third):
        def body(block):
            columns = tile_rows(pl.program_id(0), size)
            target(columns, dot_plain(left(), block[...]))

        high = weight.shape[0]
        run_tiles(body, count, [(weight, (high, size), lambda step: (0, place + step))], [])

    def set_broad(columns, value):
        r.broad[:, columns] = value.astype(jnp.bfloat16)

    def set_memory(columns, value):
        r.memory[:, columns] = value.astype(jnp.bfloat16)

    def attend_heads():
        through(r.whole_spatial, 0, 9, lambda: r.low[...], set_broad)
        for place, heads in enumerate((r.head_query, r.head_key, r.head_value)):
            split_heads(r.broad, place * width, heads, head_size, HEADS)

    def attention(queries, keys, values, mask, logsum, outs, first=0, last=HEADS):
        def step(head, carry):
            query, key, value = queries[head], keys[head], values[head]
            scores = dot_rows(key, query) * att_scale
            if mask is not None:
                scores = scores + mask[:, 0:1]
            largest = jnp.max(scores, axis=0, keepdims=True)
            total = jnp.sum(jnp.exp(scores - largest), axis=0, keepdims=True)
            logs = largest + jnp.log(total)
            logsum[head, 0:1, :] = logs
            weights = jnp.exp(scores - logs).astype(jnp.bfloat16)
            turned = lax.dot_general(
                value, weights, (((0,), (0,)), ((), ())), preferred_element_type=plain
            )
            outs[head] = turned.T.astype(jnp.bfloat16)
            return carry

        lax.fori_loop(first, last, step, 0)

    def attend_attention(half):
        attention(
            r.head_query,
            r.head_key,
            r.head_value,
            None,
            r.spatial_logsum,
            r.head_out,
            half * HEADS // 2,
            (half + 1) * HEADS // 2,
        )

    def attend_merge():
        merge_heads(r.head_out, r.middle, 0, head_size, HEADS)
        turn_out(r.middle, r.spatial_turned)

    def attend_last():
        def body(weight, latents, branch):
            columns = tile_rows(pl.program_id(0), third)
            value = dot_plain(r.middle[...], weight[...])
            value = value + r.rows_low[VEC.spatial : VEC.spatial + 1, columns]
            branch[...] = value.astype(jnp.bfloat16)
            after = latents[...].astype(plain)
            after = after + r.mods[ROW.gate_a : ROW.gate_a + 1, columns] * value
            r.running[:, columns] = after
            r.low[:, columns] = after.astype(jnp.bfloat16)

        run_tiles(
            body,
            3,
            [
                (r.whole_spatial, (width, third), lambda step: (0, 9 + step)),
                by_columns(r.latents, third),
            ],
            [by_columns(r.branch_attend, third)],
        )
        turn_out(r.low, r.after_turned)

    def context():
        def body(weight):
            columns = tile_rows(pl.program_id(0), third)
            r.context[:, columns] = dot_plain(r.own_text[...], weight[...]).astype(jnp.bfloat16)

        run_tiles(body, 3, [by_columns(r.whole_context, third)], [])
        turn_out(r.context, r.context_turned)

    def cross_heads():
        through(r.whole_text, 3, 6, lambda: r.context[...], set_memory)
        split_heads(r.memory, 0, r.cross_key, head_size, HEADS)
        split_heads(r.memory, width, r.cross_value, head_size, HEADS)
        through(r.whole_text, 0, 3, lambda: r.low[...], set_broad)
        split_heads(r.broad, 0, r.cross_query, head_size, HEADS)

    def cross_attention():
        attention(
            r.cross_query, r.cross_key, r.cross_value, r.text_mask, r.cross_logsum, r.head_out
        )
        merge_heads(r.head_out, r.middle, 0, head_size, HEADS)
        turn_out(r.middle, r.cross_turned)

    def add_cross(columns, value):
        r.running[:, columns] += value + r.rows_low[VEC.cross : VEC.cross + 1, columns]

    def cross_last():
        through(r.whole_text, 9, 3, lambda: r.middle[...], add_cross)

    def feed_first():
        def body(out):
            rows = tile_rows(pl.program_id(0), tile)
            out[...] = normed(r.running[rows, :], r.feed_rate, rows, ROW.shift_m, ROW.scale_m)

        run_tiles(body, 4, [], [by_rows(r.feed_normal, tile)])
        turn_out(r.low, r.feed_turned)

    def feed_hidden():
        size = 512

        def body(weight, slope, turned):
            columns = tile_rows(pl.program_id(0), size)
            values = dot_plain(r.low[...], weight[...]) + r.rows_expand[0:1, columns]
            inner = math.sqrt(2.0 / math.pi)
            square = values * values
            bent = jnp.tanh(inner * values * (1.0 + 0.044715 * square))
            half = 0.5 * (1.0 + bent)
            hidden = values * half
            steep = inner * (1.0 + 3.0 * 0.044715 * square)
            slope[...] = (half + 0.5 * values * (1.0 - bent * bent) * steep).astype(jnp.bfloat16)
            r.broad[:, columns] = hidden.astype(jnp.bfloat16)
            turned[...] = hidden.T.astype(jnp.bfloat16)

        run_tiles(
            body,
            r.broad.shape[1] // size,
            [by_columns(r.whole_expand, size)],
            [by_columns(r.gelu_slope, size), by_rows(r.hidden_turned, size)],
        )

    def feed_last():
        def body(weight, branch, after, sent):
            columns = tile_rows(pl.program_id(0), third)
            value = dot_plain(r.broad[...], weight[...])
            value = value + r.rows_low[VEC.reduce : VEC.reduce + 1, columns]
            branch[...] = value.astype(jnp.bfloat16)
            value = r.running[:, columns] + r.mods[ROW.gate_m : ROW.gate_m + 1, columns] * value
            after[...] = value
            sent[...] = value.astype(jnp.bfloat16).reshape(sent.shape)

        shape = r.sent.shape
        run_tiles(
            body,
            3,
            [by_columns(r.whole_reduce, third)],
            [
                by_columns(r.branch_feed, third),
                by_columns(r.after_feed, third),
                (r.sent, shape[:3] + (third,), lambda step: (0, 0, 0, step)),
            ],
        )

    return types.SimpleNamespace(**locals())


def forward_kernel(att_scale, names, *refs):
    r = types.SimpleNamespace(**dict(zip(names, refs)))
    r.held = [
        r.held_spatial, r.held_context, r.held_text, r.held_expand, r.held_reduce, r.held_time
    ]
    do = forward_stages(r, att_scale)
    shares = [
        r.share_spatial, r.share_context, r.share_text, r.share_expand, r.share_reduce, r.share_time
    ]
    wholes = [
        r.whole_spatial, r.whole_context, r.whole_text, r.whole_expand, r.whole_reduce, r.whole_time
    ]
    talls, count = FORWARD_TALLS, len(FORWARD_TALLS)
    column, frame, depth, core, across_x, across_y, sibling = neighbours()
    frame_peers = [(column, (frame + shift) % 8) for shift in range(1, 8)]
    greet(frame_peers + [(across_x, frame), (across_y, frame)])
    copies = Copies(r.send_sems, r.recv_sems)
    locals_started = []

    def local(source, target):
        copy = pltpu.make_async_copy(source, target, r.local_sems.at[len(locals_started)])
        copy.start()
        locals_started.append(copy)
        return copy

    mods, rows, arrivals = [], [], {index: [] for index in range(count)}
    from_x, from_y, from_far, own_place = {}, {}, {}, {}

    def send_mods():
        own = local(r.mod_parts.at[frame], r.mods_got.at[frame])
        for peer in frame_peers:
            mods.append(copies.start(r.mod_parts.at[peer[1]], r.mods_got.at[frame], peer))
        own.wait()

    def send_rows():
        own = local(r.row_parts, r.rows_got.at[frame])
        for peer in frame_peers:
            rows.append(copies.start(r.row_parts, r.rows_got.at[frame], peer))
        own.wait()

    def send(index):
        share, whole, tall = shares[index], wholes[index], talls[index]
        own = whole_share(whole, tall, frame)
        held = r.held[index]
        load = local(share, held)
        arrivals[index].append(copies.start(share, own, (column, sibling)))
        own_place[index] = (load, held, own)

    def place(index):
        load, held, own = own_place[index]
        load.wait()
        own_place[index] = local(held, own)

    order = (
        jnp.where(depth == 0, 3, 1),
        jnp.where((depth == 0) | (depth == 3), 2, 3),
        jnp.where(depth == 0, 1, jnp.where(depth == 3, 3, 2)),
    )

    def next_frame(step):
        return jnp.clip(depth + step, 0, 3) * 2 + core

    def send_depth(index):
        share, whole, tall = shares[index], wholes[index], talls[index]
        source = share_unit(share, tall, column)
        target = whole_unit(whole, tall, column, frame)
        for step, shift in ((1, 1), (-1, 3)):
            copies.start_if(
                (depth < 3) if step == 1 else (depth > 0),
                source,
                target,
                (column, next_frame(step)),
                r.depth_sems.at[index, shift],
            )

    def pass_depth(index, shift):
        source = ((depth + 4 - shift) % 4) * 2 + core
        piece = whole_unit(wholes[index], talls[index], column, source)
        copies.start_if(
            (depth >= shift) & (depth < 3),
            piece,
            piece,
            (column, next_frame(1)),
            r.depth_sems.at[index, (shift + 1) % 4],
        )
        copies.start_if(
            (depth < shift) & (depth > 0),
            piece,
            piece,
            (column, next_frame(-1)),
            r.depth_sems.at[index, shift - 1],
        )

    def wait_depth(index, shift):
        source = ((depth + 4 - shift) % 4) * 2 + core
        piece = whole_unit(wholes[index], talls[index], column, source)
        pltpu.make_async_remote_copy(
            src_ref=piece,
            dst_ref=piece,
            send_sem=r.send_sems.at[0],
            recv_sem=r.depth_sems.at[index, shift],
            device_id=(column, sibling),
            device_id_type=MESH_ID,
        ).wait_recv()

    def pass_on(index, turn, unit, device):
        source = ((depth + 4 - order[turn]) % 4) * 2 + core
        piece = whole_unit(wholes[index], talls[index], unit, source)
        return copies.start(piece, piece, device)

    def first(index, turns=(0, 1, 2)):
        for turn in turns:
            wait_depth(index, order[turn])
            pass_depth(index, order[turn])
            from_x[index, turn] = pass_on(index, turn, column, (across_x, frame))
            from_y[index, turn] = pass_on(index, turn, column, (across_y, frame))
            arrivals[index].append(pass_on(index, turn, column, (column, sibling)))
        if index + 2 < count and turns[-1] == 2:
            send(index + 2)
            send_depth(index + 2)

    def second(index):
        for turn in range(3):
            x_first = (index + turn) % 2 == 0
            from_x[index, turn].wait_recv()
            if x_first:
                from_far[index, turn] = pass_on(index, turn, across_x, (across_y, frame))
            arrivals[index].append(pass_on(index, turn, across_x, (column, sibling)))
            from_y[index, turn].wait_recv()
            if not x_first:
                from_far[index, turn] = pass_on(index, turn, across_y, (across_x, frame))
            arrivals[index].append(pass_on(index, turn, across_y, (column, sibling)))

    def third(index):
        for turn in range(3):
            from_far[index, turn].wait_recv()
            arrivals[index].append(pass_on(index, turn, 3 - column, (column, sibling)))

    def ready(index):
        place(index)
        for copy in arrivals[index]:
            copy.wait_recv()
        own_place[index].wait()

    def arrive(got):
        for copy in got:
            copy.wait_recv()

    send_mods()
    for index in (0, 1):
        send(index)
        send_depth(index)
    do.clear()
    arrive(mods)
    do.sum_mods()
    do.attend_first()
    first(0)
    send_rows()
    second(0)
    first(1)
    third(0)
    ready(0)
    do.attend_heads()
    kept = [
        local(r.head_query, r.queries),
        local(r.head_key, r.keys),
        local(r.head_value, r.values),
    ]
    second(1)
    first(2, (0, 1))
    do.attend_attention(0)
    third(1)
    first(2, (2,))
    do.attend_attention(1)
    do.attend_merge()
    first(3, (0, 1))
    second(2)
    arrive(rows)
    do.sum_rows()
    do.attend_last()
    first(3, (2,))
    third(2)
    ready(1)
    do.context()
    second(3)
    ready(2)
    do.cross_heads()
    kept += [
        local(r.cross_query, r.cross_queries),
        local(r.cross_key, r.cross_keys),
        local(r.cross_value, r.cross_values),
    ]
    first(4, (0, 1))
    third(3)
    do.cross_attention()
    first(4, (2,))
    second(4)
    do.cross_last()
    do.feed_first()
    first(5, (0, 1))
    ready(3)
    do.feed_hidden()
    third(4)
    first(5, (2,))
    ready(4)
    do.feed_last()
    cols = []
    own = local(r.sent.at[frame], r.held_cols)
    for peer in frame_peers:
        cols.append(copies.start(r.sent.at[peer[1]], r.time_cols.at[:, frame], peer))
    own.wait()
    own = local(r.held_cols, r.time_cols.at[:, frame])
    second(5)
    third(5)
    ready(5)
    arrive(cols)
    own.wait()
    copies.finish()
    for copy in kept:
        copy.wait()


def forward(att_scale, o):
    anywhere = pl.BlockSpec(memory_space=pl.ANY)
    inside = pl.BlockSpec(memory_space=pltpu.VMEM)
    tokens, width = o.latents.shape
    text_count = o.own_text.shape[0]
    hidden = 4 * width
    low, full = jnp.bfloat16, jnp.float32
    shape = jax.ShapeDtypeStruct
    hbm_in = dict(
        share_spatial=o.share_spatial,
        share_context=o.share_context,
        share_text=o.share_text,
        share_expand=o.share_expand,
        share_reduce=o.share_reduce,
        share_time=o.share_time,
        latents=o.latents,
        mod_parts=o.mod_parts,
        row_parts=o.row_parts,
    )
    vmem_in = dict(own_text=o.own_text, text_mask=o.text_mask)
    heads = (HEADS, tokens, HEAD_LANES)
    text_heads = (HEADS, text_count, HEAD_LANES)
    whole = lambda share: shape((8 * share.shape[0], share.shape[1]), low)
    hbm_out = dict(
        whole_spatial=whole(o.share_spatial),
        whole_context=whole(o.share_context),
        whole_text=whole(o.share_text),
        whole_expand=whole(o.share_expand),
        whole_reduce=whole(o.share_reduce),
        whole_time=whole(o.share_time),
    )
    hbm_out.update(
        attend_normal=shape((tokens, width), low),
        attend_turned=shape((width, tokens), low),
        queries=shape(heads, low),
        keys=shape(heads, low),
        values=shape(heads, low),
        spatial_turned=shape((width, tokens), low),
        branch_attend=shape((tokens, width), low),
        after_turned=shape((width, tokens), low),
        context_turned=shape((width, text_count), low),
        cross_queries=shape(heads, low),
        cross_keys=shape(text_heads, low),
        cross_values=shape(text_heads, low),
        cross_turned=shape((width, tokens), low),
        feed_normal=shape((tokens, width), low),
        feed_turned=shape((width, tokens), low),
        gelu_slope=shape((tokens, hidden), low),
        hidden_turned=shape((hidden, tokens), low),
        branch_feed=shape((tokens, width), low),
        after_feed=shape((tokens, width), full),
        sent=shape((8, tokens // (8 * 16), 16, width), low),
        time_cols=shape((tokens // (8 * 16), 8, 16, width), low),
    )
    vmem_out = dict(
        mods=shape((8, width), full),
        rows_low=shape((VEC.high, width), full),
        attend_rate=shape((tokens, LANES), full),
        feed_rate=shape((tokens, LANES), full),
        spatial_logsum=shape((HEADS, 8, tokens), full),
        cross_logsum=shape((HEADS, 8, tokens), full),
    )
    remote = 21 + len(FORWARD_TALLS) * 30
    held = lambda share: pltpu.VMEM(share.shape, low)
    scratch = dict(
        running=pltpu.VMEM((tokens, width), full),
        low=pltpu.VMEM((tokens, width), low),
        middle=pltpu.VMEM((tokens, width), low),
        broad=pltpu.VMEM((tokens, hidden), low),
        head_query=pltpu.VMEM(heads, low),
        head_key=pltpu.VMEM(heads, low),
        head_value=pltpu.VMEM(heads, low),
        head_out=pltpu.VMEM(heads, low),
        cross_query=pltpu.VMEM(heads, low),
        cross_key=pltpu.VMEM(text_heads, low),
        cross_value=pltpu.VMEM(text_heads, low),
        memory=pltpu.VMEM((text_count, 2 * width), low),
        context=pltpu.VMEM((text_count, width), low),
        rows_expand=pltpu.VMEM((8, hidden), full),
        held_spatial=held(o.share_spatial),
        held_context=held(o.share_context),
        held_text=held(o.share_text),
        held_expand=held(o.share_expand),
        held_reduce=held(o.share_reduce),
        held_time=held(o.share_time),
        held_cols=pltpu.VMEM((tokens // (8 * 16), 16, width), low),
        mods_got=pltpu.VMEM((8, 8, width), full),
        rows_got=pltpu.VMEM((8, VEC.high, width), low),
        send_sems=pltpu.SemaphoreType.DMA((remote,)),
        recv_sems=pltpu.SemaphoreType.DMA((remote,)),
        depth_sems=pltpu.SemaphoreType.DMA((len(FORWARD_TALLS), 4)),
        local_sems=pltpu.SemaphoreType.DMA((4 + 2 * len(FORWARD_TALLS) + 6,)),
    )
    names = list(hbm_in) + list(vmem_in) + list(hbm_out) + list(vmem_out) + list(scratch)
    results = pl.pallas_call(
        functools.partial(forward_kernel, att_scale, names),
        out_shape=list(hbm_out.values()) + list(vmem_out.values()),
        in_specs=[anywhere] * len(hbm_in) + [inside] * len(vmem_in),
        out_specs=[anywhere] * len(hbm_out) + [inside] * len(vmem_out),
        scratch_shapes=list(scratch.values()),
        compiler_params=pltpu.CompilerParams(
            collective_id=0, has_side_effects=True, vmem_limit_bytes=60 * 1024 * 1024
        ),
        name="forward",
    )(*hbm_in.values(), *vmem_in.values())
    return types.SimpleNamespace(**dict(zip(list(hbm_out) + list(vmem_out), results)))


def pack_rows(parts, rows):
    flat = jnp.concatenate(parts, axis=-1)
    flat = jnp.pad(flat, [(0, 0)] * (flat.ndim - 1) + [(0, rows * LANES - flat.shape[-1])])
    return flat.reshape(flat.shape[:-1] + (rows, LANES))


def results(
    block_output, input_gradient, mods, sums, totals, text_total, frame_index, row_count, bias_width
):
    model_width = mods.shape[-1]
    high = lambda part: part.astype(jnp.float32)
    total_time, total_reduce, total_expand, total_text, total_spatial = totals
    rows_gradient = mods[:, :6].reshape(-1, 6 * model_width)
    rows_condition = lax.dynamic_slice_in_dim(
        mods[:, ROW.condition], frame_index * row_count, row_count, 1
    )
    back_modulation_weight = jnp.einsum(
        "nd,ne->de", rows_condition, rows_gradient, precision=lax.Precision.HIGHEST
    )
    back_modulation_bias = jnp.sum(
        lax.dynamic_slice_in_dim(rows_gradient, frame_index * bias_width, bias_width, 1), axis=0
    )
    own_rows = lax.dynamic_slice_in_dim(sums, frame_index * row_count, row_count, 1)
    own_row = lambda which: own_rows[which - 8]
    own_expand = lax.dynamic_slice_in_dim(
        sums[ROW.expand - 8 : ROW.expand - 4].reshape(-1), frame_index * 4 * row_count, 4 * row_count, 0
    )
    own_gate = lax.dynamic_slice_in_dim(
        jnp.sum(mods[:, ROW.gate_t], axis=0), frame_index * row_count, row_count, 0
    )
    vec_total = (
        own_row(ROW.spatial),
        own_row(ROW.cross),
        own_expand,
        own_row(ROW.reduce),
        own_row(ROW.gain),
        own_row(ROW.shift),
        own_row(ROW.temporal),
        own_gate,
    )
    matrix_totals = (
        high(total_spatial[:, : 3 * model_width]),
        high(total_text[:, 4 * model_width : 5 * model_width]),
        high(total_text[:, :model_width]),
        high(total_text[:, model_width : 3 * model_width]),
        high(total_text[:, 3 * model_width : 4 * model_width]),
        high(total_expand),
        high(total_reduce),
        high(total_time[:, : 3 * model_width]),
        high(total_time[:, 3 * model_width :]),
    )
    others = (back_modulation_weight, back_modulation_bias, high(text_total)) + tuple(vec_total)
    return (
        block_output,
        input_gradient,
        others[0],
        others[1],
        matrix_totals[0],
        matrix_totals[1],
        others[3],
        others[2],
        matrix_totals[2],
        matrix_totals[3],
        matrix_totals[4],
        others[4],
        matrix_totals[5],
        others[5],
        matrix_totals[6],
        others[6],
        others[7],
        others[8],
        matrix_totals[7],
        matrix_totals[8],
        others[9],
        others[10],
    )


def on_device(
    latents,
    cotangent,
    text_tokens,
    text_lengths,
    clip_frames,
    timesteps,
    motion_free,
    modulation_weight,
    modulation_bias,
    spatial_input,
    spatial_output,
    spatial_bias,
    text_projection,
    cross_query,
    cross_memory,
    cross_output,
    cross_bias,
    expand_weight,
    expand_bias,
    reduce_weight,
    reduce_bias,
    temporal_gain,
    temporal_shift,
    temporal_input,
    temporal_output,
    temporal_bias,
    temporal_gate,
):
    frame_count = lax.axis_size("frame")
    frame_index = lax.axis_index("frame")
    patch_count = latents.shape[2]
    model_width = latents.shape[3]
    head_size = model_width // HEADS
    att_scale = 1.0 / math.sqrt(head_size)
    slot_count = clip_frames.shape[1]
    text_count = text_tokens.shape[2]
    frame_ids = jnp.arange(frame_count, dtype=jnp.int32)
    clip_ids = assign_clips(clip_frames[0], frame_count)
    slot_ids = jnp.arange(slot_count, dtype=jnp.int32)
    own_clip = jnp.sum(jnp.where(frame_ids == frame_index, clip_ids, 0))
    own_onehot = (slot_ids == own_clip).astype(jnp.float32)
    own_keep = 1.0 - jnp.sum(jnp.where(slot_ids == own_clip, motion_free[0], 0)).astype(jnp.float32)
    own_length = jnp.sum(jnp.where(slot_ids == own_clip, text_lengths[0], 0))
    conditioning = embed_time(timesteps[0], model_width).astype(jnp.bfloat16)
    row_count = modulation_weight.shape[0]
    cond_rows = lax.dynamic_slice_in_dim(conditioning, frame_index * row_count, row_count, 1)
    bias_width = modulation_bias.shape[0]
    bias_placed = lax.dynamic_update_slice_in_dim(
        jnp.zeros((6 * model_width,), jnp.float32),
        modulation_bias.astype(jnp.float32),
        frame_index * bias_width,
        0,
    )
    modulation_part = (
        jnp.dot(cond_rows, modulation_weight, preferred_element_type=jnp.float32)
        + bias_placed[None, :]
    )
    share_rows = text_projection.shape[0]
    if one_slice():
        near = 16
        text_high = -(-text_count // LANES) * LANES
        frame_onehot = (clip_ids[:, None] == slot_ids[None, :]).astype(jnp.float32)
        frame_modulation = jnp.sum(frame_onehot[:, :, None] * modulation_part[None], axis=1)
        frame_modulation = frame_modulation.reshape(frame_count, 6, model_width)
        here = (frame_ids == frame_index).astype(jnp.bfloat16)
        shares = jnp.stack(
            [
                spatial_bias,
                cross_bias,
                reduce_bias,
                temporal_gain,
                temporal_shift,
                temporal_bias,
                temporal_gate,
            ]
        )
        row_parts = jnp.concatenate(
            [
                (shares[:, None] * here[None, :, None]).reshape(-1, model_width),
                (expand_bias[None] * here[:, None]).reshape(-1, model_width),
            ]
        )
        own_text = lax.dynamic_index_in_dim(text_tokens[0], own_clip, 0, keepdims=False)
        text_places = jnp.arange(text_high, dtype=jnp.int32) < own_length
        tokens = latents[0, 0]
        operands = dict(
            share_spatial=jnp.concatenate([spatial_input, spatial_output], axis=1),
            share_context=text_projection,
            share_text=jnp.concatenate([cross_query, cross_memory, cross_output], axis=1),
            share_expand=expand_weight,
            share_reduce=reduce_weight,
            share_time=jnp.concatenate([temporal_input, temporal_output], axis=1),
            latents=tokens,
            mod_parts=jnp.pad(frame_modulation, ((0, 0), (0, 2), (0, 0))),
            row_parts=jnp.pad(row_parts, ((0, VEC.high - row_parts.shape[0]), (0, 0))),
            own_text=jnp.pad(own_text, ((0, text_high - text_count), (0, 0))),
            text_mask=jnp.broadcast_to(
                jnp.where(text_places, 0.0, big_negative)[:, None], (text_high, LANES)
            ),
        )
        operands = types.SimpleNamespace(**operands)
        vars(operands).update(vars(forward(att_scale, operands)))
        keep_frames = 1.0 - jnp.sum(
            frame_onehot * motion_free[0].astype(jnp.float32)[None, :], axis=1
        )
        sequence = jnp.arange(frame_count * near, dtype=jnp.int32)
        same = (sequence[:, None] % near == sequence[None, :] % near) & (
            jnp.repeat(clip_ids, near)[:, None] == jnp.repeat(clip_ids, near)[None, :]
        )
        row_keep = jnp.tile(jnp.repeat(keep_frames, near), patch_count // (frame_count * near))
        rows = operands.rows_low
        own_conditioning = jnp.sum(own_onehot[:, None] * conditioning.astype(jnp.float32), axis=0)
        vars(operands).update(
            cotangent=cotangent[0, 0],
            cot_rows=cotangent[0, 0].reshape(operands.sent.shape),
            vectors=jnp.stack(
                [
                    rows[VEC.gain],
                    rows[VEC.shift],
                    rows[VEC.temporal],
                    rows[VEC.gate],
                    rows[VEC.gate] * own_keep,
                    jnp.full((model_width,), own_keep),
                    own_conditioning,
                    jnp.zeros((model_width,), jnp.float32),
                ]
            ),
            time_keep=jnp.broadcast_to(row_keep[:, None], (patch_count, LANES)),
            time_mask=jnp.where(same, 0.0, big_negative),
        )
        text_share = lax.dynamic_slice_in_dim(
            text_tokens[0], frame_index * text_projection.shape[0], text_projection.shape[0], 2
        )
        frame_text = jnp.pad(text_share, ((0, 0), (0, text_high - text_count), (0, 0)))
        text_turned = jnp.einsum("fs,stk->kft", frame_onehot.astype(jnp.bfloat16), frame_text)
        text_turned = text_turned.reshape(text_projection.shape[0], -1)
        got = backward(att_scale, True, operands, text_turned)
        return results(
            got.block_out[None, None],
            got.tokens_out[None, None],
            got.mods_out.reshape(-1, 8, model_width),
            jnp.sum(got.sums_out, axis=0),
            [got.share_time, got.share_reduce, got.share_expand, got.share_text, got.share_input],
            got.text_out,
            frame_index,
            row_count,
            bias_width,
        )
    text_share = lax.dynamic_slice_in_dim(
        text_tokens[0], frame_index * text_projection.shape[0], text_projection.shape[0], 2
    )
    own_text = lax.dynamic_index_in_dim(text_tokens[0], own_clip, 0, keepdims=False)
    vectors = (
        spatial_bias,
        cross_bias,
        expand_bias,
        reduce_bias,
        temporal_gain,
        temporal_shift,
        temporal_bias,
        temporal_gate,
    )
    vector_sizes = [vector.shape[0] for vector in vectors]
    vector_rows = -(-sum(vector_sizes) // (8 * LANES)) * 8
    packed_vectors = pack_rows([vector.astype(jnp.float32) for vector in vectors], vector_rows)
    mod_rows_high = -(-(6 * model_width) // (8 * LANES)) * 8
    frame_onehot = (clip_ids[:, None] == slot_ids[None, :]).astype(jnp.float32)
    frame_modulation = jnp.sum(frame_onehot[:, :, None] * modulation_part[None], axis=1)
    wholes, vecs, mods = gather_all(
        (
            text_projection,
            jnp.concatenate([spatial_input, spatial_output], axis=1),
            jnp.concatenate([cross_query, cross_memory, cross_output], axis=1),
            expand_weight,
            reduce_weight,
            jnp.concatenate([temporal_input, temporal_output], axis=1),
        ),
        packed_vectors,
        pack_rows([frame_modulation], mod_rows_high),
    )
    projection, whole_spatial, whole_text, whole_expand, whole_reduce, whole_time = wholes
    context = jnp.dot(own_text, projection, preferred_element_type=jnp.float32)
    own_modulation = jnp.sum(mods, axis=0).reshape(-1)[: 6 * model_width]
    shift_attend, scale_attend, gate_attend, shift_feed, scale_feed, gate_feed = jnp.split(
        own_modulation, 6
    )
    vecs = vecs.reshape(frame_count, -1)[:, : sum(vector_sizes)]
    vector_ends = [sum(vector_sizes[: index + 1]) for index in range(len(vector_sizes) - 1)]
    (
        whole_bias,
        whole_cross_bias,
        whole_expand_bias,
        whole_reduce_bias,
        whole_gain,
        whole_shift,
        whole_temporal_bias,
        whole_gate,
    ) = [part.reshape(-1) for part in jnp.split(vecs, vector_ends, axis=1)]
    whole_input, whole_output = whole_spatial[:, : 3 * model_width], whole_spatial[:, 3 * model_width :]
    whole_query = whole_text[:, :model_width]
    whole_memory = whole_text[:, model_width : 3 * model_width]
    whole_cross = whole_text[:, 3 * model_width :]
    whole_temporal, whole_temporal_out = whole_time[:, : 3 * model_width], whole_time[:, 3 * model_width :]
    tokens = latents[0, 0].astype(jnp.float32)
    attend_normal, attend_rate = normal_parts(tokens)
    normed_attend = (attend_normal * (1.0 + scale_attend) + shift_attend).astype(jnp.bfloat16)
    spatial_heads = jnp.dot(normed_attend, whole_input, preferred_element_type=jnp.float32).astype(
        jnp.bfloat16
    )
    spatial_heads = spatial_heads.reshape(patch_count, 1, 3, HEADS, head_size)
    spatial_att, spatial_logsum = attend(
        spatial_heads[:, :, 0], spatial_heads[:, :, 1], spatial_heads[:, :, 2], None, att_scale
    )
    spatial_low = spatial_att.reshape(patch_count, model_width).astype(jnp.bfloat16)
    branch_attend = jnp.dot(
        spatial_low, whole_output, preferred_element_type=jnp.float32
    ) + whole_bias.astype(jnp.float32)
    after_attend = tokens + gate_attend * branch_attend
    after_low = after_attend.astype(jnp.bfloat16)
    cross_heads = jnp.dot(after_low, whole_query, preferred_element_type=jnp.float32).astype(
        jnp.bfloat16
    )
    cross_heads = cross_heads.reshape(patch_count, 1, HEADS, head_size)
    context_low = context.astype(jnp.bfloat16)
    memory_heads = jnp.dot(context_low, whole_memory, preferred_element_type=jnp.float32).astype(
        jnp.bfloat16
    )
    memory_heads = memory_heads.reshape(text_count, 1, 2, HEADS, head_size)
    text_mask = (jnp.arange(text_count, dtype=jnp.int32) < own_length)[None, None, None, :]
    cross_att, cross_logsum = attend(
        cross_heads, memory_heads[:, :, 0], memory_heads[:, :, 1], text_mask, att_scale
    )
    cross_low = cross_att.reshape(patch_count, model_width).astype(jnp.bfloat16)
    branch_cross = jnp.dot(
        cross_low, whole_cross, preferred_element_type=jnp.float32
    ) + whole_cross_bias.astype(jnp.float32)
    after_cross = after_attend + branch_cross
    feed_normal, feed_rate = normal_parts(after_cross)
    normed_feed = (feed_normal * (1.0 + scale_feed) + shift_feed).astype(jnp.bfloat16)
    hidden_pre = jnp.dot(
        normed_feed, whole_expand, preferred_element_type=jnp.float32
    ) + whole_expand_bias.astype(jnp.float32)
    hidden_low = smooth_gelu(hidden_pre).astype(jnp.bfloat16)
    gelu_slope = slope_gelu(hidden_pre).astype(jnp.bfloat16)
    branch_feed = jnp.dot(
        hidden_low, whole_reduce, preferred_element_type=jnp.float32
    ) + whole_reduce_bias.astype(jnp.float32)
    after_feed = after_cross + gate_feed * branch_feed
    sent_low = after_feed.astype(jnp.bfloat16)
    low = lambda part: part.astype(jnp.bfloat16)
    gate_keep = whole_gate.astype(jnp.float32) * own_keep
    upstream = cotangent[0, 0].astype(jnp.float32)
    keep_frames = 1.0 - jnp.sum(frame_onehot * motion_free[0].astype(jnp.float32)[None, :], axis=1)
    time_mask = (clip_ids[:, None] == clip_ids[None, :])[None, None]
    gain_float = whole_gain.astype(jnp.float32)
    shift_float = whole_shift.astype(jnp.float32)
    columns = lax.all_to_all(sent_low[None], "frame", split_axis=1, concat_axis=0, tiled=True)
    frames_here = columns.shape[0]
    positions = columns.shape[1]
    normed_time = affine_norm(columns.astype(jnp.float32), gain_float, shift_float).astype(
        jnp.bfloat16
    )
    time_heads = jnp.einsum(
        "fpd,de->fpe", normed_time, whole_temporal, preferred_element_type=jnp.float32
    )
    time_heads = time_heads.astype(jnp.bfloat16).reshape(
        frames_here, positions, 3, HEADS, head_size
    )
    time_att, time_logsum = attend(
        time_heads[:, :, 0], time_heads[:, :, 1], time_heads[:, :, 2], time_mask, att_scale
    )
    time_low = time_att.reshape(frames_here, positions, model_width).astype(jnp.bfloat16)
    result = jnp.einsum(
        "fpd,de->fpe", time_low, whole_temporal_out, preferred_element_type=jnp.float32
    )
    result = result + whole_temporal_bias.astype(jnp.float32)
    result_low = result.astype(jnp.bfloat16)
    kept_state = (normed_time, time_heads, time_low, time_logsum)
    back_sent = (upstream * gate_keep).astype(jnp.bfloat16)
    back_columns = lax.all_to_all(back_sent[None], "frame", split_axis=1, concat_axis=0, tiled=True)
    normed_time, time_heads, time_low, time_logsum = kept_state
    frames_here, positions = (columns.shape[0], columns.shape[1])
    back_temporal_bias = jnp.sum(back_columns.astype(jnp.float32), axis=(0, 1))
    back_temporal_out = jnp.einsum(
        "fpd,fpe->de", time_low, back_columns, preferred_element_type=jnp.float32
    )
    back_time_att = jnp.einsum(
        "fpe,de->fpd", back_columns, whole_temporal_out, preferred_element_type=jnp.float32
    )
    back_time_att = back_time_att.astype(jnp.bfloat16).reshape(
        frames_here, positions, HEADS, head_size
    )
    back_time_queries, back_time_keys, back_time_values = attend_back(
        time_heads[:, :, 0],
        time_heads[:, :, 1],
        time_heads[:, :, 2],
        time_mask,
        att_scale,
        time_logsum,
        back_time_att,
    )
    back_time_heads = jnp.stack([back_time_queries, back_time_keys, back_time_values], axis=2)
    back_time_heads = back_time_heads.reshape(frames_here, positions, 3 * model_width).astype(
        jnp.bfloat16
    )
    back_temporal = jnp.einsum(
        "fpd,fpe->de", normed_time, back_time_heads, preferred_element_type=jnp.float32
    )
    back_normed = jnp.einsum(
        "fpe,de->fpd", back_time_heads, whole_temporal, preferred_element_type=jnp.float32
    )
    unused_norm, norm_back = jax.vjp(
        affine_norm, columns.astype(jnp.float32), gain_float, shift_float
    )
    back_inputs, back_gain, back_shift = norm_back(back_normed)
    returned, back_return = jnp.split(
        lax.all_to_all(
            jnp.concatenate([result_low, back_inputs.astype(jnp.bfloat16)], axis=2),
            "frame",
            split_axis=0,
            concat_axis=1,
            tiled=True,
        ),
        2,
        axis=2,
    )
    temporal_value = returned[0].astype(jnp.float32)
    block_output = (after_feed + gate_keep * temporal_value).astype(jnp.bfloat16)[None, None]
    back_gate = jnp.sum(upstream * temporal_value, axis=0) * own_keep
    text_high = -(-text_count // LANES) * LANES

    def padded_heads(heads, high):
        heads = jnp.transpose(heads[:, 0], (1, 0, 2))
        return jnp.pad(heads, ((0, 0), (0, high - heads.shape[1]), (0, HEAD_LANES - head_size)))

    padded_context = jnp.pad(context_low, ((0, text_high - text_count), (0, 0)))
    text_places = jnp.arange(text_high, dtype=jnp.int32) < own_length
    operands = dict(
        whole_spatial=whole_spatial,
        whole_text=whole_text,
        whole_expand=whole_expand,
        whole_reduce=whole_reduce,
        cotangent=cotangent[0, 0],
        branch_feed=low(branch_feed),
        hidden_turned=hidden_low.T,
        gelu_slope=gelu_slope,
        feed_turned=normed_feed.T,
        feed_normal=low(feed_normal),
        cross_turned=cross_low.T,
        cross_queries=padded_heads(cross_heads, patch_count),
        cross_keys=padded_heads(memory_heads[:, :, 0], text_high),
        cross_values=padded_heads(memory_heads[:, :, 1], text_high),
        after_turned=after_low.T,
        context_turned=padded_context.T,
        branch_attend=low(branch_attend),
        spatial_turned=spatial_low.T,
        queries=padded_heads(spatial_heads[:, :, 0], patch_count),
        keys=padded_heads(spatial_heads[:, :, 1], patch_count),
        values=padded_heads(spatial_heads[:, :, 2], patch_count),
        attend_turned=normed_attend.T,
        attend_normal=low(attend_normal),
        mods=jnp.pad(own_modulation.reshape(6, model_width), ((0, 2), (0, 0))),
        feed_rate=jnp.broadcast_to(feed_rate, (patch_count, LANES)),
        attend_rate=jnp.broadcast_to(attend_rate, (patch_count, LANES)),
        cross_logsum=jnp.broadcast_to(
            cross_logsum[0, :, None, :, 0], (HEADS, 8, patch_count)
        ),
        spatial_logsum=jnp.broadcast_to(
            spatial_logsum[0, :, None, :, 0], (HEADS, 8, patch_count)
        ),
        text_mask=jnp.broadcast_to(
            jnp.where(text_places, 0.0, big_negative)[:, None], (text_high, LANES)
        ),
    )
    own_conditioning = jnp.sum(own_onehot[:, None] * conditioning.astype(jnp.float32), axis=0)
    operands.update(back_sent=back_return[0])
    got = backward(att_scale, False, types.SimpleNamespace(**operands), None)
    input_gradient = got.tokens_out[None, None]
    rows = got.row_sums
    rows = rows.at[ROW.condition].set(own_conditioning).at[ROW.gate_t].set(back_gate)
    rows = rows.at[ROW.gain].set(back_gain).at[ROW.shift].set(back_shift)
    rows = rows.at[ROW.temporal].set(back_temporal_bias)
    mods = lax.all_gather(rows[:8], ("clip", "frame"), axis=0)
    sums = lax.psum(rows[8:], ("clip", "frame"))
    all_context = lax.all_gather(got.back_context[:text_count], "frame", axis=0)
    context_total = jnp.einsum("fs,ftd->std", frame_onehot, all_context.astype(jnp.float32))
    text_total = lax.psum(
        jnp.einsum(
            "stk,std->kd",
            text_share,
            low(context_total),
            preferred_element_type=jnp.float32,
        ).astype(jnp.bfloat16),
        "clip",
    )
    totals = [
        sum_shares((low(back_temporal), low(back_temporal_out))),
        sum_shares((got.part_reduce,)),
        sum_shares((got.part_expand,)),
        sum_shares((got.part_text,)),
        sum_shares((got.part_input,)),
    ]
    return results(
        block_output,
        input_gradient,
        mods,
        sums,
        totals,
        text_total,
        frame_index,
        row_count,
        bias_width,
    )


def solution(mesh):
    placed = (
        P("clip", "frame", None, None),
        P("clip", "frame", None, None),
        P("clip", None, None, None),
        P("clip", None),
        P("clip", None),
        P("clip", None),
        P("clip", None),
        P("frame", None),
        P("frame"),
        P("frame", None),
        P("frame", None),
        P("frame"),
        P("frame", None),
        P("frame", None),
        P("frame", None),
        P("frame", None),
        P("frame"),
        P("frame", None),
        P("frame"),
        P("frame", None),
        P("frame"),
        P("frame"),
        P("frame"),
        P("frame", None),
        P("frame", None),
        P("frame"),
        P("frame"),
    )
    return jax.shard_map(
        on_device,
        mesh=mesh,
        in_specs=placed,
        out_specs=(
            P("clip", "frame", None, None),
            P("clip", "frame", None, None),
            P("frame", None),
            P("frame"),
            P("frame", None),
            P("frame", None),
            P("frame"),
            P("frame", None),
            P("frame", None),
            P("frame", None),
            P("frame", None),
            P("frame"),
            P("frame", None),
            P("frame"),
            P("frame", None),
            P("frame"),
            P("frame"),
            P("frame"),
            P("frame", None),
            P("frame", None),
            P("frame"),
            P("frame"),
        ),
        check_vma=False,
    )
```
